128 devices in a mesh: pb: 8 (over x, core), pa: 16 (over z, y).
Axes of the slice: x: 4, y: 4, z: 4, core: 2. Of those that a mesh axis runs over, the one named last changes fastest.
Arguments:
- queries: bfloat16 [32768, 768], P('pb'), may hold values from -400 to 400
- passages: bfloat16 [65536, 768], P('pa'), may hold values from -400 to 400
- tiles: int32 [32, 8], replicated, may hold values from 0 to 63, as said below
- positives: int32 [32768], P('pb'), may hold values from 0 to 64511, as said below
- cotangent: float32 [32768], P('pb'), may hold values from -6 to 6
Outputs:
- losses: float32 [32768], P(('pb', 'pa'))
- query_grads: bfloat16 [32768, 768], P(('pb', 'pa'))
- passage_grads: bfloat16 [65536, 768], P('pa', 'pb')
The draws below stay inside these ranges and needn't reach their ends.
Inputs may be any that keep to these rules, and one draw needn't show every extreme that they name: `tiles`: entries of one row are distinct; the first entry of row b is b * 2. `positives`: the positive of query i lies in passage block (i // 1024) * 2, the first tile of its query block.
All inputs are finite; a program needn't handle non-finite values.
Results may differ from the reference program's by a relative error of at most 0.015.
Values may be sent and summed in bfloat16 or wider, within the bound.
A program may use at most 128 MiB of HBM per device.

```python
import math
import jax
import jax.numpy as jnp
from jax import lax

D = 768
BLK = 1024
QB_DEV = 4
PB_DEV = 4
TILES = 8
QUERY_BLOCKS = 32
PASSAGE_BLOCKS = 64
NQ = 32768
NP = 65536
N_PB = 8
N_PA = 16


def draw_queries(key, part):
    key = jax.random.fold_in(key, 3)
    first, runner_up = jax.random.split(key, 2)
    scales = jnp.exp(jax.random.uniform(first, (NQ, 1), jnp.float32, math.log(0.5), math.log(4.0)))
    values = jax.random.normal(runner_up, (NQ, D), jnp.float32) * scales
    return values.astype(jnp.bfloat16)


def draw_passages(key, part):
    key = jax.random.fold_in(key, 5)
    first, runner_up = jax.random.split(key, 2)
    scales = jnp.exp(jax.random.uniform(first, (NP, 1), jnp.float32, math.log(0.5), math.log(3.0)))
    values = jax.random.normal(runner_up, (NP, D), jnp.float32) * scales
    return values.astype(jnp.bfloat16)


def draw_tiles(key, part):
    key = jax.random.fold_in(key, 11)
    first, runner_up = jax.random.split(key, 2)
    frequent_entry = jax.random.randint(first, (PASSAGE_BLOCKS,), 0, 4) == 0
    extra_reward = jnp.where(frequent_entry, 3000, 0).astype(jnp.int32)
    spread = PASSAGE_BLOCKS // QUERY_BLOCKS
    inbatch = jnp.arange(QUERY_BLOCKS, dtype=jnp.int32) * spread
    blocks = jnp.arange(PASSAGE_BLOCKS, dtype=jnp.int32)
    qrows = jnp.arange(QUERY_BLOCKS, dtype=jnp.int32)
    compelled = ((qrows[:, None] == 0) & (blocks[None, :] == PASSAGE_BLOCKS - 1)).astype(jnp.int32) * 100000
    precedence = jax.random.randint(runner_up, (QUERY_BLOCKS, PASSAGE_BLOCKS), 0, 4096) + extra_reward[None, :] + compelled
    precedence = jnp.where(blocks[None, :] == inbatch[:, None], -1, precedence)
    precedence = precedence * PASSAGE_BLOCKS + blocks[None, :]
    unused, picked = jax.lax.top_k(precedence, TILES - 1)
    return jnp.concatenate([inbatch[:, None], picked.astype(jnp.int32)], axis=1).astype(jnp.int32)


def draw_positives(key, part):
    key = jax.random.fold_in(key, 7)
    rows = jnp.arange(NQ, dtype=jnp.int32)
    local = rows % BLK
    offsets = jax.random.randint(key, (NQ,), 0, BLK)
    offsets = jnp.where(local == 0, 0, offsets)
    offsets = jnp.where(local == BLK - 1, BLK - 1, offsets)
    return (rows // BLK * (PASSAGE_BLOCKS // QUERY_BLOCKS) * BLK + offsets).astype(jnp.int32)


def shard_levels(own_key, extent, cuts, smallest, high):
    def one(position, blocks):
        heights = jax.random.uniform(jax.random.fold_in(jax.random.fold_in(own_key, 6), position), (blocks,), jnp.float32, smallest / len(cuts), high / len(cuts))
        return jnp.repeat(jnp.exp(heights), extent[position] // blocks).reshape((-1,) + (1,) * (len(extent) - position - 1))

    level = one(*cuts[0])
    for cut in cuts[1:]:
        level = level * one(*cut)
    return level


def bell_draw(key, shape, scale, most, shards=(), held_as=jnp.bfloat16):
    entries = jax.random.normal(key, shape, jnp.float32) * scale
    if len(shards) > 0:
        entries = shard_levels(key, shape, shards, -0.22, 0.18) * entries
    return jnp.clip(entries, min=-most, max=most).astype(held_as)


def setup_inputs(seed: int = 0) -> dict:
    keys = jax.random.split(jax.random.key(seed), 6)
    return {
        "queries": draw_queries(jax.random.fold_in(keys[5], 71), 0),
        "passages": draw_passages(jax.random.fold_in(keys[5], 71), 0),
        "tiles": draw_tiles(jax.random.fold_in(keys[5], 71), 0),
        "positives": draw_positives(jax.random.fold_in(keys[5], 71), 0),
        "cotangent": bell_draw(keys[4], (NQ,), 1.0, 6.0, ((0, 8),), jnp.float32),
    }


def reference(queries, passages, tiles, positives, cotangent):
    scale = D ** -0.5
    columns = jnp.arange(BLK, dtype=jnp.int32)
    owners = jnp.arange(N_PA, dtype=jnp.int32)
    passage_blocks = passages.reshape(PASSAGE_BLOCKS, BLK, D)

    def one_block(carry, block_id):
        query_tile = lax.dynamic_slice_in_dim(queries, block_id * BLK, BLK, 0).astype(jnp.float32)
        chosen = tiles[block_id]
        gathered = passage_blocks[chosen].astype(jnp.float32)
        scores = jnp.einsum("rd,kcd->krc", query_tile, gathered) * scale
        highs = jnp.max(scores, axis=(0, 2))
        totals = jnp.sum(jnp.exp(scores - highs[None, :, None]), axis=(0, 2))
        pos_rows = lax.dynamic_slice_in_dim(positives, block_id * BLK, BLK, 0)
        target = ((chosen[:, None, None] * BLK + columns[None, None, :]) == pos_rows[None, :, None]).astype(jnp.float32)
        picked = jnp.sum(scores * target, axis=(0, 2))
        losses = highs + jnp.log(totals) - picked
        prob = jnp.exp(scores - highs[None, :, None]) / totals[None, :, None]
        weight_rows = lax.dynamic_slice_in_dim(cotangent, block_id * BLK, BLK, 0)
        grad = (weight_rows[None, :, None] * (prob - target) * scale).astype(jnp.bfloat16)
        grad = lax.optimization_barrier(grad).astype(jnp.float32)
        dq_terms = jnp.einsum("krc,kcd->krd", grad, gathered)
        onehot = ((chosen // PB_DEV)[:, None] == owners[None, :]).astype(jnp.float32)
        dq_parts = jnp.einsum("ka,krd->ard", onehot, dq_terms)
        dq_parts = lax.optimization_barrier(dq_parts.astype(jnp.bfloat16)).astype(jnp.float32)
        dq_block = jnp.sum(dq_parts, axis=0).astype(jnp.bfloat16)
        dp_terms = jnp.einsum("krc,rd->kcd", grad, query_tile)
        carry = carry.at[chosen].add(dp_terms)
        return carry, (losses, dq_block)

    def one_group(total, group):
        block_ids = (group * QB_DEV + jnp.arange(QB_DEV, dtype=jnp.int32)).astype(jnp.int32)
        part, (losses, dq_blocks) = lax.scan(one_block, jnp.zeros((PASSAGE_BLOCKS, BLK, D), jnp.float32), block_ids)
        part = lax.optimization_barrier(part.astype(jnp.bfloat16)).astype(jnp.float32)
        return total + part, (losses, dq_blocks)

    total, (losses, dq_blocks) = lax.scan(one_group, jnp.zeros((PASSAGE_BLOCKS, BLK, D), jnp.float32), jnp.arange(N_PB, dtype=jnp.int32))
    return losses.reshape(NQ), dq_blocks.reshape(NQ, D), total.reshape(NP, D).astype(jnp.bfloat16)
```

```python
import jax
import jax.numpy as jnp
from jax import lax
from jax.experimental import pallas as pl
from jax.experimental.pallas import tpu as pltpu
from jax.sharding import PartitionSpec as P

D = 768
BLK = 1024
NB = 4
SCALE = D ** (-0.5)
LOG2E = 1.4426950408889634
CH = 256
F32 = jnp.float32
BF16 = jnp.bfloat16
LOW = -1e30


def listed(tiles_ref, group, owner, j):
    row = group * NB + j // NB
    block = owner * NB + j % NB
    hit = jnp.int32(0)
    for t in range(8):
        hit = hit | (tiles_ref[row, t] == block).astype(jnp.int32)
    return hit


def lane_iota(rows):
    return lax.broadcasted_iota(jnp.int32, (rows, 128), 1)


def column(x, lane):
    return jnp.sum(jnp.where(lane_iota(x.shape[0]) == lane, x, 0.0), axis=1, keepdims=True)


def forward_kernel(tiles_ref, rows_ref, q_hbm, p_hbm, e_hbm, m_ref, stats_ref,
                   q_v, p_v, e_v, t_v, cols_v, pick_v, q_sem, p_sem, e_sem):
    group = lax.axis_index("pb")
    owner = lax.axis_index("pa")
    q_copies = [pltpu.make_async_copy(q_hbm.at[pl.ds(b * BLK, BLK)], q_v.at[b], q_sem.at[b]) for b in range(NB)]
    p_copies = [pltpu.make_async_copy(p_hbm.at[pl.ds(b * BLK, BLK)], p_v.at[b], p_sem.at[b]) for b in range(NB)]
    for b in range(NB):
        p_copies[b].start()
        q_copies[b].start()
    m_ref[...] = jnp.full_like(m_ref, LOW)
    t_v[...] = jnp.zeros_like(t_v)
    pick_v[...] = jnp.zeros_like(pick_v)
    cols_v[...] = jnp.zeros_like(cols_v)
    cols_v[...] = jnp.concatenate([rows_ref[...], jnp.zeros((112, BLK), F32)], axis=0).T
    for b in range(NB):
        p_copies[b].wait()
        q_copies[b].wait()

    def store(slot, n):
        return pltpu.make_async_copy(e_v.at[slot], e_hbm.at[n], e_sem.at[slot])

    def step(j, n):
        hit = listed(tiles_ref, group, owner, j)

        @pl.when(hit == 1)
        def _():
            qb = j // NB
            pb = j % NB
            slot = n % 2

            @pl.when(n >= 2)
            def _():
                store(slot, 0).wait()

            first = (owner * NB + pb) == (group * NB + qb) * 2
            for c in range(BLK // CH):
                r = pl.ds(c * CH, CH)
                s = lax.dot_general(q_v[qb, r, :], p_v[pb], (((1,), (1,)), ((), ())), preferred_element_type=F32)
                top = jnp.max(s, axis=1, keepdims=True)
                e = jnp.exp2(s * (SCALE * LOG2E) - top * (SCALE * LOG2E))
                e_v[slot, r, :] = e.astype(BF16)
                here = lane_iota(CH) == j
                m_ref[r, :] = jnp.where(here, top * SCALE, m_ref[r, :])
                t_v[r, :] = jnp.where(here, jnp.sum(e, axis=1, keepdims=True), t_v[r, :])

                @pl.when(first)
                def _():
                    pos = column(cols_v[r, :], 4 + qb)
                    wide = lax.broadcasted_iota(jnp.int32, (CH, BLK), 1).astype(F32)
                    got = jnp.sum(jnp.where(wide == pos, s, 0.0), axis=1, keepdims=True) * SCALE
                    pick_v[r, :] = jnp.where(lane_iota(CH) == qb, got, pick_v[r, :])

            store(slot, n).start()

        return n + hit

    total = lax.fori_loop(0, NB * NB, step, jnp.int32(0))

    m_rows = m_ref[...].T
    t_rows = t_v[...].T
    pick_rows = pick_v[...].T
    highs, totals = [], []
    for b in range(NB):
        m4 = m_rows[b * NB : b * NB + NB, :]
        high = jnp.max(m4, axis=0, keepdims=True)
        highs.append(high)
        totals.append(jnp.sum(t_rows[b * NB : b * NB + NB, :] * jnp.exp(m4 - high), axis=0, keepdims=True))
    stats_ref[...] = jnp.concatenate(highs + totals + [pick_rows[0:8, :]], axis=0)

    @pl.when(total >= 1)
    def _():
        store((total - 1) % 2, 0).wait()

    @pl.when(total >= 2)
    def _():
        store(total % 2, 0).wait()


def backward_kernel(tiles_ref, rows_ref, m_ref, e_hbm, q_hbm, p_hbm, dq_ref, dp_ref,
                    q_v, qt_v, p_v, e_v, g_v, cols_v, dq_v, dp_v, q_sem, p_sem, e_sem):
    group = lax.axis_index("pb")
    owner = lax.axis_index("pa")
    p_copies = [pltpu.make_async_copy(p_hbm.at[pl.ds(b * BLK, BLK)], p_v.at[b], p_sem.at[b]) for b in range(NB)]
    q_copies = [pltpu.make_async_copy(q_hbm.at[pl.ds(b * BLK, BLK)], q_v.at[b], q_sem.at[b]) for b in range(NB)]
    for b in range(NB):
        p_copies[b].start()
        q_copies[b].start()

    def load(slot, n):
        return pltpu.make_async_copy(e_hbm.at[n], e_v.at[slot], e_sem.at[slot])

    count = lax.fori_loop(0, NB * NB, lambda j, n: n + listed(tiles_ref, group, owner, j), jnp.int32(0))

    @pl.when(count >= 1)
    def _():
        load(0, 0).start()

    cols_v[...] = jnp.concatenate([rows_ref[...], jnp.zeros((112, BLK), F32)], axis=0).T
    dp_v[...] = jnp.zeros_like(dp_v)
    for b in range(NB):
        p_copies[b].wait()
        q_copies[b].wait()

    def block(qb, n):
        qt_v[...] = q_v[qb].T
        dq_v[...] = jnp.zeros_like(dq_v)

        def step(pb, n):
            j = qb * NB + pb
            hit = listed(tiles_ref, group, owner, j)

            @pl.when(hit == 1)
            def _():
                slot = n % 2

                @pl.when(n + 1 < count)
                def _():
                    load(1 - slot, n + 1).start()

                load(slot, n).wait()
                first = (owner * NB + pb) == (group * NB + qb) * 2
                for c in range(BLK // CH):
                    r = pl.ds(c * CH, CH)
                    cols = cols_v[r, :]
                    ct = column(cols, 8 + qb) * SCALE
                    factor = ct * jnp.exp(column(m_ref[r, :], j) - column(cols, qb)) / column(cols, 4 + qb)
                    pos = jnp.where(first, column(cols, 12 + qb), -1.0)
                    wide = lax.broadcasted_iota(jnp.int32, (CH, BLK), 1).astype(F32)
                    g = e_v[slot, r, :].astype(F32) * factor - jnp.where(wide == pos, ct, 0.0)
                    g = g.astype(BF16)
                    g_v[r, :] = g
                    dq_v[r, :] += jnp.dot(g, p_v[pb], preferred_element_type=F32)
                for c in range(3):
                    r = pl.ds(c * CH, CH)
                    dp_v[pb, r, :] += jnp.dot(qt_v[r, :], g_v[...], preferred_element_type=F32)

            return n + hit

        n = lax.fori_loop(0, NB, step, n)
        dq_ref[pl.ds(qb * BLK, BLK), :] = dq_v[...].astype(BF16)
        return n

    lax.fori_loop(0, NB, block, jnp.int32(0))
    for b in range(NB):
        dp_ref[:, pl.ds(b * BLK, BLK)] = dp_v[b].astype(BF16)


SMEM = pl.BlockSpec(memory_space=pltpu.SMEM)
VMEM = pl.BlockSpec(memory_space=pltpu.VMEM)
ANY = pl.BlockSpec(memory_space=pl.ANY)


def forward(tiles, rows, queries, passages):
    return pl.pallas_call(
        forward_kernel,
        out_shape=[
            jax.ShapeDtypeStruct((NB * NB, BLK, BLK), BF16),
            jax.ShapeDtypeStruct((BLK, 128), F32),
            jax.ShapeDtypeStruct((16, BLK), F32),
        ],
        in_specs=[SMEM, VMEM, ANY, ANY],
        out_specs=[ANY, VMEM, VMEM],
        scratch_shapes=[
            pltpu.VMEM((NB, BLK, D), BF16),
            pltpu.VMEM((NB, BLK, D), BF16),
            pltpu.VMEM((2, BLK, BLK), BF16),
            pltpu.VMEM((BLK, 128), F32),
            pltpu.VMEM((BLK, 128), F32),
            pltpu.VMEM((BLK, 128), F32),
            pltpu.SemaphoreType.DMA((NB,)),
            pltpu.SemaphoreType.DMA((NB,)),
            pltpu.SemaphoreType.DMA((2,)),
        ],
        compiler_params=pltpu.CompilerParams(vmem_limit_bytes=56 * 2**20),
        name="forward",
    )(tiles, rows, queries, passages)


def backward(tiles, rows, m, e, queries, passages):
    return pl.pallas_call(
        backward_kernel,
        out_shape=[
            jax.ShapeDtypeStruct((NB * BLK, D), BF16),
            jax.ShapeDtypeStruct((D, NB * BLK), BF16),
        ],
        in_specs=[SMEM, VMEM, VMEM, ANY, ANY, ANY],
        out_specs=[VMEM, VMEM],
        scratch_shapes=[
            pltpu.VMEM((NB, BLK, D), BF16),
            pltpu.VMEM((D, BLK), BF16),
            pltpu.VMEM((NB, BLK, D), BF16),
            pltpu.VMEM((2, BLK, BLK), BF16),
            pltpu.VMEM((BLK, BLK), BF16),
            pltpu.VMEM((BLK, 128), F32),
            pltpu.VMEM((BLK, D), F32),
            pltpu.VMEM((NB, D, BLK), F32),
            pltpu.SemaphoreType.DMA((NB,)),
            pltpu.SemaphoreType.DMA((NB,)),
            pltpu.SemaphoreType.DMA((2,)),
        ],
        compiler_params=pltpu.CompilerParams(vmem_limit_bytes=60 * 2**20),
        name="backward",
    )(tiles, rows, m, e, queries, passages)


def per_device(queries, passages, tiles, positives, cotangent):
    col_index = lax.axis_index("pa")
    place = (positives % BLK).reshape(NB, BLK).astype(F32)
    weight = cotangent.reshape(NB, BLK)
    given = jnp.concatenate([weight, place, jnp.zeros((8, BLK), F32)], axis=0)
    e, m, stats = forward(tiles, given, queries, passages)
    peak = lax.pmax(stats[0:4], "pa")
    total, picked = lax.psum((stats[4:8] * jnp.exp(stats[0:4] - peak), stats[8:12]), "pa")
    losses_all = (peak + jnp.log(total) - picked).reshape(-1)
    share = NB * BLK // lax.axis_size("pa")
    losses = lax.dynamic_slice_in_dim(losses_all, col_index * share, share, 0)
    rows = jnp.concatenate([peak, total, weight, place], axis=0)
    dq, dp = backward(tiles, rows, m, e, queries, passages)
    query_grads = lax.psum_scatter(dq, "pa", scatter_dimension=0, tiled=True)
    passage_grads = lax.psum_scatter(dp, "pb", scatter_dimension=0, tiled=True).T
    return losses, query_grads, passage_grads


def solution(mesh):
    in_specs = (P("pb", None), P("pa", None), P(), P("pb"), P("pb"))
    out_specs = (P(("pb", "pa")), P(("pb", "pa"), None), P("pa", "pb"))
    return jax.shard_map(
        per_device, mesh=mesh, in_specs=in_specs, out_specs=out_specs, check_vma=False
    )
```

```python
import jax
import jax.numpy as jnp
from jax import lax
from jax.experimental import pallas as pl
from jax.experimental.pallas import tpu as pltpu
from jax.sharding import PartitionSpec as P

D = 768
BLK = 1024
NB = 4
SCALE = D ** (-0.5)
LOG2E = 1.4426950408889634
CH = 256
F32 = jnp.float32
BF16 = jnp.bfloat16
LOW = -1e30


def listed(tiles_ref, group, owner, j):
    row = group * NB + j // NB
    block = owner * NB + j % NB
    hit = jnp.int32(0)
    for t in range(8):
        hit = hit | (tiles_ref[row, t] == block).astype(jnp.int32)
    return hit


def lane_iota(rows):
    return lax.broadcasted_iota(jnp.int32, (rows, 128), 1)


def column(x, lane):
    return jnp.sum(jnp.where(lane_iota(x.shape[0]) == lane, x, 0.0), axis=1, keepdims=True)


def forward_kernel(tiles_ref, rows_ref, q_hbm, p_hbm, e_hbm, m_ref, stats_ref,
                   q_v, p_v, e_v, t_v, cols_v, pick_v, q_sem, p_sem, e_sem):
    group = lax.axis_index("pb")
    owner = lax.axis_index("pa")
    q_copies = [pltpu.make_async_copy(q_hbm.at[pl.ds(b * BLK, BLK)], q_v.at[b], q_sem.at[b]) for b in range(NB)]
    p_copies = [pltpu.make_async_copy(p_hbm.at[pl.ds(b * BLK, BLK)], p_v.at[b], p_sem.at[b]) for b in range(NB)]
    for b in range(NB):
        p_copies[b].start()
        q_copies[b].start()
    m_ref[...] = jnp.full_like(m_ref, LOW)
    t_v[...] = jnp.zeros_like(t_v)
    pick_v[...] = jnp.zeros_like(pick_v)
    cols_v[...] = jnp.zeros_like(cols_v)
    cols_v[...] = jnp.concatenate([rows_ref[...], jnp.zeros((112, BLK), F32)], axis=0).T
    for b in range(NB):
        p_copies[b].wait()
        q_copies[b].wait()

    def store(slot, n):
        return pltpu.make_async_copy(e_v.at[slot], e_hbm.at[n], e_sem.at[slot])

    def step(j, n):
        hit = listed(tiles_ref, group, owner, j)

        @pl.when(hit == 1)
        def _():
            qb = j // NB
            pb = j % NB
            slot = n % 2

            @pl.when(n >= 2)
            def _():
                store(slot, 0).wait()

            first = (owner * NB + pb) == (group * NB + qb) * 2
            for c in range(BLK // CH):
                r = pl.ds(c * CH, CH)
                s = lax.dot_general(q_v[qb, r, :], p_v[pb], (((1,), (1,)), ((), ())), preferred_element_type=F32)
                top = jnp.max(s, axis=1, keepdims=True)
                e = jnp.exp2(s * (SCALE * LOG2E) - top * (SCALE * LOG2E))
                e_v[slot, r, :] = e.astype(BF16)
                here = lane_iota(CH) == j
                m_ref[r, :] = jnp.where(here, top * SCALE, m_ref[r, :])
                t_v[r, :] = jnp.where(here, jnp.sum(e, axis=1, keepdims=True), t_v[r, :])

                @pl.when(first)
                def _():
                    pos = column(cols_v[r, :], 4 + qb)
                    wide = lax.broadcasted_iota(jnp.int32, (CH, BLK), 1).astype(F32)
                    got = jnp.sum(jnp.where(wide == pos, s, 0.0), axis=1, keepdims=True) * SCALE
                    pick_v[r, :] = jnp.where(lane_iota(CH) == qb, got, pick_v[r, :])

            store(slot, n).start()

        return n + hit

    total = lax.fori_loop(0, NB * NB, step, jnp.int32(0))

    m_rows = m_ref[...].T
    t_rows = t_v[...].T
    pick_rows = pick_v[...].T
    highs, totals = [], []
    for b in range(NB):
        m4 = m_rows[b * NB : b * NB + NB, :]
        high = jnp.max(m4, axis=0, keepdims=True)
        highs.append(high)
        totals.append(jnp.sum(t_rows[b * NB : b * NB + NB, :] * jnp.exp(m4 - high), axis=0, keepdims=True))
    stats_ref[...] = jnp.concatenate(highs + totals + [pick_rows[0:8, :]], axis=0)

    @pl.when(total >= 1)
    def _():
        store((total - 1) % 2, 0).wait()

    @pl.when(total >= 2)
    def _():
        store(total % 2, 0).wait()


def backward_kernel(tiles_ref, rows_ref, m_ref, e_hbm, q_hbm, p_hbm, dq_ref, dp_ref,
                    q_v, qt_v, p_v, e_v, g_v, cols_v, dq_v, dp_v, q_sem, p_sem, e_sem):
    group = lax.axis_index("pb")
    owner = lax.axis_index("pa")
    p_copies = [pltpu.make_async_copy(p_hbm.at[pl.ds(b * BLK, BLK)], p_v.at[b], p_sem.at[b]) for b in range(NB)]
    q_copies = [pltpu.make_async_copy(q_hbm.at[pl.ds(b * BLK, BLK)], q_v.at[b], q_sem.at[b]) for b in range(NB)]
    for b in range(NB):
        p_copies[b].start()
        q_copies[b].start()

    def load(slot, n):
        return pltpu.make_async_copy(e_hbm.at[n], e_v.at[slot], e_sem.at[slot])

    count = lax.fori_loop(0, NB * NB, lambda j, n: n + listed(tiles_ref, group, owner, j), jnp.int32(0))

    @pl.when(count >= 1)
    def _():
        load(0, 0).start()

    cols_v[...] = jnp.concatenate([rows_ref[...], jnp.zeros((112, BLK), F32)], axis=0).T
    dp_v[...] = jnp.zeros_like(dp_v)
    for b in range(NB):
        p_copies[b].wait()
        q_copies[b].wait()

    def block(qb, n):
        qt_v[...] = q_v[qb].T
        dq_v[...] = jnp.zeros_like(dq_v)

        def step(pb, n):
            j = qb * NB + pb
            hit = listed(tiles_ref, group, owner, j)

            @pl.when(hit == 1)
            def _():
                slot = n % 2

                @pl.when(n + 1 < count)
                def _():
                    load(1 - slot, n + 1).start()

                load(slot, n).wait()
                first = (owner * NB + pb) == (group * NB + qb) * 2
                for c in range(BLK // CH):
                    r = pl.ds(c * CH, CH)
                    cols = cols_v[r, :]
                    ct = column(cols, 8 + qb) * SCALE
                    factor = ct * jnp.exp(column(m_ref[r, :], j) - column(cols, qb)) / column(cols, 4 + qb)
                    pos = jnp.where(first, column(cols, 12 + qb), -1.0)
                    wide = lax.broadcasted_iota(jnp.int32, (CH, BLK), 1).astype(F32)
                    g = e_v[slot, r, :].astype(F32) * factor - jnp.where(wide == pos, ct, 0.0)
                    g = g.astype(BF16)
                    g_v[r, :] = g
                    dq_v[r, :] += jnp.dot(g, p_v[pb], preferred_element_type=F32)
                for c in range(3):
                    r = pl.ds(c * CH, CH)
                    dp_v[pb, r, :] += jnp.dot(qt_v[r, :], g_v[...], preferred_element_type=F32)

            return n + hit

        n = lax.fori_loop(0, NB, step, n)
        dq_ref[pl.ds(qb * BLK, BLK), :] = dq_v[...].astype(BF16)
        return n

    lax.fori_loop(0, NB, block, jnp.int32(0))
    for b in range(NB):
        dp_ref[:, pl.ds(b * BLK, BLK)] = dp_v[b].astype(BF16)


def around():
    group, owner = lax.axis_index("pb"), lax.axis_index("pa")
    return group // 2, group % 2, owner // 4, owner % 4


def device(x, core, z, y):
    return (x * 2 + core, z * 4 + y)


def greet(devices):
    barrier = pltpu.get_barrier_semaphore()
    for dev in devices:
        pl.semaphore_signal(barrier, inc=1, device_id=dev, device_id_type=pl.DeviceIdType.MESH)
    pl.semaphore_wait(barrier, len(devices))


def remote(src, dst, send_sem, recv_sem, dev):
    return pltpu.make_async_remote_copy(
        src_ref=src, dst_ref=dst, send_sem=send_sem, recv_sem=recv_sem,
        device_id=dev, device_id_type=pl.DeviceIdType.MESH)


def stats_kernel(rows_ref, out_ref, losses_ref, now, buf, send_sem, recv_sem):
    x, core, z, y = around()
    peers = [[device(x, core, (z + d) % 4, y) for d in (1, 2, 3)], [device(x, core, z, (y + d) % 4) for d in (1, 2, 3)]]
    greet(peers[0] + peers[1])
    now[0] = rows_ref[...]
    for stage in range(2):
        copies = [
            remote(now.at[stage], buf.at[stage, d], send_sem.at[stage, d], recv_sem.at[stage, d], peers[stage][d])
            for d in range(3)
        ]
        for c in copies:
            c.start()
        for c in copies:
            c.wait()
        parts = [now[stage]] + [buf[stage, d] for d in range(3)]
        high = parts[0][0:4]
        for p in parts[1:]:
            high = jnp.maximum(high, p[0:4])
        total = sum(p[4:8] * jnp.exp(p[0:4] - high) for p in parts)
        rest = sum(p[8:16] for p in parts)
        now[stage + 1] = jnp.concatenate([high, total, rest], axis=0)
    out_ref[...] = now[2]
    span = pl.ds(pl.multiple_of(y * 256, 256), 256)
    losses_ref[...] = now[2, pl.ds(z, 1), span] + jnp.log(now[2, pl.ds(4 + z, 1), span]) - now[2, pl.ds(8 + z, 1), span]


AHEAD, RAW, SUMMED = 0, 1, 2


class Ring:
    def __init__(self, me, chunk, neighbours, buf, acc, send_sem, recv_sem):
        self.me, self.chunk, self.buf, self.acc = me, chunk, buf, acc
        self.send = lambda d, kind, src: remote(
            src, buf.at[d, kind], send_sem.at[d, kind], recv_sem.at[d, kind], neighbours[d])
        self.sent = {}

    def at(self, step, half):
        return self.chunk((self.me + step) % 4, half)

    def go(self, d, kind, src):
        c = self.send(d, kind, src)
        c.start()
        self.sent[d, kind] = c

    def ahead(self):
        self.go(0, AHEAD, self.at(2, 0))
        self.go(1, AHEAD, self.at(2, 1))

    def raw(self):
        self.go(0, RAW, self.at(1, 1))
        self.go(1, RAW, self.at(3, 0))

    def forward(self):
        for d, step in ((0, 1), (1, 3)):
            self.sent[d, AHEAD].wait_recv()
            self.acc[d] = (self.at(step, d)[...].astype(F32) + self.buf[d, AHEAD].astype(F32)).astype(BF16)
            self.go(d, SUMMED, self.acc.at[d])

    def result(self, half):
        a, b = (SUMMED, RAW) if half == 0 else (RAW, SUMMED)
        self.sent[0, a].wait_recv()
        self.sent[1, b].wait_recv()
        return self.at(0, half)[...].astype(F32) + self.buf[0, a].astype(F32) + self.buf[1, b].astype(F32)

    def drain(self):
        for c in self.sent.values():
            c.wait_send()


def scatter_kernel(dq_ref, dp_ref, qg_ref, pg_ref,
                   a1_buf, a1_acc, a1_sum, b1_buf, b1_acc, b1_sum, a2_buf, a2_acc, b2_buf, b2_acc,
                   x_buf, x_acc, x_sum, core_buf, ssem, rsem, core_ssem, core_rsem):
    x, core, z, y = around()
    z_next = [device(x, core, (z + 1) % 4, y), device(x, core, (z + 3) % 4, y)]
    y_next = [device(x, core, z, (y + 1) % 4), device(x, core, z, (y + 3) % 4)]
    x_next = [device((x + 1) % 4, core, z, y), device((x + 3) % 4, core, z, y)]
    mate = device(x, 1 - core, z, y)
    greet(z_next + y_next + x_next + [mate])
    left, right = pl.ds(0, 384), pl.ds(384, 384)
    a1 = Ring(z, lambda j, h: dq_ref.at[j, pl.ds(2 * h, 2), :, left], z_next, a1_buf, a1_acc, ssem.at[0], rsem.at[0])
    b1 = Ring(y, lambda j, h: dq_ref.at[pl.ds(2 * h, 2), j, :, right], y_next, b1_buf, b1_acc, ssem.at[1], rsem.at[1])
    a2 = Ring(y, lambda j, h: a1_sum.at[j, pl.ds(128 * h, 128)], y_next, a2_buf, a2_acc, ssem.at[2], rsem.at[2])
    b2 = Ring(z, lambda j, h: b1_sum.at[j, pl.ds(128 * h, 128)], z_next, b2_buf, b2_acc, ssem.at[3], rsem.at[3])
    xr = Ring(x, lambda j, h: x_sum.at[j, h], x_next, x_buf, x_acc, ssem.at[4], rsem.at[4])
    cores = []
    for k, step in enumerate((2, 1, 3, 0)):
        place = (x + step) % 4
        cores.append(remote(dp_ref.at[place, 1 - core], core_buf.at[k], core_ssem.at[k], core_rsem.at[k], mate))
    cores[0].start()
    a1.ahead()
    b1.ahead()
    cores[1].start()
    a1.raw()
    b1.raw()
    cores[2].start()
    cores[3].start()

    def add_core(k, step):
        place = (x + step) % 4
        cores[k].wait_recv()
        for h in range(2):
            x_sum[place, h] = (dp_ref[place, core, h].astype(F32) + core_buf[k, h].astype(F32)).astype(BF16)

    add_core(0, 2)
    xr.ahead()
    add_core(1, 1)
    add_core(2, 3)
    xr.raw()
    add_core(3, 0)
    a1.forward()
    b1.forward()
    xr.forward()
    for h in range(2):
        a1_sum[pl.ds(2 * h, 2)] = a1.result(h).astype(BF16)
    a2.ahead()
    a2.raw()
    for h in range(2):
        b1_sum[pl.ds(2 * h, 2)] = b1.result(h).astype(BF16)
    b2.ahead()
    b2.raw()
    a2.forward()
    b2.forward()
    for h in range(2):
        pg_ref[pl.ds(48 * h, 48), :] = xr.result(h)
    for h in range(2):
        qg_ref[pl.ds(128 * h, 128), left] = a2.result(h).astype(BF16)
        qg_ref[pl.ds(128 * h, 128), right] = b2.result(h).astype(BF16)
    for ring in (a1, b1, a2, b2, xr):
        ring.drain()
    for c in cores:
        c.wait_send()


SMEM = pl.BlockSpec(memory_space=pltpu.SMEM)
VMEM = pl.BlockSpec(memory_space=pltpu.VMEM)
ANY = pl.BlockSpec(memory_space=pl.ANY)


def forward(tiles, rows, queries, passages):
    return pl.pallas_call(
        forward_kernel,
        out_shape=[
            jax.ShapeDtypeStruct((NB * NB, BLK, BLK), BF16),
            jax.ShapeDtypeStruct((BLK, 128), F32),
            jax.ShapeDtypeStruct((16, BLK), F32),
        ],
        in_specs=[SMEM, VMEM, ANY, ANY],
        out_specs=[ANY, VMEM, VMEM],
        scratch_shapes=[
            pltpu.VMEM((NB, BLK, D), BF16),
            pltpu.VMEM((NB, BLK, D), BF16),
            pltpu.VMEM((2, BLK, BLK), BF16),
            pltpu.VMEM((BLK, 128), F32),
            pltpu.VMEM((BLK, 128), F32),
            pltpu.VMEM((BLK, 128), F32),
            pltpu.SemaphoreType.DMA((NB,)),
            pltpu.SemaphoreType.DMA((NB,)),
            pltpu.SemaphoreType.DMA((2,)),
        ],
        compiler_params=pltpu.CompilerParams(vmem_limit_bytes=56 * 2**20),
        name="forward",
    )(tiles, rows, queries, passages)


def backward(tiles, rows, m, e, queries, passages):
    return pl.pallas_call(
        backward_kernel,
        out_shape=[
            jax.ShapeDtypeStruct((NB * BLK, D), BF16),
            jax.ShapeDtypeStruct((D, NB * BLK), BF16),
        ],
        in_specs=[SMEM, VMEM, VMEM, ANY, ANY, ANY],
        out_specs=[VMEM, VMEM],
        scratch_shapes=[
            pltpu.VMEM((NB, BLK, D), BF16),
            pltpu.VMEM((D, BLK), BF16),
            pltpu.VMEM((NB, BLK, D), BF16),
            pltpu.VMEM((2, BLK, BLK), BF16),
            pltpu.VMEM((BLK, BLK), BF16),
            pltpu.VMEM((BLK, 128), F32),
            pltpu.VMEM((BLK, D), F32),
            pltpu.VMEM((NB, D, BLK), F32),
            pltpu.SemaphoreType.DMA((NB,)),
            pltpu.SemaphoreType.DMA((NB,)),
            pltpu.SemaphoreType.DMA((2,)),
        ],
        compiler_params=pltpu.CompilerParams(vmem_limit_bytes=60 * 2**20),
        name="backward",
    )(tiles, rows, m, e, queries, passages)


def combine(rows):
    return pl.pallas_call(
        stats_kernel,
        out_shape=[jax.ShapeDtypeStruct((16, BLK), F32), jax.ShapeDtypeStruct((1, 256), F32)],
        in_specs=[VMEM],
        out_specs=[VMEM, VMEM],
        scratch_shapes=[
            pltpu.VMEM((3, 16, BLK), F32),
            pltpu.VMEM((2, 3, 16, BLK), F32),
            pltpu.SemaphoreType.DMA((2, 3)),
            pltpu.SemaphoreType.DMA((2, 3)),
        ],
        compiler_params=pltpu.CompilerParams(collective_id=1, has_side_effects=True),
        name="combine",
    )(rows)


def scatter(dq, dp):
    big, small = (2, 3, 2, 256, 384), (2, 3, 128, 384)
    return pl.pallas_call(
        scatter_kernel,
        out_shape=[jax.ShapeDtypeStruct((256, D), BF16), jax.ShapeDtypeStruct((96, NB * BLK), F32)],
        in_specs=[VMEM, VMEM],
        out_specs=[VMEM, VMEM],
        scratch_shapes=[
            pltpu.VMEM(big, BF16), pltpu.VMEM((2, 2, 256, 384), BF16), pltpu.VMEM((4, 256, 384), BF16),
            pltpu.VMEM(big, BF16), pltpu.VMEM((2, 2, 256, 384), BF16), pltpu.VMEM((4, 256, 384), BF16),
            pltpu.VMEM(small, BF16), pltpu.VMEM((2, 128, 384), BF16),
            pltpu.VMEM(small, BF16), pltpu.VMEM((2, 128, 384), BF16),
            pltpu.VMEM((2, 3, 48, NB * BLK), BF16), pltpu.VMEM((2, 48, NB * BLK), BF16),
            pltpu.VMEM((4, 2, 48, NB * BLK), BF16),
            pltpu.VMEM((4, 2, 48, NB * BLK), BF16),
            pltpu.SemaphoreType.DMA((5, 2, 3)), pltpu.SemaphoreType.DMA((5, 2, 3)),
            pltpu.SemaphoreType.DMA((4,)), pltpu.SemaphoreType.DMA((4,)),
        ],
        compiler_params=pltpu.CompilerParams(
            collective_id=2, has_side_effects=True, vmem_limit_bytes=56 * 2**20),
        name="scatter",
    )(dq.reshape(4, 4, 256, D), dp.reshape(4, 2, 2, 48, NB * BLK))


def per_device(queries, passages, tiles, positives, cotangent):
    place = (positives % BLK).reshape(NB, BLK).astype(F32)
    weight = cotangent.reshape(NB, BLK)
    given = jnp.concatenate([weight, place, jnp.zeros((8, BLK), F32)], axis=0)
    e, m, stats = forward(tiles, given, queries, passages)
    stats, losses = combine(stats)
    rows = jnp.concatenate([stats[0:8], weight, place], axis=0)
    dq, dp = backward(tiles, rows, m, e, queries, passages)
    query_grads, passage_grads = scatter(dq, dp)
    return losses.reshape(256), query_grads, passage_grads.T.astype(BF16)


def solution(mesh):
    in_specs = (P("pb", None), P("pa", None), P(), P("pb"), P("pb"))
    out_specs = (P(("pb", "pa")), P(("pb", "pa"), None), P("pa", "pb"))
    return jax.shard_map(
        per_device, mesh=mesh, in_specs=in_specs, out_specs=out_specs, check_vma=False
    )
```

```python
import jax
import jax.numpy as jnp
from jax import lax
from jax.experimental import pallas as pl
from jax.experimental.pallas import tpu as pltpu
from jax.sharding import PartitionSpec as P

D = 768
BLK = 1024
NB = 4
LISTED = 8
SL = 64
SCALE = D ** (-0.5)
LOG2E = 1.4426950408889634
CH = 256
F32 = jnp.float32
BF16 = jnp.bfloat16


def around():
    group, owner = lax.axis_index("pb"), lax.axis_index("pa")
    return group // 2, group % 2, owner // 4, owner % 4


def device(x, core, z, y):
    return (x * 2 + core, z * 4 + y)


def greet(devices):
    barrier = pltpu.get_barrier_semaphore()
    for dev in devices:
        pl.semaphore_signal(barrier, inc=1, device_id=dev, device_id_type=pl.DeviceIdType.MESH)
    pl.semaphore_wait(barrier, len(devices))


def remote(src, dst, send_sem, recv_sem, dev):
    return pltpu.make_async_remote_copy(
        src_ref=src, dst_ref=dst, send_sem=send_sem, recv_sem=recv_sem,
        device_id=dev, device_id_type=pl.DeviceIdType.MESH)


def stats_kernel(rows_ref, out_ref, losses_ref, now, buf, send_sem, recv_sem):
    x, core, z, y = around()
    peers = [[device(x, core, (z + d) % 4, y) for d in (1, 2, 3)], [device(x, core, z, (y + d) % 4) for d in (1, 2, 3)]]
    greet(peers[0] + peers[1])
    now[0] = rows_ref[...]
    for stage in range(2):
        copies = [
            remote(now.at[stage], buf.at[stage, d], send_sem.at[stage, d], recv_sem.at[stage, d], peers[stage][d])
            for d in range(3)
        ]
        for c in copies:
            c.start()
        for c in copies:
            c.wait()
        parts = [now[stage]] + [buf[stage, d] for d in range(3)]
        high = parts[0][0:4]
        for p in parts[1:]:
            high = jnp.maximum(high, p[0:4])
        total = sum(p[4:8] * jnp.exp(p[0:4] - high) for p in parts)
        rest = sum(p[8:16] for p in parts)
        now[stage + 1] = jnp.concatenate([high, total, rest], axis=0)
    out_ref[...] = now[2]
    span = pl.ds(pl.multiple_of(y * 256, 256), 256)
    losses_ref[...] = now[2, pl.ds(z, 1), span] + jnp.log(now[2, pl.ds(4 + z, 1), span]) - now[2, pl.ds(8 + z, 1), span]


AHEAD, RAW, SUMMED = 0, 1, 2


class Ring:
    def __init__(self, me, chunk, neighbours, buf, acc, send_sem, recv_sem):
        self.me, self.chunk, self.buf, self.acc = me, chunk, buf, acc
        self.send = lambda d, kind, src: remote(
            src, buf.at[d, kind], send_sem.at[d, kind], recv_sem.at[d, kind], neighbours[d])
        self.sent = {}

    def at(self, step, half):
        return self.chunk((self.me + step) % 4, half)

    def go(self, d, kind, src):
        c = self.send(d, kind, src)
        c.start()
        self.sent[d, kind] = c

    def ahead(self):
        self.go(0, AHEAD, self.at(2, 0))
        self.go(1, AHEAD, self.at(2, 1))

    def raw(self):
        self.go(0, RAW, self.at(1, 1))
        self.go(1, RAW, self.at(3, 0))

    def forward(self):
        for d, step in ((0, 1), (1, 3)):
            self.sent[d, AHEAD].wait_recv()
            self.acc[d] = (self.at(step, d)[...].astype(F32) + self.buf[d, AHEAD].astype(F32)).astype(BF16)
            self.go(d, SUMMED, self.acc.at[d])

    def result(self, half):
        a, b = (SUMMED, RAW) if half == 0 else (RAW, SUMMED)
        self.sent[0, a].wait_recv()
        self.sent[1, b].wait_recv()
        return self.at(0, half)[...].astype(F32) + self.buf[0, a].astype(F32) + self.buf[1, b].astype(F32)

    def drain(self):
        for c in self.sent.values():
            c.wait_send()


def distribute_kernel(p_hbm, sel_hbm, own_sem, ssem, rsem, mate_ssem, mate_rsem, x_ssem, x_rsem, fwd_ssem, fwd_rsem):
    x, core, z, y = around()
    me = z * 4 + y
    mate = device(x, 1 - core, z, y)
    to = (x + 1 + 2 * core) % 4
    source = (x + 3 + 2 * core) % 4
    x_to, x_from = device(to, core, z, y), device(source, core, z, y)
    peers = [(dz, dy) for dz in (0, 2, 1, 3) for dy in (2, 1, 3, 0) if dz or dy]
    place = {k: ((z + k[0]) % 4, (y + k[1]) % 4) for k in peers}
    greet([device(x, core, *place[k]) for k in peers] + [mate, x_to, x_from])
    mine = (x + core) % 4
    theirs = (source + core) % 4
    own = pltpu.make_async_copy(p_hbm.at[mine, me], sel_hbm.at[mine, me], own_sem)
    own.start()
    sends = []
    for k in peers:
        tz, ty = place[k]
        c = remote(p_hbm.at[mine, tz * 4 + ty], sel_hbm.at[mine, me], ssem.at[tz * 4 + ty], rsem.at[me],
                   device(x, core, tz, ty))
        c.start()
        sends.append(c)
    hands = []
    own.wait()

    def group(b, zz):
        return sel_hbm.at[b, pl.ds(zz * 4, 4)]

    order = [(z + dz) % 4 for dz in (0, 2, 3, 1)]
    for n, zz in enumerate(order):
        for dy in range(4):
            if n == 0 and dy == 0:
                continue
            yy = (y + dy) % 4
            remote(p_hbm.at[mine, me], sel_hbm.at[mine, zz * 4 + yy], ssem.at[me], rsem.at[zz * 4 + yy],
                   device(x, core, zz, yy)).wait_recv()
        for a, b, dev in ((x_ssem, x_rsem, x_to), (mate_ssem, mate_rsem, mate)):
            c = remote(group(mine, zz), group(mine, zz), a.at[n], b.at[n], dev)
            c.start()
            hands.append(c)
    for n, zz in enumerate(order):
        remote(group(mine, zz), group(theirs, zz), x_ssem.at[n], x_rsem.at[n], x_from).wait_recv()
        c = remote(group(theirs, zz), group(theirs, zz), fwd_ssem.at[n], fwd_rsem.at[n], mate)
        c.start()
        hands.append(c)
    for n, zz in enumerate(order):
        for a, b in ((mate_ssem, mate_rsem), (fwd_ssem, fwd_rsem)):
            remote(group(mine, zz), group(mine, zz), a.at[n], b.at[n], mate).wait_recv()
    for c in sends + hands:
        c.wait_send()


def forward_kernel(tiles_ref, rows_ref, q_hbm, sel_hbm, e_ref, pq_ref, stats_ref, q_v, sel_v, q_sem, sel_sem):
    group = lax.axis_index("pb")
    owner = lax.axis_index("pa")
    sel_copy = pltpu.make_async_copy(sel_hbm, sel_v, sel_sem)
    sel_copy.start()
    q_copies = [pltpu.make_async_copy(q_hbm.at[b], q_v.at[b], q_sem.at[b]) for b in range(NB)]
    for c in q_copies:
        c.start()
    sel_copy.wait()
    for b in range(NB):
        for t in range(LISTED):
            block = tiles_ref[group * NB + b, t]
            pq_ref[b, pl.ds(t * SL, SL), :] = sel_v[block % NB, block // NB]
        q_copies[b].wait()
        for c in range(BLK // CH):
            r = pl.ds(c * CH, CH)
            s = lax.dot_general(pq_ref[b], q_v[b, r, :], (((1,), (1,)), ((), ())), preferred_element_type=F32)
            top = jnp.max(s, axis=0, keepdims=True)
            e = jnp.exp2(s * (SCALE * LOG2E) - top * (SCALE * LOG2E))
            e_ref[b, :, r] = e.astype(BF16)
            stats_ref[b : b + 1, r] = top * SCALE
            stats_ref[NB + b : NB + b + 1, r] = jnp.sum(e, axis=0, keepdims=True)
            pos = rows_ref[NB + b : NB + b + 1, r] - (owner * SL).astype(F32)
            at = lax.broadcasted_iota(jnp.int32, (SL, CH), 0).astype(F32) == pos
            stats_ref[2 * NB + b : 2 * NB + b + 1, r] = (
                jnp.sum(jnp.where(at, s[0:SL], 0.0), axis=0, keepdims=True) * SCALE)
    stats_ref[12:16, :] = jnp.zeros((4, BLK), F32)


def backward_kernel(tiles_ref, rows_ref, m_ref, all_ref, e_ref, pq_ref, q_ref, dq_ref, dp_ref, part_v, slot_s):
    group = lax.axis_index("pb")
    owner = lax.axis_index("pa")
    for b in range(NB):
        part_v[b, LISTED] = jnp.zeros((SL, D), F32)

        def clear(p, carry, b=b):
            slot_s[b, p] = LISTED
            return carry

        lax.fori_loop(0, 64, clear, 0)
        for t in range(LISTED):
            slot_s[b, tiles_ref[group * NB + b, t]] = t
    for b in range(NB):
        one = slice(b, b + 1)
        weight = rows_ref[one, :] * SCALE
        factor = weight * jnp.exp(m_ref[one, :] - all_ref[one, :]) / all_ref[NB + b : NB + b + 1, :]
        pos = rows_ref[NB + b : NB + b + 1, :] - (owner * SL).astype(F32)
        at = lax.broadcasted_iota(jnp.int32, (SL, BLK), 0).astype(F32) == pos
        g0 = (e_ref[b, 0:SL, :].astype(F32) * factor - jnp.where(at, weight, 0.0)).astype(BF16)
        g1 = (e_ref[b, SL:, :].astype(F32) * factor).astype(BF16)
        g = jnp.concatenate([g0, g1], axis=0)
        dq_ref[b] = lax.dot_general(
            g, pq_ref[b], (((0,), (0,)), ((), ())), preferred_element_type=F32).astype(BF16)
        part_v[b, 0:LISTED] = jnp.dot(g, q_ref[b], preferred_element_type=F32).reshape(LISTED, SL, D)

    def dense(n, carry):
        rows = []
        for k in range(4):
            p = n * 4 + k
            rows.append(sum(part_v[b, slot_s[b, p]] for b in range(NB)))
        dp_ref[:, pl.ds(pl.multiple_of(n * 256, 256), 256)] = jnp.concatenate(rows, axis=0).astype(BF16).T
        return carry

    lax.fori_loop(0, 16, dense, 0)


def scatter_kernel(dq_ref, dp_ref, qg_ref, pg_ref,
                   a1_buf, a1_acc, a1_sum, b1_buf, b1_acc, b1_sum, a2_buf, a2_acc, b2_buf, b2_acc,
                   x_buf, x_acc, x_sum, core_buf, back, got, ssem, rsem, core_ssem, core_rsem, back_ssem, back_rsem):
    x, core, z, y = around()
    z_next = [device(x, core, (z + 1) % 4, y), device(x, core, (z + 3) % 4, y)]
    y_next = [device(x, core, z, (y + 1) % 4), device(x, core, z, (y + 3) % 4)]
    x_next = [device((x + 1) % 4, core, z, y), device((x + 3) % 4, core, z, y)]
    mate = device(x, 1 - core, z, y)
    me = z * 4 + y
    peers = [(dz, dy) for dz in (2, 1, 3, 0) for dy in (2, 1, 3, 0) if dz or dy]
    greet([device(x, core, (z + dz) % 4, (y + dy) % 4) for dz, dy in peers] + x_next + [mate])
    left, right = pl.ds(0, 384), pl.ds(384, 384)
    a1 = Ring(z, lambda j, h: dq_ref.at[j, pl.ds(2 * h, 2), :, left], z_next, a1_buf, a1_acc, ssem.at[0], rsem.at[0])
    b1 = Ring(y, lambda j, h: dq_ref.at[pl.ds(2 * h, 2), j, :, right], y_next, b1_buf, b1_acc, ssem.at[1], rsem.at[1])
    a2 = Ring(y, lambda j, h: a1_sum.at[j, pl.ds(128 * h, 128)], y_next, a2_buf, a2_acc, ssem.at[2], rsem.at[2])
    b2 = Ring(z, lambda j, h: b1_sum.at[j, pl.ds(128 * h, 128)], z_next, b2_buf, b2_acc, ssem.at[3], rsem.at[3])
    xr = Ring(x, lambda j, h: x_sum.at[j, h], x_next, x_buf, x_acc, ssem.at[4], rsem.at[4])
    cores = []
    for k, step in enumerate((2, 1, 3, 0)):
        place = (x + step) % 4
        cores.append(remote(dp_ref.at[place, 1 - core], core_buf.at[k], core_ssem.at[k], core_rsem.at[k], mate))
    cores[0].start()
    a1.ahead()
    b1.ahead()
    cores[1].start()
    a1.raw()
    b1.raw()
    cores[2].start()
    cores[3].start()

    def add_core(k, step):
        place = (x + step) % 4
        cores[k].wait_recv()
        for h in range(2):
            x_sum[place, h] = (dp_ref[place, core, h].astype(F32) + core_buf[k, h].astype(F32)).astype(BF16)

    add_core(0, 2)
    xr.ahead()
    add_core(1, 1)
    add_core(2, 3)
    xr.raw()
    add_core(3, 0)
    a1.forward()
    b1.forward()
    xr.forward()
    for h in range(2):
        a1_sum[pl.ds(2 * h, 2)] = a1.result(h).astype(BF16)
    a2.ahead()
    a2.raw()
    for h in range(2):
        b1_sum[pl.ds(2 * h, 2)] = b1.result(h).astype(BF16)
    b2.ahead()
    b2.raw()
    a2.forward()
    b2.forward()
    for h in range(2):
        res = xr.result(h).astype(BF16)
        for n in range(16):
            back[n, pl.ds(48 * h, 48), :] = res[:, n * 256 : n * 256 + 256]
    returns = []
    for dz, dy in peers:
        tz, ty = (z + dz) % 4, (y + dy) % 4
        c = remote(back.at[tz * 4 + ty], got.at[me], back_ssem.at[tz * 4 + ty], back_rsem.at[me], device(x, core, tz, ty))
        c.start()
        returns.append(c)
    for h in range(2):
        qg_ref[pl.ds(128 * h, 128), left] = a2.result(h).astype(BF16)
        qg_ref[pl.ds(128 * h, 128), right] = b2.result(h).astype(BF16)
    def lay(n, shard):
        rows = shard.astype(F32).T.astype(BF16)
        for b in range(NB):
            pg_ref[b, n] = rows[b * SL : b * SL + SL, :]

    lay(me, back[me])
    for dz, dy in peers:
        n = (z + dz) % 4 * 4 + (y + dy) % 4
        remote(back.at[n], got.at[n], back_ssem.at[n], back_rsem.at[n], device(x, core, (z + dz) % 4, (y + dy) % 4)).wait_recv()
        lay(n, got[n])
    for ring in (a1, b1, a2, b2, xr):
        ring.drain()
    for c in returns:
        c.wait_send()
    for c in cores:
        c.wait_send()


SMEM = pl.BlockSpec(memory_space=pltpu.SMEM)
VMEM = pl.BlockSpec(memory_space=pltpu.VMEM)
ANY = pl.BlockSpec(memory_space=pl.ANY)


def distribute(passages):
    return pl.pallas_call(
        distribute_kernel,
        out_shape=jax.ShapeDtypeStruct((NB, 16, SL, D), BF16),
        in_specs=[ANY],
        out_specs=ANY,
        scratch_shapes=[pltpu.SemaphoreType.DMA] + [pltpu.SemaphoreType.DMA((16,))] * 2
        + [pltpu.SemaphoreType.DMA((4,))] * 6,
        compiler_params=pltpu.CompilerParams(collective_id=3, has_side_effects=True),
        name="distribute",
    )(passages.reshape(NB, 16, SL, D))


def forward(tiles, rows, queries, sel):
    return pl.pallas_call(
        forward_kernel,
        out_shape=[
            jax.ShapeDtypeStruct((NB, LISTED * SL, BLK), BF16),
            jax.ShapeDtypeStruct((NB, LISTED * SL, D), BF16),
            jax.ShapeDtypeStruct((16, BLK), F32),
        ],
        in_specs=[SMEM, VMEM, ANY, ANY],
        out_specs=[VMEM, VMEM, VMEM],
        scratch_shapes=[
            pltpu.VMEM((NB, BLK, D), BF16),
            pltpu.VMEM((NB, 16, SL, D), BF16),
            pltpu.SemaphoreType.DMA((NB,)),
            pltpu.SemaphoreType.DMA,
        ],
        compiler_params=pltpu.CompilerParams(vmem_limit_bytes=56 * 2**20),
        name="forward",
    )(tiles, rows, queries, sel)


def backward(tiles, rows, m, everyone, e, pq, queries):
    return pl.pallas_call(
        backward_kernel,
        out_shape=[
            jax.ShapeDtypeStruct((NB, BLK, D), BF16),
            jax.ShapeDtypeStruct((D, NB * BLK), BF16),
        ],
        in_specs=[SMEM] + [VMEM] * 6,
        out_specs=[VMEM, VMEM],
        scratch_shapes=[
            pltpu.VMEM((NB, LISTED + 1, SL, D), F32),
            pltpu.SMEM((NB, 64), jnp.int32),
        ],
        compiler_params=pltpu.CompilerParams(vmem_limit_bytes=58 * 2**20),
        name="backward",
    )(tiles, rows, m, everyone, e, pq, queries)


def combine(rows):
    return pl.pallas_call(
        stats_kernel,
        out_shape=[jax.ShapeDtypeStruct((16, BLK), F32), jax.ShapeDtypeStruct((1, 256), F32)],
        in_specs=[VMEM],
        out_specs=[VMEM, VMEM],
        scratch_shapes=[
            pltpu.VMEM((3, 16, BLK), F32),
            pltpu.VMEM((2, 3, 16, BLK), F32),
            pltpu.SemaphoreType.DMA((2, 3)),
            pltpu.SemaphoreType.DMA((2, 3)),
        ],
        compiler_params=pltpu.CompilerParams(collective_id=1, has_side_effects=True),
        name="combine",
    )(rows)


def scatter(dq, dp):
    big, small = (2, 3, 2, 256, 384), (2, 3, 128, 384)
    return pl.pallas_call(
        scatter_kernel,
        out_shape=[jax.ShapeDtypeStruct((256, D), BF16), jax.ShapeDtypeStruct((NB, 16, SL, 96), BF16)],
        in_specs=[VMEM, VMEM],
        out_specs=[VMEM, VMEM],
        scratch_shapes=[
            pltpu.VMEM(big, BF16), pltpu.VMEM((2, 2, 256, 384), BF16), pltpu.VMEM((4, 256, 384), BF16),
            pltpu.VMEM(big, BF16), pltpu.VMEM((2, 2, 256, 384), BF16), pltpu.VMEM((4, 256, 384), BF16),
            pltpu.VMEM(small, BF16), pltpu.VMEM((2, 128, 384), BF16),
            pltpu.VMEM(small, BF16), pltpu.VMEM((2, 128, 384), BF16),
            pltpu.VMEM((2, 3, 48, NB * BLK), BF16), pltpu.VMEM((2, 48, NB * BLK), BF16),
            pltpu.VMEM((4, 2, 48, NB * BLK), BF16),
            pltpu.VMEM((4, 2, 48, NB * BLK), BF16),
            pltpu.VMEM((16, 96, 256), BF16), pltpu.VMEM((16, 96, 256), BF16),
            pltpu.SemaphoreType.DMA((5, 2, 3)), pltpu.SemaphoreType.DMA((5, 2, 3)),
            pltpu.SemaphoreType.DMA((4,)), pltpu.SemaphoreType.DMA((4,)),
            pltpu.SemaphoreType.DMA((16,)), pltpu.SemaphoreType.DMA((16,)),
        ],
        compiler_params=pltpu.CompilerParams(
            collective_id=2, has_side_effects=True, vmem_limit_bytes=56 * 2**20),
        name="scatter",
    )(dq.reshape(4, 4, 256, D), dp.reshape(4, 2, 2, 48, NB * BLK))


def per_device(queries, passages, tiles, positives, cotangent):
    place = (positives % BLK).reshape(NB, BLK).astype(F32)
    rows = jnp.concatenate([cotangent.reshape(NB, BLK), place], axis=0)
    queries = queries.reshape(NB, BLK, D)
    sel = distribute(passages)
    e, pq, stats = forward(tiles, rows, queries, sel)
    everyone, losses = combine(stats)
    dq, dp = backward(tiles, rows, stats, everyone, e, pq, queries)
    query_grads, passage_grads = scatter(dq, dp)
    return losses.reshape(256), query_grads, passage_grads.reshape(NB * BLK, 96)


def solution(mesh):
    in_specs = (P("pb", None), P("pa", None), P(), P("pb"), P("pb"))
    out_specs = (P(("pb", "pa")), P(("pb", "pa"), None), P("pa", "pb"))
    return jax.shard_map(
        per_device, mesh=mesh, in_specs=in_specs, out_specs=out_specs, check_vma=False
    )
```

```python
import jax
import jax.numpy as jnp
from jax import lax
from jax.experimental import pallas as pl
from jax.experimental.pallas import tpu as pltpu
from jax.sharding import PartitionSpec as P

D = 768
BLK = 1024
NB = 4
LISTED = 8
SL = 64
PHASES = 4
PR = SL // PHASES
PIECES = 2
SCALE = D ** (-0.5)
LOG2E = 1.4426950408889634
CH = 256
F32 = jnp.float32
BF16 = jnp.bfloat16


def around():
    group, owner = lax.axis_index("pb"), lax.axis_index("pa")
    return group // 2, group % 2, owner // 4, owner % 4


def device(x, core, z, y):
    return (x * 2 + core, z * 4 + y)


def greet(devices):
    barrier = pltpu.get_barrier_semaphore()
    for dev in devices:
        pl.semaphore_signal(barrier, inc=1, device_id=dev, device_id_type=pl.DeviceIdType.MESH)
    pl.semaphore_wait(barrier, len(devices))


def remote(src, dst, send_sem, recv_sem, dev):
    return pltpu.make_async_remote_copy(
        src_ref=src, dst_ref=dst, send_sem=send_sem, recv_sem=recv_sem,
        device_id=dev, device_id_type=pl.DeviceIdType.MESH)


AHEAD, RAW, SUMMED = 0, 1, 2


class Ring:
    def __init__(self, me, chunk, neighbours, buf, acc, send_sem, recv_sem):
        self.me, self.chunk, self.buf, self.acc = me, chunk, buf, acc
        self.send = lambda d, kind, src: remote(
            src, buf.at[d, kind], send_sem.at[d, kind], recv_sem.at[d, kind], neighbours[d])
        self.sent = {}

    def at(self, step, half):
        return self.chunk((self.me + step) % 4, half)

    def go(self, d, kind, src):
        c = self.send(d, kind, src)
        c.start()
        self.sent[d, kind] = c

    def ahead(self):
        self.go(0, AHEAD, self.at(2, 0))
        self.go(1, AHEAD, self.at(2, 1))

    def raw(self):
        self.go(0, RAW, self.at(1, 1))
        self.go(1, RAW, self.at(3, 0))

    def forward(self):
        for d, step in ((0, 1), (1, 3)):
            self.sent[d, AHEAD].wait_recv()
            self.acc[d] = (self.at(step, d)[...].astype(F32) + self.buf[d, AHEAD].astype(F32)).astype(BF16)
            self.go(d, SUMMED, self.acc.at[d])

    def result(self, half):
        a, b = (SUMMED, RAW) if half == 0 else (RAW, SUMMED)
        self.sent[0, a].wait_recv()
        self.sent[1, b].wait_recv()
        return self.at(0, half)[...].astype(F32) + self.buf[0, a].astype(F32) + self.buf[1, b].astype(F32)

    def drain(self):
        for c in self.sent.values():
            c.wait_send()


class Exchange:
    def __init__(self, now, buf, send_sem, recv_sem, peers):
        self.now, self.buf, self.peers = now, buf, peers
        self.sems = send_sem, recv_sem
        self.sent = {}

    def start(self, stage):
        for d in range(3):
            c = remote(self.now.at[stage], self.buf.at[stage, d], self.sems[0].at[stage, d], self.sems[1].at[stage, d],
                       self.peers[stage][d])
            c.start()
            self.sent[stage, d] = c

    def parts(self, stage):
        for d in range(3):
            self.sent[stage, d].wait_recv()
        return [self.now[stage]] + [self.buf[stage, d] for d in range(3)]

    def drain(self):
        for c in self.sent.values():
            c.wait_send()


def whole_kernel(tiles_ref, pos_ref, ct_ref, q_hbm, p_hbm, losses_ref, qg_ref, pg_ref,
                 q_v, sel_v, pq_v, e_v, part_v, dp_v, slot_s,
                 now, now_buf, pick, pick_buf,
                 a1_buf, a1_acc, a1_sum, b1_buf, b1_acc, b1_sum, a2_buf, a2_acc, b2_buf, b2_acc,
                 x_buf, x_acc, core_buf, back, got,
                 q_sem, own_sem, d_ssem, d_rsem, hand_ssem, hand_rsem, ex_ssem, ex_rsem,
                 r_ssem, r_rsem, core_ssem, core_rsem, back_ssem, back_rsem):
    group, owner = lax.axis_index("pb"), lax.axis_index("pa")
    x, core, z, y = around()
    me = z * 4 + y
    peers = [((z + dz) % 4, (y + dy) % 4) for dz in (2, 1, 3, 0) for dy in (2, 1, 3, 0) if dz or dy]
    z_peers = [device(x, core, (z + d) % 4, y) for d in (1, 2, 3)]
    y_peers = [device(x, core, z, (y + d) % 4) for d in (1, 2, 3)]
    x_next = [device((x + 1) % 4, core, z, y), device((x + 3) % 4, core, z, y)]
    mate = device(x, 1 - core, z, y)
    for b in range(NB):
        pltpu.make_async_copy(q_hbm.at[b], q_v.at[b], q_sem.at[b]).start()
    greet([device(x, core, tz, ty) for tz, ty in peers] + x_next + [mate])

    to = (x + 1 + 2 * core) % 4
    source = (x + 3 + 2 * core) % 4
    x_to, x_from = device(to, core, z, y), device(source, core, z, y)
    mine = (x + core) % 4
    theirs = (source + core) % 4

    def rows(n):
        return pl.ds(n * PR, PR)

    own = pltpu.make_async_copy(p_hbm.at[mine, me], sel_v.at[mine, me], own_sem)
    own.start()
    sends = []

    def fetch(n):
        for tz, ty in peers:
            c = remote(p_hbm.at[mine, tz * 4 + ty, rows(n)], sel_v.at[mine, me, rows(n)],
                       d_ssem.at[n, tz * 4 + ty], d_rsem.at[n, me], device(x, core, tz, ty))
            c.start()
            sends.append(c)

    def hand(n, kind, b, dev):
        return remote(sel_v.at[b, :, rows(n)], sel_v.at[b, :, rows(n)], hand_ssem.at[kind, n], hand_rsem.at[kind, n], dev)

    def hand_on(n):
        hand(n, 0, theirs, x_from).wait_recv()
        c = hand(n, 2, theirs, mate)
        c.start()
        sends.append(c)

    fetch(0)
    fetch(1)
    for b in range(NB):
        def find(p, carry, b=b):
            at = jnp.int32(LISTED)
            for t in range(LISTED):
                at = jnp.where(tiles_ref[group * NB + b, t] == p, t, at)
            slot_s[b, p] = at
            return carry

        lax.fori_loop(0, 64, find, 0)
        part_v[b, LISTED] = jnp.zeros((SL, D), F32)
    now[...] = jnp.zeros_like(now)
    pick[...] = jnp.zeros_like(pick)
    own.wait()
    for n in range(PHASES):
        for tz, ty in peers:
            o = tz * 4 + ty
            remote(p_hbm.at[mine, o, rows(n)], sel_v.at[mine, o, rows(n)], d_ssem.at[n, o], d_rsem.at[n, o],
                   device(x, core, tz, ty)).wait_recv()
        for kind, dev in ((0, x_to), (1, mate)):
            c = hand(n, kind, mine, dev)
            c.start()
            sends.append(c)
        if n + 2 < PHASES:
            fetch(n + 2)
        if n >= 1:
            hand_on(n - 1)
    hand_on(PHASES - 1)
    for n in range(PHASES):
        hand(n, 1, (x + 1 - core) % 4, mate).wait_recv()
        hand(n, 2, (x + 2 + core) % 4, mate).wait_recv()
    for b in range(NB):
        pltpu.make_async_copy(q_hbm.at[b], q_v.at[b], q_sem.at[b]).wait()

    def forward(b, carry):
        for t in range(LISTED):
            block = tiles_ref[group * NB + b, t]
            pq_v[b, pl.ds(t * SL, SL), :] = sel_v[block & 3, block >> 2]
        base = (group * NB + b) * 2 * BLK + owner * SL
        for c in range(BLK // CH):
            r = pl.ds(c * CH, CH)
            s = lax.dot_general(pq_v[b], q_v[b, r, :], (((1,), (1,)), ((), ())), preferred_element_type=F32)
            top = jnp.max(s, axis=0, keepdims=True)
            e = jnp.exp2(s * (SCALE * LOG2E) - top * (SCALE * LOG2E))
            e_v[b, :, r] = e.astype(BF16)
            now[0, pl.ds(b, 1), r] = top * SCALE
            now[0, pl.ds(NB + b, 1), r] = jnp.sum(e, axis=0, keepdims=True)
            at = lax.broadcasted_iota(jnp.int32, (SL, CH), 0) == pos_ref[pl.ds(b, 1), r] - base
            pick[0, pl.ds(b, 1), r] = jnp.sum(jnp.where(at, s[0:SL], 0.0), axis=0, keepdims=True) * SCALE
        return carry

    lax.fori_loop(0, NB, forward, 0)

    stats = Exchange(now, now_buf, ex_ssem.at[0], ex_rsem.at[0], [z_peers, y_peers])
    picks = Exchange(pick, pick_buf, ex_ssem.at[1], ex_rsem.at[1], [z_peers, y_peers])
    stats.start(0)
    picks.start(0)
    for stage in range(2):
        parts = stats.parts(stage)
        high = parts[0][0:4]
        for p in parts[1:]:
            high = jnp.maximum(high, p[0:4])
        total = sum(p[4:8] * jnp.exp(p[0:4] - high) for p in parts)
        now[stage + 1, 0:4] = high
        now[stage + 1, 4:8] = total
        if stage == 0:
            stats.start(1)

    def backward(b, carry):
        one = pl.ds(b, 1)
        weight = ct_ref[one, :] * SCALE
        factor = weight * jnp.exp(now[0, one, :] - now[2, one, :]) / now[2, pl.ds(NB + b, 1), :]
        base = (group * NB + b) * 2 * BLK + owner * SL
        at = lax.broadcasted_iota(jnp.int32, (SL, BLK), 0) == pos_ref[one, :] - base
        e_v[b, 0:SL, :] = (e_v[b, 0:SL, :].astype(F32) * factor - jnp.where(at, weight, 0.0)).astype(BF16)
        e_v[b, SL:, :] = (e_v[b, SL:, :].astype(F32) * factor).astype(BF16)
        part_v[b, 0:LISTED] = jnp.dot(e_v[b], q_v[b], preferred_element_type=F32).reshape(LISTED, SL, D)
        return carry

    lax.fori_loop(0, NB, backward, 0)
    picked = sum(picks.parts(0))
    pick[1] = picked
    picks.start(1)

    def dense(piece):
        def one(n, carry):
            blocks = []
            for o in range(2):
                for k in range(2):
                    p = (2 * n + o) * NB + 2 * piece + k
                    blocks.append(sum(part_v[b, slot_s[b, p]] for b in range(NB)))
            flat = jnp.concatenate(blocks, axis=0).astype(BF16).T
            dp_v[piece, :, :, :, :, pl.ds(pl.multiple_of(n * 256, 256), 256)] = flat.reshape(4, 2, 2, 48, 256)
            return carry

        lax.fori_loop(0, 8, one, 0)

    cores = {}

    def to_core(piece):
        for k, step in enumerate((2, 1, 3, 0)):
            c = remote(dp_v.at[piece, (x + step) % 4, 1 - core], core_buf.at[piece, k],
                       core_ssem.at[piece, k], core_rsem.at[piece, k], mate)
            c.start()
            cores[piece, k] = c

    def add_core(piece, k):
        place = (x + (2, 1, 3, 0)[k]) % 4
        cores[piece, k].wait_recv()
        for h in range(2):
            dp_v[piece, place, core, h] = (
                dp_v[piece, place, core, h].astype(F32) + core_buf[piece, k, h].astype(F32)).astype(BF16)

    for piece in range(PIECES):
        dense(piece)
        to_core(piece)

    for c in sends:
        c.wait_send()

    def product(b):
        for c in range(3):
            r = pl.ds(c * 256, 256)
            out = lax.dot_general(e_v[b], pq_v[b, :, r], (((0,), (0,)), ((), ())), preferred_element_type=F32)
            sel_v[b, :, :, r] = out.astype(BF16).reshape(16, SL, 256)

    z_next = [z_peers[0], z_peers[2]]
    y_next = [y_peers[0], y_peers[2]]
    left, right = pl.ds(0, 384), pl.ds(384, 384)
    a1 = Ring(z, lambda j, h: sel_v.at[j, pl.ds(8 * h, 8), :, left], z_next, a1_buf, a1_acc, r_ssem.at[0], r_rsem.at[0])
    b1 = Ring(y, lambda j, h: sel_v.at[pl.ds(2 * h, 2), pl.ds(4 * j, 4), :, right], y_next, b1_buf, b1_acc,
              r_ssem.at[1], r_rsem.at[1])
    a2 = Ring(y, lambda j, h: a1_sum.at[j, pl.ds(2 * h, 2)], y_next, a2_buf, a2_acc, r_ssem.at[2], r_rsem.at[2])
    b2 = Ring(z, lambda j, h: b1_sum.at[j, pl.ds(2 * h, 2)], z_next, b2_buf, b2_acc, r_ssem.at[3], r_rsem.at[3])
    xr = [Ring(x, lambda j, h, n=n: dp_v.at[n, j, core, h], x_next, x_buf.at[n], x_acc.at[n],
               r_ssem.at[4 + n], r_rsem.at[4 + n]) for n in range(PIECES)]
    returns = []

    def go_back(piece):
        for h in range(2):
            res = xr[piece].result(h).astype(BF16)
            for n in range(16):
                back[piece, n, pl.ds(48 * h, 48), :] = res[:, n * 128 : n * 128 + 128]
        for tz, ty in peers:
            o = tz * 4 + ty
            c = remote(back.at[piece, o], got.at[piece, me], back_ssem.at[piece, o], back_rsem.at[piece, me],
                       device(x, core, tz, ty))
            c.start()
            returns.append(c)

    product((z + 2) % 4)
    a1.ahead()
    add_core(0, 0)
    xr[0].ahead()
    add_core(0, 1)
    add_core(0, 2)
    xr[0].raw()
    product((z + 1) % 4)
    product((z + 3) % 4)
    a1.raw()
    add_core(0, 3)
    for k in range(4):
        add_core(1, k)
        if k == 0:
            xr[1].ahead()
        if k == 2:
            xr[1].raw()
    xr[0].forward()
    product(z)
    b1.ahead()
    b1.raw()
    a1.forward()
    xr[1].forward()
    b1.forward()
    go_back(0)
    for h in range(2):
        a1_sum[pl.ds(2 * h, 2)] = a1.result(h).astype(BF16).reshape(2, 4, SL, 384)
    a2.ahead()
    a2.raw()
    for h in range(2):
        b1_sum[pl.ds(2 * h, 2)] = b1.result(h).astype(BF16)
    b2.ahead()
    b2.raw()
    go_back(1)
    a2.forward()
    b2.forward()
    picked = sum(picks.parts(1))
    pick[2] = picked
    span = pl.ds(pl.multiple_of(y * 256, 256), 256)
    losses_ref[...] = now[2, pl.ds(z, 1), span] + jnp.log(now[2, pl.ds(4 + z, 1), span]) - pick[2, pl.ds(z, 1), span]

    def lay(piece, n, shard):
        out = shard.astype(F32).T.astype(BF16)
        for k in range(2):
            pg_ref[2 * piece + k, n] = out[k * SL : k * SL + SL, :]

    for piece in range(PIECES):
        lay(piece, me, back[piece, me])
    for piece in range(PIECES):
        for tz, ty in peers:
            n = tz * 4 + ty
            remote(back.at[piece, n], got.at[piece, n], back_ssem.at[piece, n], back_rsem.at[piece, n],
                   device(x, core, tz, ty)).wait_recv()
            lay(piece, n, got[piece, n])
    for h in range(2):
        qg_ref[pl.ds(128 * h, 128), left] = a2.result(h).astype(BF16).reshape(128, 384)
        qg_ref[pl.ds(128 * h, 128), right] = b2.result(h).astype(BF16).reshape(128, 384)
    for part in [stats, picks, a1, b1, a2, b2] + xr:
        part.drain()
    for c in list(cores.values()) + returns:
        c.wait_send()


SMEM = pl.BlockSpec(memory_space=pltpu.SMEM)
VMEM = pl.BlockSpec(memory_space=pltpu.VMEM)
ANY = pl.BlockSpec(memory_space=pl.ANY)


def whole(tiles, positives, cotangent, queries, passages):
    dma = pltpu.SemaphoreType.DMA
    return pl.pallas_call(
        whole_kernel,
        out_shape=[
            jax.ShapeDtypeStruct((1, 256), F32),
            jax.ShapeDtypeStruct((256, D), BF16),
            jax.ShapeDtypeStruct((NB, 16, SL, 96), BF16),
        ],
        in_specs=[SMEM, VMEM, VMEM, ANY, ANY],
        out_specs=[VMEM, VMEM, VMEM],
        scratch_shapes=[
            pltpu.VMEM((NB, BLK, D), BF16),
            pltpu.VMEM((NB, 16, SL, D), BF16),
            pltpu.VMEM((NB, LISTED * SL, D), BF16),
            pltpu.VMEM((NB, LISTED * SL, BLK), BF16),
            pltpu.VMEM((NB, LISTED + 1, SL, D), F32),
            pltpu.VMEM((PIECES, 4, 2, 2, 48, 2048), BF16),
            pltpu.SMEM((NB, 64), jnp.int32),
            pltpu.VMEM((3, 8, BLK), F32), pltpu.VMEM((2, 3, 8, BLK), F32),
            pltpu.VMEM((3, 8, BLK), F32), pltpu.VMEM((2, 3, 8, BLK), F32),
            pltpu.VMEM((2, 3, 8, SL, 384), BF16), pltpu.VMEM((2, 8, SL, 384), BF16),
            pltpu.VMEM((4, 4, SL, 384), BF16),
            pltpu.VMEM((2, 3, 2, 4, SL, 384), BF16), pltpu.VMEM((2, 2, 4, SL, 384), BF16),
            pltpu.VMEM((4, 4, SL, 384), BF16),
            pltpu.VMEM((2, 3, 2, SL, 384), BF16), pltpu.VMEM((2, 2, SL, 384), BF16),
            pltpu.VMEM((2, 3, 2, SL, 384), BF16), pltpu.VMEM((2, 2, SL, 384), BF16),
            pltpu.VMEM((PIECES, 2, 3, 48, 2048), BF16), pltpu.VMEM((PIECES, 2, 48, 2048), BF16),
            pltpu.VMEM((PIECES, 4, 2, 48, 2048), BF16),
            pltpu.VMEM((PIECES, 16, 96, 128), BF16), pltpu.VMEM((PIECES, 16, 96, 128), BF16),
            dma((NB,)), dma,
            dma((PHASES, 16)), dma((PHASES, 16)),
            dma((3, PHASES)), dma((3, PHASES)),
            dma((2, 2, 3)), dma((2, 2, 3)),
            dma((6, 2, 3)), dma((6, 2, 3)),
            dma((PIECES, 4)), dma((PIECES, 4)),
            dma((PIECES, 16)), dma((PIECES, 16)),
        ],
        compiler_params=pltpu.CompilerParams(
            collective_id=1, has_side_effects=True, vmem_limit_bytes=62 * 2**20),
        name="whole",
    )(tiles, positives, cotangent, queries, passages)


def per_device(queries, passages, tiles, positives, cotangent):
    losses, query_grads, passage_grads = whole(
        tiles, positives.reshape(NB, BLK), cotangent.reshape(NB, BLK),
        queries.reshape(NB, BLK, D), passages.reshape(NB, 16, SL, D))
    return losses.reshape(256), query_grads, passage_grads.reshape(NB * BLK, 96)


def solution(mesh):
    in_specs = (P("pb", None), P("pa", None), P(), P("pb"), P("pb"))
    out_specs = (P(("pb", "pa")), P(("pb", "pa"), None), P("pa", "pb"))
    return jax.shard_map(
        per_device, mesh=mesh, in_specs=in_specs, out_specs=out_specs, check_vma=False
    )
```

```python
import jax
import jax.numpy as jnp
from jax import lax
from jax.experimental import pallas as pl
from jax.experimental.pallas import tpu as pltpu
from jax.sharding import PartitionSpec as P

D = 768
BLK = 1024
NB = 4
LISTED = 8
SL = 64
PHASES = ((0, 16, 0, 384), (0, 16, 384, 384), (16, 16, 0, D), (32, 16, 0, D), (48, 16, 0, 384), (48, 16, 384, 384))
AT_ONCE = 3
PIECES = 2
SCALE = D ** (-0.5)
LOG2E = 1.4426950408889634
CH = 256
F32 = jnp.float32
BF16 = jnp.bfloat16


def around():
    group, owner = lax.axis_index("pb"), lax.axis_index("pa")
    return group // 2, group % 2, owner // 4, owner % 4


def device(x, core, z, y):
    return (x * 2 + core, z * 4 + y)


def greet(devices):
    barrier = pltpu.get_barrier_semaphore()
    for dev in devices:
        pl.semaphore_signal(barrier, inc=1, device_id=dev, device_id_type=pl.DeviceIdType.MESH)
    pl.semaphore_wait(barrier, len(devices))


def remote(src, dst, send_sem, recv_sem, dev):
    return pltpu.make_async_remote_copy(
        src_ref=src, dst_ref=dst, send_sem=send_sem, recv_sem=recv_sem,
        device_id=dev, device_id_type=pl.DeviceIdType.MESH)


AHEAD, RAW, SUMMED = 0, 1, 2


class Ring:
    def __init__(self, me, chunk, neighbours, buf, acc, send_sem, recv_sem):
        self.me, self.chunk, self.buf, self.acc = me, chunk, buf, acc
        self.send = lambda d, kind, src: remote(
            src, buf.at[d, kind], send_sem.at[d, kind], recv_sem.at[d, kind], neighbours[d])
        self.sent = {}

    def at(self, step, half):
        return self.chunk((self.me + step) % 4, half)

    def go(self, d, kind, src):
        c = self.send(d, kind, src)
        c.start()
        self.sent[d, kind] = c

    def ahead(self):
        self.go(0, AHEAD, self.at(2, 0))
        self.go(1, AHEAD, self.at(2, 1))

    def raw(self):
        self.go(0, RAW, self.at(1, 1))
        self.go(1, RAW, self.at(3, 0))

    def forward(self):
        for d, step in ((0, 1), (1, 3)):
            self.sent[d, AHEAD].wait_recv()
            self.acc[d] = (self.at(step, d)[...].astype(F32) + self.buf[d, AHEAD].astype(F32)).astype(BF16)
            self.go(d, SUMMED, self.acc.at[d])

    def result(self, half):
        a, b = (SUMMED, RAW) if half == 0 else (RAW, SUMMED)
        self.sent[0, a].wait_recv()
        self.sent[1, b].wait_recv()
        return self.at(0, half)[...].astype(F32) + self.buf[0, a].astype(F32) + self.buf[1, b].astype(F32)

    def drain(self):
        for c in self.sent.values():
            c.wait_send()


class Exchange:
    def __init__(self, now, buf, send_sem, recv_sem, peers):
        self.now, self.buf, self.peers = now, buf, peers
        self.sems = send_sem, recv_sem
        self.sent = {}

    def start(self, stage):
        for d in range(3):
            c = remote(self.now.at[stage], self.buf.at[stage, d], self.sems[0].at[stage, d], self.sems[1].at[stage, d],
                       self.peers[stage][d])
            c.start()
            self.sent[stage, d] = c

    def parts(self, stage):
        for d in range(3):
            self.sent[stage, d].wait_recv()
        return [self.now[stage]] + [self.buf[stage, d] for d in range(3)]

    def drain(self):
        for c in self.sent.values():
            c.wait_send()


def whole_kernel(tiles_ref, pos_ref, ct_ref, q_hbm, p_hbm, losses_ref, qg_ref, pg_ref,
                 q_v, sel_v, pq_v, e_v, part_v, dp_v, slot_s, pos_v, ct_v, now, now_buf,
                 a1_buf, a1_acc, a1_sum, b1_buf, b1_acc, b1_sum, a2_buf, a2_acc, b2_buf, b2_acc,
                 x_buf, x_acc, core_buf, back, got,
                 q_sem, own_sem, d_ssem, d_rsem, hand_ssem, hand_rsem, ex_ssem, ex_rsem,
                 r_ssem, r_rsem, core_ssem, core_rsem, back_ssem, back_rsem):
    group, owner = lax.axis_index("pb"), lax.axis_index("pa")
    x, core, z, y = around()
    me = z * 4 + y
    peers = [((z + dz) % 4, (y + dy) % 4) for dz in (2, 1, 3, 0) for dy in (2, 1, 3, 0) if dz or dy]
    z_peers = [device(x, core, (z + d) % 4, y) for d in (1, 2, 3)]
    y_peers = [device(x, core, z, (y + d) % 4) for d in (1, 2, 3)]
    x_next = [device((x + 1) % 4, core, z, y), device((x + 3) % 4, core, z, y)]
    mate = device(x, 1 - core, z, y)
    for b in range(NB):
        pltpu.make_async_copy(q_hbm.at[b], q_v.at[b], q_sem.at[b]).start()
    greet([device(x, core, tz, ty) for tz, ty in peers] + x_next + [mate])

    to = (x + 1 + 2 * core) % 4
    source = (x + 3 + 2 * core) % 4
    x_to, x_from = device(to, core, z, y), device(source, core, z, y)
    mine = (x + core) % 4
    theirs = (source + core) % 4

    def part(ref, n):
        row, rows, col, cols = PHASES[n]
        return ref.at[..., pl.ds(row, rows), pl.ds(col, cols)]

    own = pltpu.make_async_copy(p_hbm.at[mine, me], sel_v.at[mine, me], own_sem)
    own.start()
    sends = []

    def fetch(n):
        for tz, ty in peers:
            c = remote(part(p_hbm.at[mine, tz * 4 + ty], n), part(sel_v.at[mine, me], n),
                       d_ssem.at[n, tz * 4 + ty], d_rsem.at[n, me], device(x, core, tz, ty))
            c.start()
            sends.append(c)

    def hand(n, kind, b, dev):
        return remote(part(sel_v.at[b], n), part(sel_v.at[b], n), hand_ssem.at[kind, n], hand_rsem.at[kind, n], dev)

    def hand_on(n):
        hand(n, 0, theirs, x_from).wait_recv()
        c = hand(n, 2, theirs, mate)
        c.start()
        sends.append(c)

    for n in range(AT_ONCE):
        fetch(n)
    for b in range(NB):
        def find(p, carry, b=b):
            at = jnp.int32(LISTED)
            for t in range(LISTED):
                at = jnp.where(tiles_ref[t, group * NB + b] == p, t, at)
            slot_s[b, p] = at
            return carry

        lax.fori_loop(0, 64, find, 0)
        part_v[b, LISTED] = jnp.zeros((SL, D), BF16)
        for n in range(8):
            pos_v[b : b + 1, n * 128 : n * 128 + 128] = pos_ref[8 * b + n : 8 * b + n + 1, :]
            ct_v[b : b + 1, n * 128 : n * 128 + 128] = ct_ref[8 * b + n : 8 * b + n + 1, :]
    now[...] = jnp.zeros_like(now)
    own.wait()
    for n in range(len(PHASES)):
        for tz, ty in peers:
            o = tz * 4 + ty
            remote(part(p_hbm.at[mine, o], n), part(sel_v.at[mine, o], n), d_ssem.at[n, o], d_rsem.at[n, o],
                   device(x, core, tz, ty)).wait_recv()
        for kind, dev in ((0, x_to), (1, mate)):
            c = hand(n, kind, mine, dev)
            c.start()
            sends.append(c)
        if n + AT_ONCE < len(PHASES):
            fetch(n + AT_ONCE)
        if n >= 1:
            hand_on(n - 1)
    hand_on(len(PHASES) - 1)
    for n in range(len(PHASES)):
        hand(n, 1, (x + 1 - core) % 4, mate).wait_recv()
        hand(n, 2, (x + 2 + core) % 4, mate).wait_recv()
    for b in range(NB):
        pltpu.make_async_copy(q_hbm.at[b], q_v.at[b], q_sem.at[b]).wait()

    def forward(half, k):
        b = 2 * half + k
        for t in range(LISTED):
            block = tiles_ref[t, group * NB + b]
            pq_v[b, pl.ds(t * SL, SL), :] = sel_v[block & 3, block >> 2]
        base = (group * NB + b) * 2 * BLK + owner * SL
        for c in range(BLK // CH):
            r = pl.ds(c * CH, CH)
            s = lax.dot_general(pq_v[b], q_v[b, r, :], (((1,), (1,)), ((), ())), preferred_element_type=F32)
            top = jnp.max(s, axis=0, keepdims=True)
            e = jnp.exp2(s * (SCALE * LOG2E) - top * (SCALE * LOG2E))
            e_v[b, :, r] = e.astype(BF16)
            now[half, 0, pl.ds(k, 1), r] = top * SCALE
            now[half, 0, pl.ds(2 + k, 1), r] = jnp.sum(e, axis=0, keepdims=True)
            at = lax.broadcasted_iota(jnp.int32, (SL, CH), 0) == pos_v[pl.ds(b, 1), r] - base
            now[half, 0, pl.ds(4 + k, 1), r] = jnp.sum(jnp.where(at, s[0:SL], 0.0), axis=0, keepdims=True) * SCALE

    def run(body, steps):
        def one(n, carry):
            body(n)
            return carry

        lax.fori_loop(0, steps, one, 0)

    stats = [Exchange(now.at[h], now_buf.at[h], ex_ssem.at[h], ex_rsem.at[h], [z_peers, y_peers]) for h in range(2)]

    def combine(half, stage):
        parts = stats[half].parts(stage)
        high = parts[0][0:2]
        for p in parts[1:]:
            high = jnp.maximum(high, p[0:2])
        now[half, stage + 1, 0:2] = high
        now[half, stage + 1, 2:4] = sum(p[2:4] * jnp.exp(p[0:2] - high) for p in parts)
        now[half, stage + 1, 4:6] = sum(p[4:6] for p in parts)
        if stage == 0:
            stats[half].start(1)

    run(lambda k: forward(0, k), 2)
    stats[0].start(0)
    run(lambda k: forward(1, k), 2)
    stats[1].start(0)
    combine(0, 0)
    combine(1, 0)
    combine(0, 1)

    def grads(half, k):
        b = 2 * half + k
        weight = ct_v[pl.ds(b, 1), :] * SCALE
        factor = weight * jnp.exp(now[half, 0, pl.ds(k, 1), :] - now[half, 2, pl.ds(k, 1), :]) / now[half, 2, pl.ds(2 + k, 1), :]
        base = (group * NB + b) * 2 * BLK + owner * SL
        at = lax.broadcasted_iota(jnp.int32, (SL, BLK), 0) == pos_v[pl.ds(b, 1), :] - base
        e_v[b, 0:SL, :] = (e_v[b, 0:SL, :].astype(F32) * factor - jnp.where(at, weight, 0.0)).astype(BF16)
        e_v[b, SL:, :] = (e_v[b, SL:, :].astype(F32) * factor).astype(BF16)

    def passage_product(b):
        out = jnp.dot(e_v[b], q_v[b], preferred_element_type=F32)
        part_v[b, 0:LISTED] = out.astype(BF16).reshape(LISTED, SL, D)

    def query_product(b, quarter):
        r = pl.ds(pl.multiple_of(quarter * 256, 256), 256)
        out = lax.dot_general(e_v[b, :, r], pq_v[b], (((0,), (0,)), ((), ())), preferred_element_type=F32)
        sel_v[b, pl.ds(quarter * 4, 4)] = out.astype(BF16).reshape(4, SL, D)

    def dense(piece, n):
        blocks = []
        for o in range(2):
            for k in range(2):
                p = (2 * n + o) * NB + 2 * piece + k
                blocks.append((part_v[0, slot_s[0, p]] + part_v[1, slot_s[1, p]])
                              + (part_v[2, slot_s[2, p]] + part_v[3, slot_s[3, p]]))
        flat = jnp.concatenate(blocks, axis=0).T
        dp_v[piece, :, :, :, :, pl.ds(pl.multiple_of(n * 256, 256), 256)] = flat.reshape(4, 2, 2, 48, 256)

    cores = {}

    def to_core(piece):
        for k, step in enumerate((2, 1, 3, 0)):
            c = remote(dp_v.at[piece, (x + step) % 4, 1 - core], core_buf.at[piece, k],
                       core_ssem.at[piece, k], core_rsem.at[piece, k], mate)
            c.start()
            cores[piece, k] = c

    def add_core(piece, k):
        place = (x + (2, 1, 3, 0)[k]) % 4
        cores[piece, k].wait_recv()
        for h in range(2):
            dp_v[piece, place, core, h] = (
                dp_v[piece, place, core, h].astype(F32) + core_buf[piece, k, h].astype(F32)).astype(BF16)

    z_next = [z_peers[0], z_peers[2]]
    y_next = [y_peers[0], y_peers[2]]
    left, right = pl.ds(0, 384), pl.ds(384, 384)
    a1 = Ring(z, lambda j, h: sel_v.at[j, pl.ds(8 * h, 8), :, left], z_next, a1_buf, a1_acc, r_ssem.at[0], r_rsem.at[0])
    b1 = Ring(y, lambda j, h: sel_v.at[pl.ds(2 * h, 2), pl.ds(4 * j, 4), :, right], y_next, b1_buf, b1_acc,
              r_ssem.at[1], r_rsem.at[1])
    a2 = Ring(y, lambda j, h: a1_sum.at[j, pl.ds(2 * h, 2)], y_next, a2_buf, a2_acc, r_ssem.at[2], r_rsem.at[2])
    b2 = Ring(z, lambda j, h: b1_sum.at[j, pl.ds(2 * h, 2)], z_next, b2_buf, b2_acc, r_ssem.at[3], r_rsem.at[3])
    xr = [Ring(x, lambda j, h, n=n: dp_v.at[n, j, core, h], x_next, x_buf.at[n], x_acc.at[n],
               r_ssem.at[4 + n], r_rsem.at[4 + n]) for n in range(PIECES)]
    returns = []

    def go_back(piece):
        for h in range(2):
            res = xr[piece].result(h).astype(BF16)
            for n in range(16):
                back[piece, n, pl.ds(48 * h, 48), :] = res[:, n * 128 : n * 128 + 128]
        for tz, ty in peers:
            o = tz * 4 + ty
            c = remote(back.at[piece, o], got.at[piece, me], back_ssem.at[piece, o], back_rsem.at[piece, me],
                       device(x, core, tz, ty))
            c.start()
            returns.append(c)

    def both(k):
        grads(0, k)
        passage_product(k)

    run(both, 2)
    combine(1, 1)
    run(lambda k: grads(1, k), 2)
    for c in sends:
        c.wait_send()
    run(lambda n: query_product((z + 2) % 4, n), 4)
    run(lambda n: query_product((z + 3 + n) % 4, (y + 2) % 4), 3)
    a1.ahead()
    b1.ahead()
    run(lambda k: passage_product(2 + k), 2)

    def mixed(n):
        dense(0, n)
        query_product((z + 1 + 2 * (n // 3)) % 4 * (n < 6) + z * (n >= 6), (y + 3 + n % 3) % 4)

    run(mixed, 8)
    to_core(0)
    query_product(z, (y + 1) % 4)
    a1.raw()
    b1.raw()
    run(lambda n: dense(1, n), 8)
    to_core(1)
    add_core(0, 0)
    xr[0].ahead()
    add_core(0, 1)
    add_core(0, 2)
    xr[0].raw()
    add_core(0, 3)
    for k in range(4):
        add_core(1, k)
        if k == 0:
            xr[1].ahead()
        if k == 2:
            xr[1].raw()
    a1.forward()
    b1.forward()
    xr[0].forward()
    xr[1].forward()
    go_back(0)
    for h in range(2):
        a1_sum[pl.ds(2 * h, 2)] = a1.result(h).astype(BF16).reshape(2, 4, SL, 384)
    a2.ahead()
    a2.raw()
    for h in range(2):
        b1_sum[pl.ds(2 * h, 2)] = b1.result(h).astype(BF16)
    b2.ahead()
    b2.raw()
    go_back(1)
    a2.forward()
    b2.forward()
    span = pl.ds(pl.multiple_of(y * 256, 256), 256)

    def final(row):
        return now[z // 2, 2, pl.ds(2 * row + z % 2, 1), span]

    losses_ref[...] = final(0) + jnp.log(final(1)) - final(2)

    for piece in range(PIECES):
        got[piece, me] = back[piece, me]
        for tz, ty in peers:
            n = tz * 4 + ty
            remote(back.at[piece, n], got.at[piece, n], back_ssem.at[piece, n], back_rsem.at[piece, n],
                   device(x, core, tz, ty)).wait_recv()
        for n in range(8):
            one, two = got[piece, 2 * n], got[piece, 2 * n + 1]
            for k in range(2):
                h = slice(k * SL, k * SL + SL)
                first = (2 * piece + k) * BLK + n * 128
                pg_ref[:, first : first + 128] = jnp.concatenate([one[:, h], two[:, h]], axis=1)
    for h in range(2):
        qg_ref[pl.ds(128 * h, 128), left] = a2.result(h).astype(BF16).reshape(128, 384)
        qg_ref[pl.ds(128 * h, 128), right] = b2.result(h).astype(BF16).reshape(128, 384)
    for moved in stats + [a1, b1, a2, b2] + xr:
        moved.drain()
    for c in list(cores.values()) + returns:
        c.wait_send()


SMEM = pl.BlockSpec(memory_space=pltpu.SMEM)
VMEM = pl.BlockSpec(memory_space=pltpu.VMEM)
ANY = pl.BlockSpec(memory_space=pl.ANY)


def whole(tiles, positives, cotangent, queries, passages):
    dma = pltpu.SemaphoreType.DMA
    return pl.pallas_call(
        whole_kernel,
        out_shape=[
            jax.ShapeDtypeStruct((1, 256), F32),
            jax.ShapeDtypeStruct((256, D), BF16),
            jax.ShapeDtypeStruct((96, NB * BLK), BF16),
        ],
        in_specs=[SMEM, VMEM, VMEM, ANY, ANY],
        out_specs=[VMEM, VMEM, VMEM],
        scratch_shapes=[
            pltpu.VMEM((NB, BLK, D), BF16),
            pltpu.VMEM((NB, 16, SL, D), BF16),
            pltpu.VMEM((NB, LISTED * SL, D), BF16),
            pltpu.VMEM((NB, LISTED * SL, BLK), BF16),
            pltpu.VMEM((NB, LISTED + 1, SL, D), BF16),
            pltpu.VMEM((PIECES, 4, 2, 2, 48, 2048), BF16),
            pltpu.SMEM((NB, 64), jnp.int32),
            pltpu.VMEM((8, BLK), jnp.int32), pltpu.VMEM((8, BLK), F32),
            pltpu.VMEM((2, 3, 8, BLK), F32), pltpu.VMEM((2, 2, 3, 8, BLK), F32),
            pltpu.VMEM((2, 3, 8, SL, 384), BF16), pltpu.VMEM((2, 8, SL, 384), BF16),
            pltpu.VMEM((4, 4, SL, 384), BF16),
            pltpu.VMEM((2, 3, 2, 4, SL, 384), BF16), pltpu.VMEM((2, 2, 4, SL, 384), BF16),
            pltpu.VMEM((4, 4, SL, 384), BF16),
            pltpu.VMEM((2, 3, 2, SL, 384), BF16), pltpu.VMEM((2, 2, SL, 384), BF16),
            pltpu.VMEM((2, 3, 2, SL, 384), BF16), pltpu.VMEM((2, 2, SL, 384), BF16),
            pltpu.VMEM((PIECES, 2, 3, 48, 2048), BF16), pltpu.VMEM((PIECES, 2, 48, 2048), BF16),
            pltpu.VMEM((PIECES, 4, 2, 48, 2048), BF16),
            pltpu.VMEM((PIECES, 16, 96, 128), BF16), pltpu.VMEM((PIECES, 16, 96, 128), BF16),
            dma((NB,)), dma,
            dma((len(PHASES), 16)), dma((len(PHASES), 16)),
            dma((3, len(PHASES))), dma((3, len(PHASES))),
            dma((2, 2, 3)), dma((2, 2, 3)),
            dma((6, 2, 3)), dma((6, 2, 3)),
            dma((PIECES, 4)), dma((PIECES, 4)),
            dma((PIECES, 16)), dma((PIECES, 16)),
        ],
        compiler_params=pltpu.CompilerParams(
            collective_id=1, has_side_effects=True, vmem_limit_bytes=62 * 2**20),
        name="whole",
    )(tiles, positives, cotangent, queries, passages)


def per_device(queries, passages, tiles, positives, cotangent):
    losses, query_grads, passage_grads = whole(
        tiles.T, positives.reshape(32, 128), cotangent.reshape(32, 128),
        queries.reshape(NB, BLK, D), passages.reshape(NB, 16, SL, D))
    return losses.reshape(256), query_grads, passage_grads.T


def solution(mesh):
    in_specs = (P("pb", None), P("pa", None), P(), P("pb"), P("pb"))
    out_specs = (P(("pb", "pa")), P(("pb", "pa"), None), P("pa", "pb"))
    return jax.shard_map(
        per_device, mesh=mesh, in_specs=in_specs, out_specs=out_specs, check_vma=False
    )
```

```python
import jax
import jax.numpy as jnp
from jax import lax
from jax.experimental import pallas as pl
from jax.experimental.pallas import tpu as pltpu
from jax.sharding import PartitionSpec as P

D = 768
BLK = 1024
NB = 4
LISTED = 8
SL = 64
PHASES = tuple((0, SL, c, 128) for c in range(0, D, 128))
AT_ONCE = 3
PIECES = 2
SCALE = D ** (-0.5)
LOG2E = 1.4426950408889634
CH = 256
F32 = jnp.float32
BF16 = jnp.bfloat16


def around():
    group, owner = lax.axis_index("pb"), lax.axis_index("pa")
    return group // 2, group % 2, owner // 4, owner % 4


def device(x, core, z, y):
    return (x * 2 + core, z * 4 + y)


def greet(devices):
    barrier = pltpu.get_barrier_semaphore()
    for dev in devices:
        pl.semaphore_signal(barrier, inc=1, device_id=dev, device_id_type=pl.DeviceIdType.MESH)
    pl.semaphore_wait(barrier, len(devices))


def remote(src, dst, send_sem, recv_sem, dev):
    return pltpu.make_async_remote_copy(
        src_ref=src, dst_ref=dst, send_sem=send_sem, recv_sem=recv_sem,
        device_id=dev, device_id_type=pl.DeviceIdType.MESH)


AHEAD, RAW, SUMMED = 0, 1, 2


class Ring:
    def __init__(self, me, chunk, neighbours, buf, acc, send_sem, recv_sem):
        self.me, self.chunk, self.buf, self.acc = me, chunk, buf, acc
        self.send = lambda d, kind, src: remote(
            src, buf.at[d, kind], send_sem.at[d, kind], recv_sem.at[d, kind], neighbours[d])
        self.sent = {}

    def at(self, step, half):
        return self.chunk((self.me + step) % 4, half)

    def go(self, d, kind, src):
        c = self.send(d, kind, src)
        c.start()
        self.sent[d, kind] = c

    def ahead(self):
        self.go(0, AHEAD, self.at(2, 0))
        self.go(1, AHEAD, self.at(2, 1))

    def raw(self):
        self.go(0, RAW, self.at(1, 1))
        self.go(1, RAW, self.at(3, 0))

    def forward(self):
        for d, step in ((0, 1), (1, 3)):
            self.sent[d, AHEAD].wait_recv()
            self.acc[d] = (self.at(step, d)[...].astype(F32) + self.buf[d, AHEAD].astype(F32)).astype(BF16)
            self.go(d, SUMMED, self.acc.at[d])

    def result(self, half):
        a, b = (SUMMED, RAW) if half == 0 else (RAW, SUMMED)
        self.sent[0, a].wait_recv()
        self.sent[1, b].wait_recv()
        return self.at(0, half)[...].astype(F32) + self.buf[0, a].astype(F32) + self.buf[1, b].astype(F32)

    def drain(self):
        for c in self.sent.values():
            c.wait_send()


class Exchange:
    def __init__(self, now, buf, send_sem, recv_sem, peers):
        self.now, self.buf, self.peers = now, buf, peers
        self.sems = send_sem, recv_sem
        self.sent = {}

    def start(self, stage):
        for d in range(3):
            c = remote(self.now.at[stage], self.buf.at[stage, d], self.sems[0].at[stage, d], self.sems[1].at[stage, d],
                       self.peers[stage][d])
            c.start()
            self.sent[stage, d] = c

    def parts(self, stage):
        for d in range(3):
            self.sent[stage, d].wait_recv()
        return [self.now[stage]] + [self.buf[stage, d] for d in range(3)]

    def drain(self):
        for c in self.sent.values():
            c.wait_send()


def whole_kernel(tiles_ref, pos_ref, ct_ref, q_hbm, p_hbm, losses_ref, qg_ref, got,
                 q_v, sel_v, pq_v, e_v, part_v, dp_v, slot_s, pos_v, ct_v, now, now_buf, pick, pick_buf,
                 a1_buf, a1_acc, a1_sum, b1_buf, b1_acc, b1_sum, a2_buf, a2_acc, b2_buf, b2_acc,
                 x_buf, x_acc, core_buf, back,
                 q_sem, own_sem, d_ssem, d_rsem, hand_ssem, hand_rsem, ex_ssem, ex_rsem,
                 r_ssem, r_rsem, core_ssem, core_rsem, back_ssem, back_rsem, keep_sem):
    group, owner = lax.axis_index("pb"), lax.axis_index("pa")
    x, core, z, y = around()
    me = z * 4 + y
    peers = [((z + dz) % 4, (y + dy) % 4) for dz in (2, 1, 3, 0) for dy in (2, 1, 3, 0) if dz or dy]
    z_peers = [device(x, core, (z + d) % 4, y) for d in (1, 2, 3)]
    y_peers = [device(x, core, z, (y + d) % 4) for d in (1, 2, 3)]
    x_next = [device((x + 1) % 4, core, z, y), device((x + 3) % 4, core, z, y)]
    mate = device(x, 1 - core, z, y)
    for b in range(NB):
        pltpu.make_async_copy(q_hbm.at[b], q_v.at[b], q_sem.at[b]).start()
    greet([device(x, core, tz, ty) for tz, ty in peers] + x_next + [mate])

    to = (x + 1 + 2 * core) % 4
    source = (x + 3 + 2 * core) % 4
    x_to, x_from = device(to, core, z, y), device(source, core, z, y)
    mine = (x + core) % 4
    theirs = (source + core) % 4

    def part(ref, n):
        row, rows, col, cols = PHASES[n]
        return ref.at[..., pl.ds(row, rows), pl.ds(col, cols)]

    own = pltpu.make_async_copy(p_hbm.at[mine, me], sel_v.at[mine, me], own_sem)
    own.start()
    sends = []

    def fetch(n):
        for tz, ty in peers:
            c = remote(part(p_hbm.at[mine, tz * 4 + ty], n), part(sel_v.at[mine, me], n),
                       d_ssem.at[n, tz * 4 + ty], d_rsem.at[n, me], device(x, core, tz, ty))
            c.start()
            sends.append(c)

    def hand(n, kind, b, dev):
        return remote(part(sel_v.at[b], n), part(sel_v.at[b], n), hand_ssem.at[kind, n], hand_rsem.at[kind, n], dev)

    def hand_on(n):
        hand(n, 0, theirs, x_from).wait_recv()
        c = hand(n, 2, theirs, mate)
        c.start()
        sends.append(c)

    for n in range(AT_ONCE):
        fetch(n)
    for b in range(NB):
        def find(p, carry, b=b):
            at = jnp.int32(LISTED)
            for t in range(LISTED):
                at = jnp.where(tiles_ref[t, group * NB + b] == p, t, at)
            slot_s[b, p] = at
            return carry

        lax.fori_loop(0, 64, find, 0)
        part_v[b, LISTED] = jnp.zeros((SL, D), BF16)
        for n in range(8):
            pos_v[b : b + 1, n * 128 : n * 128 + 128] = pos_ref[8 * b + n : 8 * b + n + 1, :]
            ct_v[b : b + 1, n * 128 : n * 128 + 128] = ct_ref[8 * b + n : 8 * b + n + 1, :]
    own.wait()
    for n in range(len(PHASES)):
        for tz, ty in peers:
            o = tz * 4 + ty
            remote(part(p_hbm.at[mine, o], n), part(sel_v.at[mine, o], n), d_ssem.at[n, o], d_rsem.at[n, o],
                   device(x, core, tz, ty)).wait_recv()
        for kind, dev in ((0, x_to), (1, mate)):
            c = hand(n, kind, mine, dev)
            c.start()
            sends.append(c)
        if n + AT_ONCE < len(PHASES):
            fetch(n + AT_ONCE)
        if n >= 1:
            hand_on(n - 1)
    hand_on(len(PHASES) - 1)
    for n in range(len(PHASES)):
        hand(n, 1, (x + 1 - core) % 4, mate).wait_recv()
        hand(n, 2, (x + 2 + core) % 4, mate).wait_recv()
    for b in range(NB):
        pltpu.make_async_copy(q_hbm.at[b], q_v.at[b], q_sem.at[b]).wait()

    def forward(half, k):
        b = 2 * half + k
        for t in range(LISTED):
            block = tiles_ref[t, group * NB + b]
            pq_v[b, pl.ds(t * SL, SL), :] = sel_v[block & 3, block >> 2]
        base = (group * NB + b) * 2 * BLK + owner * SL
        for c in range(BLK // CH):
            r = pl.ds(c * CH, CH)
            s = lax.dot_general(pq_v[b], q_v[b, r, :], (((1,), (1,)), ((), ())), preferred_element_type=F32)
            top = jnp.max(s, axis=0, keepdims=True)
            e = jnp.exp2(s * (SCALE * LOG2E) - top * (SCALE * LOG2E))
            e_v[b, :, r] = e.astype(BF16)
            now[half, 0, pl.ds(k, 1), r] = top * SCALE
            now[half, 0, pl.ds(2 + k, 1), r] = jnp.sum(e, axis=0, keepdims=True)
            at = lax.broadcasted_iota(jnp.int32, (SL, CH), 0) == pos_v[pl.ds(b, 1), r] - base
            pick[0, pl.ds(b, 1), r] = jnp.sum(jnp.where(at, s[0:SL], 0.0), axis=0, keepdims=True) * SCALE

    def run(body, steps):
        def one(n, carry):
            body(n)
            return carry

        lax.fori_loop(0, steps, one, 0)

    turns = [z_peers, y_peers], [y_peers, z_peers]
    stats = [Exchange(now.at[h], now_buf.at[h], ex_ssem.at[h], ex_rsem.at[h], turns[h]) for h in range(2)]
    picks = Exchange(pick, pick_buf, ex_ssem.at[2], ex_rsem.at[2], turns[0])

    def combine(half, stage):
        parts = stats[half].parts(stage)
        high = parts[0][0:2]
        for p in parts[1:]:
            high = jnp.maximum(high, p[0:2])
        now[half, stage + 1, 0:2] = high
        now[half, stage + 1, 2:4] = sum(p[2:4] * jnp.exp(p[0:2] - high) for p in parts)
        if stage == 0:
            stats[half].start(1)

    run(lambda k: forward(0, k), 2)
    stats[0].start(0)
    run(lambda k: forward(1, k), 2)
    stats[1].start(0)
    combine(0, 0)
    combine(1, 0)
    combine(0, 1)

    def grads(half, k):
        b = 2 * half + k
        weight = ct_v[pl.ds(b, 1), :] * SCALE
        factor = weight * jnp.exp(now[half, 0, pl.ds(k, 1), :] - now[half, 2, pl.ds(k, 1), :]) / now[half, 2, pl.ds(2 + k, 1), :]
        base = (group * NB + b) * 2 * BLK + owner * SL
        at = lax.broadcasted_iota(jnp.int32, (SL, BLK), 0) == pos_v[pl.ds(b, 1), :] - base
        e_v[b, 0:SL, :] = (e_v[b, 0:SL, :].astype(F32) * factor - jnp.where(at, weight, 0.0)).astype(BF16)
        e_v[b, SL:, :] = (e_v[b, SL:, :].astype(F32) * factor).astype(BF16)

    def passage_product(b):
        out = jnp.dot(e_v[b], q_v[b], preferred_element_type=F32)
        part_v[b, 0:LISTED] = out.astype(BF16).reshape(LISTED, SL, D)

    def query_product(b, quarter):
        r = pl.ds(pl.multiple_of(quarter * 256, 256), 256)
        out = lax.dot_general(e_v[b, :, r], pq_v[b], (((0,), (0,)), ((), ())), preferred_element_type=F32)
        sel_v[b, pl.ds(quarter * 4, 4)] = out.astype(BF16).reshape(4, SL, D)

    def dense(piece, n):
        blocks = []
        for o in range(2):
            for k in range(2):
                p = (2 * n + o) * NB + 2 * piece + k
                blocks.append((part_v[0, slot_s[0, p]] + part_v[1, slot_s[1, p]])
                              + (part_v[2, slot_s[2, p]] + part_v[3, slot_s[3, p]]))
        flat = jnp.concatenate(blocks, axis=0).T
        dp_v[piece, :, :, :, :, pl.ds(pl.multiple_of(n * 256, 256), 256)] = flat.reshape(4, 2, 2, 48, 256)

    cores = {}

    def to_core(piece):
        for k, step in enumerate((2, 1, 3, 0)):
            c = remote(dp_v.at[piece, (x + step) % 4, 1 - core], core_buf.at[piece, k],
                       core_ssem.at[piece, k], core_rsem.at[piece, k], mate)
            c.start()
            cores[piece, k] = c

    def add_core(piece, k):
        place = (x + (2, 1, 3, 0)[k]) % 4
        cores[piece, k].wait_recv()
        for h in range(2):
            dp_v[piece, place, core, h] = (
                dp_v[piece, place, core, h].astype(F32) + core_buf[piece, k, h].astype(F32)).astype(BF16)

    z_next = [z_peers[0], z_peers[2]]
    y_next = [y_peers[0], y_peers[2]]
    left, right = pl.ds(0, 384), pl.ds(384, 384)
    a1 = Ring(z, lambda j, h: sel_v.at[j, pl.ds(8 * h, 8), :, left], z_next, a1_buf, a1_acc, r_ssem.at[0], r_rsem.at[0])
    b1 = Ring(y, lambda j, h: sel_v.at[pl.ds(2 * h, 2), pl.ds(4 * j, 4), :, right], y_next, b1_buf, b1_acc,
              r_ssem.at[1], r_rsem.at[1])
    a2 = Ring(y, lambda j, h: a1_sum.at[j, pl.ds(2 * h, 2)], y_next, a2_buf, a2_acc, r_ssem.at[2], r_rsem.at[2])
    b2 = Ring(z, lambda j, h: b1_sum.at[j, pl.ds(2 * h, 2)], z_next, b2_buf, b2_acc, r_ssem.at[3], r_rsem.at[3])
    xr = [Ring(x, lambda j, h, n=n: dp_v.at[n, j, core, h], x_next, x_buf.at[n], x_acc.at[n],
               r_ssem.at[4 + n], r_rsem.at[4 + n]) for n in range(PIECES)]
    returns, keeps = [], []

    def go_back(piece):
        for h in range(2):
            res = xr[piece].result(h).astype(BF16)
            for n in range(16):
                back[piece, n, pl.ds(48 * h, 48), :] = res[:, n * 128 : n * 128 + 128]
        for tz, ty in peers:
            o = tz * 4 + ty
            c = remote(back.at[piece, o], got.at[piece, me], back_ssem.at[piece, o], back_rsem.at[piece, me],
                       device(x, core, tz, ty))
            c.start()
            returns.append(c)
        c = pltpu.make_async_copy(back.at[piece, me], got.at[piece, me], keep_sem.at[piece])
        c.start()
        keeps.append(c)

    def both(k):
        grads(0, k)
        passage_product(k)

    run(both, 2)
    combine(1, 1)
    picks.start(0)
    run(lambda k: grads(1, k), 2)
    for c in sends:
        c.wait_send()
    run(lambda n: query_product((z + 2) % 4, n), 4)
    run(lambda n: query_product((z + 3 + n) % 4, (y + 2) % 4), 3)
    a1.ahead()
    b1.ahead()
    run(lambda k: passage_product(2 + k), 2)
    run(lambda n: dense(0, n), 8)
    to_core(0)
    run(lambda n: query_product((z + 1 + 2 * (n // 3)) % 4, (y + 3 + n % 3) % 4), 6)
    a1.raw()
    add_core(0, 0)
    xr[0].ahead()
    add_core(0, 1)
    add_core(0, 2)
    xr[0].raw()
    run(lambda n: query_product(z, (y + 3 + n) % 4), 3)
    b1.raw()
    run(lambda n: dense(1, n), 8)
    to_core(1)
    add_core(0, 3)
    pick[1] = sum(picks.parts(0))
    picks.start(1)
    a1.forward()
    b1.forward()
    add_core(1, 0)
    xr[1].ahead()
    xr[0].forward()
    add_core(1, 1)
    add_core(1, 2)
    xr[1].raw()
    add_core(1, 3)
    xr[1].forward()
    for h in range(2):
        a1_sum[pl.ds(2 * h, 2)] = a1.result(h).astype(BF16).reshape(2, 4, SL, 384)
    a2.ahead()
    a2.raw()
    go_back(0)
    for h in range(2):
        b1_sum[pl.ds(2 * h, 2)] = b1.result(h).astype(BF16)
    b2.ahead()
    b2.raw()
    a2.forward()
    b2.forward()
    go_back(1)
    span = pl.ds(pl.multiple_of(y * 256, 256), 256)
    pick[2] = sum(picks.parts(1))

    def final(row):
        return now[z // 2, 2, pl.ds(2 * row + z % 2, 1), span]

    losses_ref[...] = final(0) + jnp.log(final(1)) - pick[2, pl.ds(z, 1), span]
    for h in range(2):
        qg_ref[pl.ds(128 * h, 128), left] = a2.result(h).astype(BF16).reshape(128, 384)
        qg_ref[pl.ds(128 * h, 128), right] = b2.result(h).astype(BF16).reshape(128, 384)
    for piece in range(PIECES):
        for tz, ty in peers:
            n = tz * 4 + ty
            remote(back.at[piece, n], got.at[piece, n], back_ssem.at[piece, n], back_rsem.at[piece, n],
                   device(x, core, tz, ty)).wait_recv()
    for moved in stats + [picks, a1, b1, a2, b2] + xr:
        moved.drain()
    for c in list(cores.values()) + returns:
        c.wait_send()
    for c in keeps:
        c.wait()


def lay_kernel(losses_in, qg_in, got, losses_ref, qg_ref, pg_ref):
    losses_ref[...] = losses_in[...]
    qg_ref[...] = qg_in[...]
    for piece in range(PIECES):
        for n in range(8):
            one, two = got[piece, 2 * n], got[piece, 2 * n + 1]
            for k in range(2):
                h = slice(k * SL, k * SL + SL)
                first = (2 * piece + k) * BLK + n * 128
                pg_ref[:, first : first + 128] = jnp.concatenate([one[:, h], two[:, h]], axis=1)


SMEM = pl.BlockSpec(memory_space=pltpu.SMEM)
VMEM = pl.BlockSpec(memory_space=pltpu.VMEM)
ANY = pl.BlockSpec(memory_space=pl.ANY)


def whole(tiles, positives, cotangent, queries, passages):
    dma = pltpu.SemaphoreType.DMA
    return pl.pallas_call(
        whole_kernel,
        out_shape=[
            jax.ShapeDtypeStruct((1, 256), F32),
            jax.ShapeDtypeStruct((256, D), BF16),
            jax.ShapeDtypeStruct((PIECES, 16, 96, 128), BF16),
        ],
        in_specs=[SMEM, VMEM, VMEM, ANY, ANY],
        out_specs=[VMEM, VMEM, ANY],
        scratch_shapes=[
            pltpu.VMEM((NB, BLK, D), BF16),
            pltpu.VMEM((NB, 16, SL, D), BF16),
            pltpu.VMEM((NB, LISTED * SL, D), BF16),
            pltpu.VMEM((NB, LISTED * SL, BLK), BF16),
            pltpu.VMEM((NB, LISTED + 1, SL, D), BF16),
            pltpu.VMEM((PIECES, 4, 2, 2, 48, 2048), BF16),
            pltpu.SMEM((NB, 64), jnp.int32),
            pltpu.VMEM((8, BLK), jnp.int32), pltpu.VMEM((8, BLK), F32),
            pltpu.VMEM((2, 3, 4, BLK), F32), pltpu.VMEM((2, 2, 3, 4, BLK), F32),
            pltpu.VMEM((3, 4, BLK), F32), pltpu.VMEM((2, 3, 4, BLK), F32),
            pltpu.VMEM((2, 3, 8, SL, 384), BF16), pltpu.VMEM((2, 8, SL, 384), BF16),
            pltpu.VMEM((4, 4, SL, 384), BF16),
            pltpu.VMEM((2, 3, 2, 4, SL, 384), BF16), pltpu.VMEM((2, 2, 4, SL, 384), BF16),
            pltpu.VMEM((4, 4, SL, 384), BF16),
            pltpu.VMEM((2, 3, 2, SL, 384), BF16), pltpu.VMEM((2, 2, SL, 384), BF16),
            pltpu.VMEM((2, 3, 2, SL, 384), BF16), pltpu.VMEM((2, 2, SL, 384), BF16),
            pltpu.VMEM((PIECES, 2, 3, 48, 2048), BF16), pltpu.VMEM((PIECES, 2, 48, 2048), BF16),
            pltpu.VMEM((PIECES, 4, 2, 48, 2048), BF16),
            pltpu.VMEM((PIECES, 16, 96, 128), BF16),
            dma((NB,)), dma,
            dma((len(PHASES), 16)), dma((len(PHASES), 16)),
            dma((3, len(PHASES))), dma((3, len(PHASES))),
            dma((3, 2, 3)), dma((3, 2, 3)),
            dma((6, 2, 3)), dma((6, 2, 3)),
            dma((PIECES, 4)), dma((PIECES, 4)),
            dma((PIECES, 16)), dma((PIECES, 16)), dma((PIECES,)),
        ],
        compiler_params=pltpu.CompilerParams(
            collective_id=1, has_side_effects=True, vmem_limit_bytes=62 * 2**20),
        name="whole",
    )(tiles, positives, cotangent, queries, passages)


def lay(losses, query_grads, got):
    return pl.pallas_call(
        lay_kernel,
        out_shape=[
            jax.ShapeDtypeStruct((1, 256), F32),
            jax.ShapeDtypeStruct((256, D), BF16),
            jax.ShapeDtypeStruct((96, NB * BLK), BF16),
        ],
        in_specs=[VMEM, VMEM, VMEM],
        out_specs=[VMEM, VMEM, VMEM],
        name="lay",
    )(losses, query_grads, got)


def per_device(queries, passages, tiles, positives, cotangent):
    losses, query_grads, passage_grads = lay(*whole(
        tiles.T, positives.reshape(32, 128), cotangent.reshape(32, 128),
        queries.reshape(NB, BLK, D), passages.reshape(NB, 16, SL, D)))
    return losses.reshape(256), query_grads, passage_grads.T


def solution(mesh):
    in_specs = (P("pb", None), P("pa", None), P(), P("pb"), P("pb"))
    out_specs = (P(("pb", "pa")), P(("pb", "pa"), None), P("pa", "pb"))
    return jax.shard_map(
        per_device, mesh=mesh, in_specs=in_specs, out_specs=out_specs, check_vma=False
    )
```

```python
import jax
import jax.numpy as jnp
from jax import lax
from jax.experimental import pallas as pl
from jax.experimental.pallas import tpu as pltpu
from jax.sharding import PartitionSpec as P

D = 768
BLK = 1024
NB = 4
LISTED = 8
SL = 64
PHASES = tuple((c, False, True) for c in range(0, 640, 128)) + ((640, False, False), (640, True, False))
AT_ONCE = 3
PIECES = 2
SCALE = D ** (-0.5)
LOG2E = 1.4426950408889634
CH = 256
F32 = jnp.float32
BF16 = jnp.bfloat16


def around():
    group, owner = lax.axis_index("pb"), lax.axis_index("pa")
    return group // 2, group % 2, owner // 4, owner % 4


def device(x, core, z, y):
    return (x * 2 + core, z * 4 + y)


def greet(devices):
    barrier = pltpu.get_barrier_semaphore()
    for dev in devices:
        pl.semaphore_signal(barrier, inc=1, device_id=dev, device_id_type=pl.DeviceIdType.MESH)
    pl.semaphore_wait(barrier, len(devices))


def remote(src, dst, send_sem, recv_sem, dev):
    return pltpu.make_async_remote_copy(
        src_ref=src, dst_ref=dst, send_sem=send_sem, recv_sem=recv_sem,
        device_id=dev, device_id_type=pl.DeviceIdType.MESH)


AHEAD, RAW, SUMMED = 0, 1, 2


class Ring:
    def __init__(self, me, chunk, neighbours, buf, acc, send_sem, recv_sem):
        self.me, self.chunk, self.buf, self.acc = me, chunk, buf, acc
        self.send = lambda d, kind, src: remote(
            src, buf.at[d, kind], send_sem.at[d, kind], recv_sem.at[d, kind], neighbours[d])
        self.sent = {}

    def at(self, step, half):
        return self.chunk((self.me + step) % 4, half)

    def go(self, d, kind, src):
        c = self.send(d, kind, src)
        c.start()
        self.sent[d, kind] = c

    def ahead(self):
        self.go(0, AHEAD, self.at(2, 0))
        self.go(1, AHEAD, self.at(2, 1))

    def raw(self):
        self.go(0, RAW, self.at(1, 1))
        self.go(1, RAW, self.at(3, 0))

    def forward(self):
        for d, step in ((0, 1), (1, 3)):
            self.sent[d, AHEAD].wait_recv()
            self.acc[d] = (self.at(step, d)[...].astype(F32) + self.buf[d, AHEAD].astype(F32)).astype(BF16)
            self.go(d, SUMMED, self.acc.at[d])

    def result(self, half):
        a, b = (SUMMED, RAW) if half == 0 else (RAW, SUMMED)
        self.sent[0, a].wait_recv()
        self.sent[1, b].wait_recv()
        return self.at(0, half)[...].astype(F32) + self.buf[0, a].astype(F32) + self.buf[1, b].astype(F32)

    def drain(self):
        for c in self.sent.values():
            c.wait_send()


class Exchange:
    def __init__(self, now, buf, send_sem, recv_sem, peers):
        self.now, self.buf, self.peers = now, buf, peers
        self.sems = send_sem, recv_sem
        self.sent = {}

    def start(self, stage):
        for d in range(3):
            c = remote(self.now.at[stage], self.buf.at[stage, d], self.sems[0].at[stage, d], self.sems[1].at[stage, d],
                       self.peers[stage][d])
            c.start()
            self.sent[stage, d] = c

    def parts(self, stage):
        for d in range(3):
            self.sent[stage, d].wait_recv()
        return [self.now[stage]] + [self.buf[stage, d] for d in range(3)]

    def drain(self):
        for c in self.sent.values():
            c.wait_send()


def whole_kernel(tiles_ref, pos_ref, ct_ref, q_hbm, p_hbm, losses_ref, qg_ref, got,
                 q_v, sel_v, pq_v, e_v, part_v, dp_v, slot_s, pos_v, ct_v, now, now_buf, pick, pick_buf,
                 a1_buf, a1_acc, a1_sum, b1_buf, b1_acc, b1_sum, a2_buf, a2_acc, b2_buf, b2_acc,
                 x_buf, x_acc, core_buf, back,
                 q_sem, own_sem, d_ssem, d_rsem, hand_ssem, hand_rsem, ex_ssem, ex_rsem, tell_ssem, tell_rsem,
                 r_ssem, r_rsem, core_ssem, core_rsem, back_ssem, back_rsem, keep_sem):
    group, owner = lax.axis_index("pb"), lax.axis_index("pa")
    x, core, z, y = around()
    me = z * 4 + y
    peers = [((z + dz) % 4, (y + dy) % 4) for dz in (2, 1, 3, 0) for dy in (2, 1, 3, 0) if dz or dy]
    z_peers = [device(x, core, (z + d) % 4, y) for d in (1, 2, 3)]
    y_peers = [device(x, core, z, (y + d) % 4) for d in (1, 2, 3)]
    x_next = [device((x + 1) % 4, core, z, y), device((x + 3) % 4, core, z, y)]
    mate = device(x, 1 - core, z, y)
    for b in range(NB):
        pltpu.make_async_copy(q_hbm.at[b], q_v.at[b], q_sem.at[b]).start()
    greet([device(x, core, tz, ty) for tz, ty in peers] + x_next + [mate])

    to = (x + 1 + 2 * core) % 4
    source = (x + 3 + 2 * core) % 4
    x_to, x_from = device(to, core, z, y), device(source, core, z, y)
    mine = (x + core) % 4
    theirs = (source + core) % 4

    def part(ref, n):
        return ref.at[..., pl.ds(PHASES[n][0], 128)]

    def which(n):
        return theirs if PHASES[n][1] else mine

    owns = [pltpu.make_async_copy(p_hbm.at[mine, me], sel_v.at[mine, me], own_sem.at[0]),
            pltpu.make_async_copy(part(p_hbm.at[theirs, me], -1), part(sel_v.at[theirs, me], -1), own_sem.at[1])]
    for c in owns:
        c.start()
    sends = []

    def fetch(n):
        for tz, ty in peers:
            c = remote(part(p_hbm.at[which(n), tz * 4 + ty], n), part(sel_v.at[which(n), me], n),
                       d_ssem.at[n, tz * 4 + ty], d_rsem.at[n, me], device(x, core, tz, ty))
            c.start()
            sends.append(c)

    def hand(n, kind, b, dev):
        return remote(part(sel_v.at[b], n), part(sel_v.at[b], n), hand_ssem.at[kind, n], hand_rsem.at[kind, n], dev)

    def hand_on(n):
        hand(n, 0, theirs, x_from).wait_recv()
        c = hand(n, 2, theirs, mate)
        c.start()
        sends.append(c)

    for n in range(AT_ONCE):
        fetch(n)
    for b in range(NB):
        def find(p, carry, b=b):
            at = jnp.int32(LISTED)
            for t in range(LISTED):
                at = jnp.where(tiles_ref[t, group * NB + b] == p, t, at)
            slot_s[b, p] = at
            return carry

        lax.fori_loop(0, 64, find, 0)
        part_v[b, LISTED] = jnp.zeros((SL, D), BF16)
        for n in range(8):
            pos_v[b : b + 1, n * 128 : n * 128 + 128] = pos_ref[8 * b + n : 8 * b + n + 1, :]
            ct_v[b : b + 1, n * 128 : n * 128 + 128] = ct_ref[8 * b + n : 8 * b + n + 1, :]
    for c in owns:
        c.wait()
    for n in range(len(PHASES)):
        for tz, ty in peers:
            o = tz * 4 + ty
            remote(part(p_hbm.at[which(n), o], n), part(sel_v.at[which(n), o], n), d_ssem.at[n, o], d_rsem.at[n, o],
                   device(x, core, tz, ty)).wait_recv()
        for kind, dev in ((0, x_to), (1, mate)) if PHASES[n][2] else ((1, mate),):
            c = hand(n, kind, which(n), dev)
            c.start()
            sends.append(c)
        if n + AT_ONCE < len(PHASES):
            fetch(n + AT_ONCE)
        if n >= 1 and PHASES[n - 1][2]:
            hand_on(n - 1)
    for n in range(len(PHASES)):
        hand(n, 1, (x + 2 + core) % 4 if PHASES[n][1] else (x + 1 - core) % 4, mate).wait_recv()
        if PHASES[n][2]:
            hand(n, 2, (x + 2 + core) % 4, mate).wait_recv()
    for b in range(NB):
        pltpu.make_async_copy(q_hbm.at[b], q_v.at[b], q_sem.at[b]).wait()

    def forward(half, k):
        b = 2 * half + k
        for t in range(LISTED):
            block = tiles_ref[t, group * NB + b]
            pq_v[b, pl.ds(t * SL, SL), :] = sel_v[block & 3, block >> 2]
        base = (group * NB + b) * 2 * BLK + owner * SL
        for c in range(BLK // CH):
            r = pl.ds(c * CH, CH)
            s = lax.dot_general(pq_v[b], q_v[b, r, :], (((1,), (1,)), ((), ())), preferred_element_type=F32)
            top = jnp.max(s, axis=0, keepdims=True)
            e = jnp.exp2(s * (SCALE * LOG2E) - top * (SCALE * LOG2E))
            e_v[b, :, r] = e.astype(BF16)
            now[half, 0, pl.ds(k, 1), r] = top * SCALE
            now[half, 0, pl.ds(2 + k, 1), r] = jnp.sum(e, axis=0, keepdims=True)
            at = lax.broadcasted_iota(jnp.int32, (SL, CH), 0) == pos_v[pl.ds(b, 1), r] - base
            pick[0, pl.ds(b, 1), r] = jnp.sum(jnp.where(at, s[0:SL], 0.0), axis=0, keepdims=True) * SCALE

    def run(body, steps):
        def one(n, carry):
            body(n)
            return carry

        lax.fori_loop(0, steps, one, 0)

    spread = []

    def tell(half):
        for tz, ty in peers:
            c = remote(now.at[half, 0], now_buf.at[half, me], tell_ssem.at[half, tz * 4 + ty], tell_rsem.at[half, me],
                       device(x, core, tz, ty))
            c.start()
            spread.append(c)

    picks = Exchange(pick, pick_buf, ex_ssem, ex_rsem, [z_peers, y_peers])

    def combine(half):
        parts = [now[half, 0]]
        for tz, ty in peers:
            o = tz * 4 + ty
            remote(now.at[half, 0], now_buf.at[half, o], tell_ssem.at[half, o], tell_rsem.at[half, o],
                   device(x, core, tz, ty)).wait_recv()
            parts.append(now_buf[half, o])
        high = parts[0][0:2]
        for p in parts[1:]:
            high = jnp.maximum(high, p[0:2])
        now[half, 1, 0:2] = high
        now[half, 1, 2:4] = sum(p[2:4] * jnp.exp(p[0:2] - high) for p in parts)

    run(lambda k: forward(0, k), 2)
    tell(0)
    run(lambda k: forward(1, k), 2)
    tell(1)
    combine(0)

    def grads(half, k):
        b = 2 * half + k
        weight = ct_v[pl.ds(b, 1), :] * SCALE
        factor = weight * jnp.exp(now[half, 0, pl.ds(k, 1), :] - now[half, 1, pl.ds(k, 1), :]) / now[half, 1, pl.ds(2 + k, 1), :]
        base = (group * NB + b) * 2 * BLK + owner * SL
        at = lax.broadcasted_iota(jnp.int32, (SL, BLK), 0) == pos_v[pl.ds(b, 1), :] - base
        e_v[b, 0:SL, :] = (e_v[b, 0:SL, :].astype(F32) * factor - jnp.where(at, weight, 0.0)).astype(BF16)
        e_v[b, SL:, :] = (e_v[b, SL:, :].astype(F32) * factor).astype(BF16)

    def passage_product(b):
        out = jnp.dot(e_v[b], q_v[b], preferred_element_type=F32)
        part_v[b, 0:LISTED] = out.astype(BF16).reshape(LISTED, SL, D)

    def query_product(b, quarter):
        r = pl.ds(pl.multiple_of(quarter * 256, 256), 256)
        out = lax.dot_general(e_v[b, :, r], pq_v[b], (((0,), (0,)), ((), ())), preferred_element_type=F32)
        sel_v[b, pl.ds(quarter * 4, 4)] = out.astype(BF16).reshape(4, SL, D)

    def dense(piece, n):
        blocks = []
        for o in range(2):
            for k in range(2):
                p = (2 * n + o) * NB + 2 * piece + k
                blocks.append((part_v[0, slot_s[0, p]] + part_v[1, slot_s[1, p]])
                              + (part_v[2, slot_s[2, p]] + part_v[3, slot_s[3, p]]))
        flat = jnp.concatenate(blocks, axis=0).T
        dp_v[piece, :, :, :, :, pl.ds(pl.multiple_of(n * 256, 256), 256)] = flat.reshape(4, 2, 2, 48, 256)

    cores = {}

    def to_core(piece):
        for k, step in enumerate((2, 1, 3, 0)):
            c = remote(dp_v.at[piece, (x + step) % 4, 1 - core], core_buf.at[piece, k],
                       core_ssem.at[piece, k], core_rsem.at[piece, k], mate)
            c.start()
            cores[piece, k] = c

    def add_core(piece, k):
        place = (x + (2, 1, 3, 0)[k]) % 4
        cores[piece, k].wait_recv()
        for h in range(2):
            dp_v[piece, place, core, h] = (
                dp_v[piece, place, core, h].astype(F32) + core_buf[piece, k, h].astype(F32)).astype(BF16)

    z_next = [z_peers[0], z_peers[2]]
    y_next = [y_peers[0], y_peers[2]]
    left, right = pl.ds(0, 384), pl.ds(384, 384)
    a1 = Ring(z, lambda j, h: sel_v.at[j, pl.ds(8 * h, 8), :, left], z_next, a1_buf, a1_acc, r_ssem.at[0], r_rsem.at[0])
    b1 = Ring(y, lambda j, h: sel_v.at[pl.ds(2 * h, 2), pl.ds(4 * j, 4), :, right], y_next, b1_buf, b1_acc,
              r_ssem.at[1], r_rsem.at[1])
    a2 = Ring(y, lambda j, h: a1_sum.at[j, pl.ds(2 * h, 2)], y_next, a2_buf, a2_acc, r_ssem.at[2], r_rsem.at[2])
    b2 = Ring(z, lambda j, h: b1_sum.at[j, pl.ds(2 * h, 2)], z_next, b2_buf, b2_acc, r_ssem.at[3], r_rsem.at[3])
    xr = [Ring(x, lambda j, h, n=n: dp_v.at[n, j, core, h], x_next, x_buf.at[n], x_acc.at[n],
               r_ssem.at[4 + n], r_rsem.at[4 + n]) for n in range(PIECES)]
    returns, keeps = [], []

    def go_back(piece):
        for h in range(2):
            res = xr[piece].result(h).astype(BF16)
            for n in range(16):
                back[piece, n, pl.ds(48 * h, 48), :] = res[:, n * 128 : n * 128 + 128]
        for tz, ty in peers:
            o = tz * 4 + ty
            c = remote(back.at[piece, o], got.at[piece, me], back_ssem.at[piece, o], back_rsem.at[piece, me],
                       device(x, core, tz, ty))
            c.start()
            returns.append(c)
        c = pltpu.make_async_copy(back.at[piece, me], got.at[piece, me], keep_sem.at[piece])
        c.start()
        keeps.append(c)

    def both(k):
        grads(0, k)
        passage_product(k)

    run(both, 2)
    combine(1)
    run(lambda k: grads(1, k), 2)
    for c in sends:
        c.wait_send()
    opposite = (z + 2) % 4
    for c in range(3):
        r = pl.ds(c * 256, 256)
        out = lax.dot_general(e_v[opposite], pq_v[opposite, :, r], (((0,), (0,)), ((), ())), preferred_element_type=F32)
        sel_v[opposite, :, :, r] = out.astype(BF16).reshape(16, SL, 256)
    a1.ahead()
    run(lambda n: query_product((z + 3 + n) % 4, (y + 2) % 4), 3)
    b1.ahead()
    run(lambda k: passage_product(2 + k), 2)
    run(lambda n: dense(0, n), 8)
    to_core(0)
    run(lambda n: query_product((z + 1 + 2 * (n // 3)) % 4, (y + 3 + n % 3) % 4), 6)
    a1.raw()
    add_core(0, 0)
    xr[0].ahead()
    add_core(0, 1)
    add_core(0, 2)
    xr[0].raw()
    run(lambda n: query_product(z, (y + 3 + n) % 4), 3)
    b1.raw()
    run(lambda n: dense(1, n), 8)
    to_core(1)
    add_core(0, 3)
    a1.forward()
    b1.forward()
    xr[0].forward()
    add_core(1, 0)
    xr[1].ahead()
    add_core(1, 1)
    add_core(1, 2)
    xr[1].raw()
    add_core(1, 3)
    picks.start(0)
    go_back(0)
    pick[1] = sum(picks.parts(0))
    picks.start(1)
    xr[1].forward()
    for h in range(2):
        a1_sum[pl.ds(2 * h, 2)] = a1.result(h).astype(BF16).reshape(2, 4, SL, 384)
    a2.ahead()
    a2.raw()
    for h in range(2):
        b1_sum[pl.ds(2 * h, 2)] = b1.result(h).astype(BF16)
    b2.ahead()
    b2.raw()
    a2.forward()
    b2.forward()
    go_back(1)
    span = pl.ds(pl.multiple_of(y * 256, 256), 256)
    pick[2] = sum(picks.parts(1))

    def final(row):
        return now[z // 2, 1, pl.ds(2 * row + z % 2, 1), span]

    losses_ref[...] = final(0) + jnp.log(final(1)) - pick[2, pl.ds(z, 1), span]
    for h in range(2):
        qg_ref[pl.ds(128 * h, 128), left] = a2.result(h).astype(BF16).reshape(128, 384)
        qg_ref[pl.ds(128 * h, 128), right] = b2.result(h).astype(BF16).reshape(128, 384)
    for piece in range(PIECES):
        for tz, ty in peers:
            n = tz * 4 + ty
            remote(back.at[piece, n], got.at[piece, n], back_ssem.at[piece, n], back_rsem.at[piece, n],
                   device(x, core, tz, ty)).wait_recv()
    for moved in [picks, a1, b1, a2, b2] + xr:
        moved.drain()
    for c in list(cores.values()) + returns + spread:
        c.wait_send()
    for c in keeps:
        c.wait()


def lay_kernel(losses_in, qg_in, got, losses_ref, qg_ref, pg_ref):
    losses_ref[...] = losses_in[...]
    qg_ref[...] = qg_in[...]
    for piece in range(PIECES):
        for n in range(8):
            one, two = got[piece, 2 * n], got[piece, 2 * n + 1]
            for k in range(2):
                h = slice(k * SL, k * SL + SL)
                first = (2 * piece + k) * BLK + n * 128
                pg_ref[:, first : first + 128] = jnp.concatenate([one[:, h], two[:, h]], axis=1)


SMEM = pl.BlockSpec(memory_space=pltpu.SMEM)
VMEM = pl.BlockSpec(memory_space=pltpu.VMEM)
ANY = pl.BlockSpec(memory_space=pl.ANY)


def whole(tiles, positives, cotangent, queries, passages):
    dma = pltpu.SemaphoreType.DMA
    return pl.pallas_call(
        whole_kernel,
        out_shape=[
            jax.ShapeDtypeStruct((1, 256), F32),
            jax.ShapeDtypeStruct((256, D), BF16),
            jax.ShapeDtypeStruct((PIECES, 16, 96, 128), BF16),
        ],
        in_specs=[SMEM, VMEM, VMEM, ANY, ANY],
        out_specs=[VMEM, VMEM, ANY],
        scratch_shapes=[
            pltpu.VMEM((NB, BLK, D), BF16),
            pltpu.VMEM((NB, 16, SL, D), BF16),
            pltpu.VMEM((NB, LISTED * SL, D), BF16),
            pltpu.VMEM((NB, LISTED * SL, BLK), BF16),
            pltpu.VMEM((NB, LISTED + 1, SL, D), BF16),
            pltpu.VMEM((PIECES, 4, 2, 2, 48, 2048), BF16),
            pltpu.SMEM((NB, 64), jnp.int32),
            pltpu.VMEM((8, BLK), jnp.int32), pltpu.VMEM((8, BLK), F32),
            pltpu.VMEM((2, 2, 4, BLK), F32), pltpu.VMEM((2, 16, 4, BLK), F32),
            pltpu.VMEM((3, 4, BLK), F32), pltpu.VMEM((2, 3, 4, BLK), F32),
            pltpu.VMEM((2, 3, 8, SL, 384), BF16), pltpu.VMEM((2, 8, SL, 384), BF16),
            pltpu.VMEM((4, 4, SL, 384), BF16),
            pltpu.VMEM((2, 3, 2, 4, SL, 384), BF16), pltpu.VMEM((2, 2, 4, SL, 384), BF16),
            pltpu.VMEM((4, 4, SL, 384), BF16),
            pltpu.VMEM((2, 3, 2, SL, 384), BF16), pltpu.VMEM((2, 2, SL, 384), BF16),
            pltpu.VMEM((2, 3, 2, SL, 384), BF16), pltpu.VMEM((2, 2, SL, 384), BF16),
            pltpu.VMEM((PIECES, 2, 3, 48, 2048), BF16), pltpu.VMEM((PIECES, 2, 48, 2048), BF16),
            pltpu.VMEM((PIECES, 4, 2, 48, 2048), BF16),
            pltpu.VMEM((PIECES, 16, 96, 128), BF16),
            dma((NB,)), dma((2,)),
            dma((len(PHASES), 16)), dma((len(PHASES), 16)),
            dma((3, len(PHASES))), dma((3, len(PHASES))),
            dma((2, 3)), dma((2, 3)), dma((2, 16)), dma((2, 16)),
            dma((6, 2, 3)), dma((6, 2, 3)),
            dma((PIECES, 4)), dma((PIECES, 4)),
            dma((PIECES, 16)), dma((PIECES, 16)), dma((PIECES,)),
        ],
        compiler_params=pltpu.CompilerParams(
            collective_id=1, has_side_effects=True, vmem_limit_bytes=62 * 2**20),
        name="whole",
    )(tiles, positives, cotangent, queries, passages)


def lay(losses, query_grads, got):
    return pl.pallas_call(
        lay_kernel,
        out_shape=[
            jax.ShapeDtypeStruct((1, 256), F32),
            jax.ShapeDtypeStruct((256, D), BF16),
            jax.ShapeDtypeStruct((96, NB * BLK), BF16),
        ],
        in_specs=[VMEM, VMEM, VMEM],
        out_specs=[VMEM, VMEM, VMEM],
        name="lay",
    )(losses, query_grads, got)


def per_device(queries, passages, tiles, positives, cotangent):
    losses, query_grads, passage_grads = lay(*whole(
        tiles.T, positives.reshape(32, 128), cotangent.reshape(32, 128),
        queries.reshape(NB, BLK, D), passages.reshape(NB, 16, SL, D)))
    return losses.reshape(256), query_grads, passage_grads.T


def solution(mesh):
    in_specs = (P("pb", None), P("pa", None), P(), P("pb"), P("pb"))
    out_specs = (P(("pb", "pa")), P(("pb", "pa"), None), P("pa", "pb"))
    return jax.shard_map(
        per_device, mesh=mesh, in_specs=in_specs, out_specs=out_specs, check_vma=False
    )
```

```python
import jax
import jax.numpy as jnp
from jax import lax
from jax.experimental import pallas as pl
from jax.experimental.pallas import tpu as pltpu
from jax.sharding import PartitionSpec as P

D = 768
BLK = 1024
NB = 4
LISTED = 8
SL = 64
HALF = SL // 2
PHASES = ((0, 0, False, True), (0, 256, False, True), (0, 512, False, True),
          (1, 0, False, True), (1, 256, False, True), (1, 512, False, False), (1, 512, True, False))
EARLY = 3
AT_ONCE = 3
PIECES = 2
SCALE = D ** (-0.5)
LOG2E = 1.4426950408889634
CH = 256
F32 = jnp.float32
BF16 = jnp.bfloat16


def around():
    group, owner = lax.axis_index("pb"), lax.axis_index("pa")
    return group // 2, group % 2, owner // 4, owner % 4


def device(x, core, z, y):
    return (x * 2 + core, z * 4 + y)


def greet(devices):
    barrier = pltpu.get_barrier_semaphore()
    for dev in devices:
        pl.semaphore_signal(barrier, inc=1, device_id=dev, device_id_type=pl.DeviceIdType.MESH)
    pl.semaphore_wait(barrier, len(devices))


def remote(src, dst, send_sem, recv_sem, dev):
    return pltpu.make_async_remote_copy(
        src_ref=src, dst_ref=dst, send_sem=send_sem, recv_sem=recv_sem,
        device_id=dev, device_id_type=pl.DeviceIdType.MESH)


AHEAD, RAW, SUMMED = 0, 1, 2


class Ring:
    def __init__(self, me, chunk, neighbours, buf, acc, send_sem, recv_sem):
        self.me, self.chunk, self.buf, self.acc = me, chunk, buf, acc
        self.send = lambda d, kind, src: remote(
            src, buf.at[d, kind], send_sem.at[d, kind], recv_sem.at[d, kind], neighbours[d])
        self.sent = {}

    def at(self, step, half):
        return self.chunk((self.me + step) % 4, half)

    def go(self, d, kind, src):
        c = self.send(d, kind, src)
        c.start()
        self.sent[d, kind] = c

    def ahead(self):
        self.go(0, AHEAD, self.at(2, 0))
        self.go(1, AHEAD, self.at(2, 1))

    def raw(self):
        self.go(0, RAW, self.at(1, 1))
        self.go(1, RAW, self.at(3, 0))

    def forward(self):
        for d, step in ((0, 1), (1, 3)):
            self.sent[d, AHEAD].wait_recv()
            self.acc[d] = (self.at(step, d)[...].astype(F32) + self.buf[d, AHEAD].astype(F32)).astype(BF16)
            self.go(d, SUMMED, self.acc.at[d])

    def result(self, half):
        a, b = (SUMMED, RAW) if half == 0 else (RAW, SUMMED)
        self.sent[0, a].wait_recv()
        self.sent[1, b].wait_recv()
        return self.at(0, half)[...].astype(F32) + self.buf[0, a].astype(F32) + self.buf[1, b].astype(F32)

    def drain(self):
        for c in self.sent.values():
            c.wait_send()


class Exchange:
    def __init__(self, now, buf, send_sem, recv_sem, peers):
        self.now, self.buf, self.peers = now, buf, peers
        self.sems = send_sem, recv_sem
        self.sent = {}

    def start(self, stage):
        for d in range(3):
            c = remote(self.now.at[stage], self.buf.at[stage, d], self.sems[0].at[stage, d], self.sems[1].at[stage, d],
                       self.peers[stage][d])
            c.start()
            self.sent[stage, d] = c

    def parts(self, stage):
        for d in range(3):
            self.sent[stage, d].wait_recv()
        return [self.now[stage]] + [self.buf[stage, d] for d in range(3)]

    def drain(self):
        for c in self.sent.values():
            c.wait_send()


def whole_kernel(tiles_ref, pos_hbm, ct_hbm, q_hbm, p_hbm, losses_hbm, qg_hbm, got,
                 pos_ref, ct_ref, losses_ref, qg_ref, q_v, sel_a, sel_b, dq_v, pq_v, e_v, part_v, dp_v, slot_s, pos_v, ct_v, local, now, now_buf, pick, pick_buf,
                 a1_buf, a1_acc, a1_sum, b1_buf, b1_acc, b1_sum, a2_buf, a2_acc, b2_buf, b2_acc,
                 x_buf, x_acc, core_buf, back,
                 q_sem, own_sem, d_ssem, d_rsem, hand_ssem, hand_rsem, ex_ssem, ex_rsem, tell_ssem, tell_rsem,
                 r_ssem, r_rsem, core_ssem, core_rsem, back_ssem, back_rsem, keep_sem):
    group, owner = lax.axis_index("pb"), lax.axis_index("pa")
    x, core, z, y = around()
    me = z * 4 + y
    sel_v = sel_a, sel_b
    peers = [((z + dz) % 4, (y + dy) % 4) for dz in (2, 1, 3, 0) for dy in (2, 1, 3, 0) if dz or dy]
    z_peers = [device(x, core, (z + d) % 4, y) for d in (1, 2, 3)]
    y_peers = [device(x, core, z, (y + d) % 4) for d in (1, 2, 3)]
    x_next = [device((x + 1) % 4, core, z, y), device((x + 3) % 4, core, z, y)]
    mate = device(x, 1 - core, z, y)
    for b in range(NB):
        pltpu.make_async_copy(q_hbm.at[b], q_v.at[b], q_sem.at[b]).start()
    small = [pltpu.make_async_copy(pos_hbm, pos_ref, own_sem.at[3]), pltpu.make_async_copy(ct_hbm, ct_ref, own_sem.at[4])]
    for c in small:
        c.start()
    greet([device(x, core, tz, ty) for tz, ty in peers] + x_next + [mate])

    to = (x + 1 + 2 * core) % 4
    source = (x + 3 + 2 * core) % 4
    x_to, x_from = device(to, core, z, y), device(source, core, z, y)
    mine = (x + core) % 4
    theirs = (source + core) % 4

    def given(b, s, n):
        return p_hbm.at[b, s, pl.ds(HALF * PHASES[n][0], HALF), pl.ds(PHASES[n][1], 256)]

    def kept(b, n):
        return sel_v[PHASES[n][0]].at[b, :, :, pl.ds(PHASES[n][1], 256)]

    def kept_of(b, o, n):
        return sel_v[PHASES[n][0]].at[b, o, :, pl.ds(PHASES[n][1], 256)]

    def which(n):
        return theirs if PHASES[n][2] else mine

    owns = [pltpu.make_async_copy(p_hbm.at[mine, me, pl.ds(HALF * k, HALF)], sel_v[k].at[mine, me], own_sem.at[k])
            for k in range(2)]
    owns.append(pltpu.make_async_copy(given(theirs, me, -1), kept_of(theirs, me, -1), own_sem.at[2]))
    for c in owns:
        c.start()
    sends = []

    def fetch(n):
        for tz, ty in peers:
            c = remote(given(which(n), tz * 4 + ty, n), kept_of(which(n), me, n),
                       d_ssem.at[n, tz * 4 + ty], d_rsem.at[n, me], device(x, core, tz, ty))
            c.start()
            sends.append(c)

    def hand(n, kind, b, dev):
        return remote(kept(b, n), kept(b, n), hand_ssem.at[kind, n], hand_rsem.at[kind, n], dev)

    def hand_on(n):
        hand(n, 0, theirs, x_from).wait_recv()
        c = hand(n, 2, theirs, mate)
        c.start()
        sends.append(c)

    for n in range(AT_ONCE):
        fetch(n)
    for c in small:
        c.wait()
    for b in range(NB):
        def find(p, carry, b=b):
            at = jnp.int32(LISTED)
            for t in range(LISTED):
                at = jnp.where(tiles_ref[t, group * NB + b] == p, t, at)
            slot_s[b, p] = at
            return carry

        lax.fori_loop(0, 64, find, 0)
        part_v[b, :, LISTED] = jnp.zeros((2, HALF, D), BF16)
        for n in range(8):
            pos_v[b : b + 1, n * 128 : n * 128 + 128] = pos_ref[8 * b + n : 8 * b + n + 1, :]
            ct_v[b : b + 1, n * 128 : n * 128 + 128] = ct_ref[8 * b + n : 8 * b + n + 1, :]
    for c in owns:
        c.wait()
    def forward(half, b):
        first = half * LISTED * HALF
        for t in range(LISTED):
            block = tiles_ref[t, group * NB + b]
            pq_v[b, pl.ds(first + t * HALF, HALF), :] = sel_v[half][block & 3, block >> 2]
        base = (group * NB + b) * 2 * BLK + owner * SL + half * HALF
        for c in range(BLK // CH):
            r = pl.ds(c * CH, CH)
            s = lax.dot_general(pq_v[b, pl.ds(first, LISTED * HALF), :], q_v[b, r, :], (((1,), (1,)), ((), ())),
                                preferred_element_type=F32)
            top = jnp.max(s, axis=0, keepdims=True)
            e = jnp.exp2(s * (SCALE * LOG2E) - top * (SCALE * LOG2E))
            e_v[b, pl.ds(first, LISTED * HALF), r] = e.astype(BF16)
            local[half, pl.ds(b, 1), r] = top * SCALE
            local[half, pl.ds(NB + b, 1), r] = jnp.sum(e, axis=0, keepdims=True)
            at = lax.broadcasted_iota(jnp.int32, (HALF, CH), 0) == pos_v[pl.ds(b, 1), r] - base
            got_here = jnp.sum(jnp.where(at, s[0:HALF], 0.0), axis=0, keepdims=True) * SCALE
            pick[0, pl.ds(b, 1), r] = got_here if half == 0 else pick[0, pl.ds(b, 1), r] + got_here

    def run(body, steps):
        def one(n, carry):
            body(n)
            return carry

        lax.fori_loop(0, steps, one, 0)

    def passed(n):
        hand(n, 1, (x + 2 + core) % 4 if PHASES[n][2] else (x + 1 - core) % 4, mate).wait_recv()
        if PHASES[n][3]:
            hand(n, 2, (x + 2 + core) % 4, mate).wait_recv()

    for n in range(len(PHASES)):
        for tz, ty in peers:
            o = tz * 4 + ty
            remote(given(which(n), o, n), kept_of(which(n), o, n), d_ssem.at[n, o], d_rsem.at[n, o],
                   device(x, core, tz, ty)).wait_recv()
        for kind, dev in ((0, x_to), (1, mate)) if PHASES[n][3] else ((1, mate),):
            c = hand(n, kind, which(n), dev)
            c.start()
            sends.append(c)
        if n + AT_ONCE < len(PHASES):
            fetch(n + AT_ONCE)
        if n == len(PHASES) - 2:
            for k in range(EARLY):
                passed(k)
            for b in range(NB):
                pltpu.make_async_copy(q_hbm.at[b], q_v.at[b], q_sem.at[b]).wait()
            run(lambda b: forward(0, b), NB)
        if n >= 1 and PHASES[n - 1][3]:
            hand_on(n - 1)
    for n in range(EARLY, len(PHASES)):
        passed(n)

    spread = []

    def tell(half):
        two = slice(2 * half, 2 * half + 2)
        tot = slice(NB + 2 * half, NB + 2 * half + 2)
        high = jnp.maximum(local[0, two], local[1, two])
        now[half, 0, 0:2] = high
        now[half, 0, 2:4] = sum(local[k, tot] * jnp.exp(local[k, two] - high) for k in range(2))
        for tz, ty in peers:
            c = remote(now.at[half, 0], now_buf.at[half, me], tell_ssem.at[half, tz * 4 + ty], tell_rsem.at[half, me],
                       device(x, core, tz, ty))
            c.start()
            spread.append(c)

    picks = Exchange(pick, pick_buf, ex_ssem, ex_rsem, [z_peers, y_peers])

    def combine(half):
        parts = [now[half, 0]]
        for tz, ty in peers:
            o = tz * 4 + ty
            remote(now.at[half, 0], now_buf.at[half, o], tell_ssem.at[half, o], tell_rsem.at[half, o],
                   device(x, core, tz, ty)).wait_recv()
            parts.append(now_buf[half, o])
        high = parts[0][0:2]
        for p in parts[1:]:
            high = jnp.maximum(high, p[0:2])
        now[half, 1, 0:2] = high
        now[half, 1, 2:4] = sum(p[2:4] * jnp.exp(p[0:2] - high) for p in parts)

    run(lambda k: forward(1, k), 2)
    tell(0)
    run(lambda k: forward(1, 2 + k), 2)
    tell(1)
    combine(0)

    def grads(half, k):
        b = 2 * half + k
        weight = ct_v[pl.ds(b, 1), :] * SCALE
        for k2 in range(2):
            factor = weight * jnp.exp(local[k2, pl.ds(b, 1), :] - now[half, 1, pl.ds(k, 1), :]) / now[half, 1, pl.ds(2 + k, 1), :]
            base = (group * NB + b) * 2 * BLK + owner * SL + k2 * HALF
            at = lax.broadcasted_iota(jnp.int32, (HALF, BLK), 0) == pos_v[pl.ds(b, 1), :] - base
            one = slice(k2 * LISTED * HALF, k2 * LISTED * HALF + HALF)
            rest = slice(k2 * LISTED * HALF + HALF, (k2 + 1) * LISTED * HALF)
            e_v[b, one, :] = (e_v[b, one, :].astype(F32) * factor - jnp.where(at, weight, 0.0)).astype(BF16)
            e_v[b, rest, :] = (e_v[b, rest, :].astype(F32) * factor).astype(BF16)

    def passage_product(b):
        out = jnp.dot(e_v[b], q_v[b], preferred_element_type=F32)
        part_v[b, :, 0:LISTED] = out.astype(BF16).reshape(2, LISTED, HALF, D)

    def query_product(b, quarter):
        r = pl.ds(pl.multiple_of(quarter * 256, 256), 256)
        out = lax.dot_general(e_v[b, :, r], pq_v[b], (((0,), (0,)), ((), ())), preferred_element_type=F32)
        dq_v[b, pl.ds(quarter * 4, 4)] = out.astype(BF16).reshape(4, SL, D)

    def dense(piece, n):
        blocks = []
        for o in range(2):
            for k in range(2):
                p = (2 * n + o) * NB + 2 * piece + k
                at = [slot_s[b, p] for b in range(NB)]
                for half in range(2):
                    blocks.append((part_v[0, half, at[0]] + part_v[1, half, at[1]])
                                  + (part_v[2, half, at[2]] + part_v[3, half, at[3]]))
        flat = jnp.concatenate(blocks, axis=0).T
        dp_v[piece, :, :, :, :, pl.ds(pl.multiple_of(n * 256, 256), 256)] = flat.reshape(4, 2, 2, 48, 256)

    cores = {}

    def to_core(piece):
        for k, step in enumerate((2, 1, 3, 0)):
            c = remote(dp_v.at[piece, (x + step) % 4, 1 - core], core_buf.at[piece, k],
                       core_ssem.at[piece, k], core_rsem.at[piece, k], mate)
            c.start()
            cores[piece, k] = c

    def add_core(piece, k):
        place = (x + (2, 1, 3, 0)[k]) % 4
        cores[piece, k].wait_recv()
        for h in range(2):
            dp_v[piece, place, core, h] = (
                dp_v[piece, place, core, h].astype(F32) + core_buf[piece, k, h].astype(F32)).astype(BF16)

    z_next = [z_peers[0], z_peers[2]]
    y_next = [y_peers[0], y_peers[2]]
    left, right = pl.ds(0, 384), pl.ds(384, 384)
    a1 = Ring(z, lambda j, h: dq_v.at[j, pl.ds(8 * h, 8), :, left], z_next, a1_buf, a1_acc, r_ssem.at[0], r_rsem.at[0])
    b1 = Ring(y, lambda j, h: dq_v.at[pl.ds(2 * h, 2), pl.ds(4 * j, 4), :, right], y_next, b1_buf, b1_acc,
              r_ssem.at[1], r_rsem.at[1])
    a2 = Ring(y, lambda j, h: a1_sum.at[j, pl.ds(2 * h, 2)], y_next, a2_buf, a2_acc, r_ssem.at[2], r_rsem.at[2])
    b2 = Ring(z, lambda j, h: b1_sum.at[j, pl.ds(2 * h, 2)], z_next, b2_buf, b2_acc, r_ssem.at[3], r_rsem.at[3])
    xr = [Ring(x, lambda j, h, n=n: dp_v.at[n, j, core, h], x_next, x_buf.at[n], x_acc.at[n],
               r_ssem.at[4 + n], r_rsem.at[4 + n]) for n in range(PIECES)]
    returns, keeps = [], []

    def go_back(piece):
        for h in range(2):
            res = xr[piece].result(h).astype(BF16)
            for n in range(16):
                back[piece, n, pl.ds(48 * h, 48), :] = res[:, n * 128 : n * 128 + 128]
        for tz, ty in peers:
            o = tz * 4 + ty
            c = remote(back.at[piece, o], got.at[piece, me], back_ssem.at[piece, o], back_rsem.at[piece, me],
                       device(x, core, tz, ty))
            c.start()
            returns.append(c)
        c = pltpu.make_async_copy(back.at[piece, me], got.at[piece, me], keep_sem.at[piece])
        c.start()
        keeps.append(c)

    def both(k):
        grads(0, k)
        passage_product(k)

    run(both, 2)
    combine(1)
    run(lambda k: grads(1, k), 2)
    opposite = (z + 2) % 4
    for c in range(3):
        r = pl.ds(c * 256, 256)
        out = lax.dot_general(e_v[opposite], pq_v[opposite, :, r], (((0,), (0,)), ((), ())), preferred_element_type=F32)
        dq_v[opposite, :, :, r] = out.astype(BF16).reshape(16, SL, 256)
    a1.ahead()
    run(lambda n: query_product((z + 3 + n) % 4, (y + 2) % 4), 3)
    b1.ahead()
    run(lambda k: passage_product(2 + k), 2)
    run(lambda n: dense(0, n), 8)
    to_core(0)
    run(lambda n: query_product((z + 1 + 2 * (n // 3)) % 4, (y + 3 + n % 3) % 4), 6)
    a1.raw()
    add_core(0, 0)
    xr[0].ahead()
    add_core(0, 1)
    add_core(0, 2)
    xr[0].raw()
    run(lambda n: query_product(z, (y + 3 + n) % 4), 3)
    b1.raw()
    run(lambda n: dense(1, n), 8)
    to_core(1)
    add_core(0, 3)
    a1.forward()
    b1.forward()
    xr[0].forward()
    add_core(1, 0)
    xr[1].ahead()
    add_core(1, 1)
    add_core(1, 2)
    xr[1].raw()
    add_core(1, 3)
    picks.start(0)
    go_back(0)
    pick[1] = sum(picks.parts(0))
    picks.start(1)
    xr[1].forward()
    for h in range(2):
        a1_sum[pl.ds(2 * h, 2)] = a1.result(h).astype(BF16).reshape(2, 4, SL, 384)
    a2.ahead()
    a2.raw()
    for h in range(2):
        b1_sum[pl.ds(2 * h, 2)] = b1.result(h).astype(BF16)
    b2.ahead()
    b2.raw()
    a2.forward()
    b2.forward()
    go_back(1)
    span = pl.ds(pl.multiple_of(y * 256, 256), 256)
    pick[2] = sum(picks.parts(1))

    def final(row):
        return now[z // 2, 1, pl.ds(2 * row + z % 2, 1), span]

    losses_ref[...] = final(0) + jnp.log(final(1)) - pick[2, pl.ds(z, 1), span]
    for h in range(2):
        qg_ref[pl.ds(128 * h, 128), left] = a2.result(h).astype(BF16).reshape(128, 384)
        qg_ref[pl.ds(128 * h, 128), right] = b2.result(h).astype(BF16).reshape(128, 384)
    keeps.append(pltpu.make_async_copy(losses_ref, losses_hbm, keep_sem.at[2]))
    keeps.append(pltpu.make_async_copy(qg_ref, qg_hbm, keep_sem.at[3]))
    for c in keeps[-2:]:
        c.start()
    for piece in range(PIECES):
        for tz, ty in peers:
            n = tz * 4 + ty
            remote(back.at[piece, n], got.at[piece, n], back_ssem.at[piece, n], back_rsem.at[piece, n],
                   device(x, core, tz, ty)).wait_recv()
    for moved in [picks, a1, b1, a2, b2] + xr:
        moved.drain()
    for c in sends + list(cores.values()) + returns + spread:
        c.wait_send()
    for c in keeps:
        c.wait()


def lay_kernel(losses_in, qg_in, got, losses_ref, qg_ref, pg_ref):
    losses_ref[...] = losses_in[...]
    qg_ref[...] = qg_in[...]
    for piece in range(PIECES):
        for n in range(8):
            one, two = got[piece, 2 * n], got[piece, 2 * n + 1]
            for k in range(2):
                h = slice(k * SL, k * SL + SL)
                first = (2 * piece + k) * BLK + n * 128
                pg_ref[:, first : first + 128] = jnp.concatenate([one[:, h], two[:, h]], axis=1)


SMEM = pl.BlockSpec(memory_space=pltpu.SMEM)
VMEM = pl.BlockSpec(memory_space=pltpu.VMEM)
ANY = pl.BlockSpec(memory_space=pl.ANY)


def whole(tiles, positives, cotangent, queries, passages):
    dma = pltpu.SemaphoreType.DMA
    return pl.pallas_call(
        whole_kernel,
        out_shape=[
            jax.ShapeDtypeStruct((1, 256), F32),
            jax.ShapeDtypeStruct((256, D), BF16),
            jax.ShapeDtypeStruct((PIECES, 16, 96, 128), BF16),
        ],
        in_specs=[SMEM, ANY, ANY, ANY, ANY],
        out_specs=[ANY, ANY, ANY],
        scratch_shapes=[
            pltpu.VMEM((32, 128), jnp.int32), pltpu.VMEM((32, 128), F32),
            pltpu.VMEM((1, 256), F32), pltpu.VMEM((256, D), BF16),
            pltpu.VMEM((NB, BLK, D), BF16),
            pltpu.VMEM((NB, 16, HALF, D), BF16), pltpu.VMEM((NB, 16, HALF, D), BF16),
            pltpu.VMEM((NB, 16, SL, D), BF16),
            pltpu.VMEM((NB, LISTED * SL, D), BF16),
            pltpu.VMEM((NB, LISTED * SL, BLK), BF16),
            pltpu.VMEM((NB, 2, LISTED + 1, HALF, D), BF16),
            pltpu.VMEM((PIECES, 4, 2, 2, 48, 2048), BF16),
            pltpu.SMEM((NB, 64), jnp.int32),
            pltpu.VMEM((8, BLK), jnp.int32), pltpu.VMEM((8, BLK), F32), pltpu.VMEM((2, 8, BLK), F32),
            pltpu.VMEM((2, 2, 4, BLK), F32), pltpu.VMEM((2, 16, 4, BLK), F32),
            pltpu.VMEM((3, 4, BLK), F32), pltpu.VMEM((2, 3, 4, BLK), F32),
            pltpu.VMEM((2, 3, 8, SL, 384), BF16), pltpu.VMEM((2, 8, SL, 384), BF16),
            pltpu.VMEM((4, 4, SL, 384), BF16),
            pltpu.VMEM((2, 3, 2, 4, SL, 384), BF16), pltpu.VMEM((2, 2, 4, SL, 384), BF16),
            pltpu.VMEM((4, 4, SL, 384), BF16),
            pltpu.VMEM((2, 3, 2, SL, 384), BF16), pltpu.VMEM((2, 2, SL, 384), BF16),
            pltpu.VMEM((2, 3, 2, SL, 384), BF16), pltpu.VMEM((2, 2, SL, 384), BF16),
            pltpu.VMEM((PIECES, 2, 3, 48, 2048), BF16), pltpu.VMEM((PIECES, 2, 48, 2048), BF16),
            pltpu.VMEM((PIECES, 4, 2, 48, 2048), BF16),
            pltpu.VMEM((PIECES, 16, 96, 128), BF16),
            dma((NB,)), dma((5,)),
            dma((len(PHASES), 16)), dma((len(PHASES), 16)),
            dma((3, len(PHASES))), dma((3, len(PHASES))),
            dma((2, 3)), dma((2, 3)), dma((2, 16)), dma((2, 16)),
            dma((6, 2, 3)), dma((6, 2, 3)),
            dma((PIECES, 4)), dma((PIECES, 4)),
            dma((PIECES, 16)), dma((PIECES, 16)), dma((4,)),
        ],
        compiler_params=pltpu.CompilerParams(
            collective_id=1, has_side_effects=True, vmem_limit_bytes=62 * 2**20),
        name="whole",
    )(tiles, positives, cotangent, queries, passages)


def lay(losses, query_grads, got):
    return pl.pallas_call(
        lay_kernel,
        out_shape=[
            jax.ShapeDtypeStruct((1, 256), F32),
            jax.ShapeDtypeStruct((256, D), BF16),
            jax.ShapeDtypeStruct((96, NB * BLK), BF16),
        ],
        in_specs=[VMEM, VMEM, VMEM],
        out_specs=[VMEM, VMEM, VMEM],
        name="lay",
    )(losses, query_grads, got)


def per_device(queries, passages, tiles, positives, cotangent):
    losses, query_grads, passage_grads = lay(*whole(
        tiles.T, positives.reshape(32, 128), cotangent.reshape(32, 128),
        queries.reshape(NB, BLK, D), passages.reshape(NB, 16, SL, D)))
    return losses.reshape(256), query_grads, passage_grads.T


def solution(mesh):
    in_specs = (P("pb", None), P("pa", None), P(), P("pb"), P("pb"))
    out_specs = (P(("pb", "pa")), P(("pb", "pa"), None), P("pa", "pb"))
    return jax.shard_map(
        per_device, mesh=mesh, in_specs=in_specs, out_specs=out_specs, check_vma=False
    )
```

```python
import jax
import jax.numpy as jnp
from jax import lax
from jax.experimental import pallas as pl
from jax.experimental.pallas import tpu as pltpu
from jax.sharding import PartitionSpec as P

D = 768
BLK = 1024
NB = 4
LISTED = 8
SL = 64
HALF = SL // 2
PHASES = ((0, 0, False, True), (0, 256, False, True), (0, 512, False, True),
          (1, 0, False, True), (1, 256, False, True), (1, 512, False, False), (1, 512, True, False))
EARLY = 3
AT_ONCE = 3
PIECES = 2
SCALE = D ** (-0.5)
LOG2E = 1.4426950408889634
CH = 256
F32 = jnp.float32
BF16 = jnp.bfloat16


def around():
    group, owner = lax.axis_index("pb"), lax.axis_index("pa")
    return group // 2, group % 2, owner // 4, owner % 4


def device(x, core, z, y):
    return (x * 2 + core, z * 4 + y)


def greet(devices):
    barrier = pltpu.get_barrier_semaphore()
    for dev in devices:
        pl.semaphore_signal(barrier, inc=1, device_id=dev, device_id_type=pl.DeviceIdType.MESH)
    pl.semaphore_wait(barrier, len(devices))


def remote(src, dst, send_sem, recv_sem, dev):
    return pltpu.make_async_remote_copy(
        src_ref=src, dst_ref=dst, send_sem=send_sem, recv_sem=recv_sem,
        device_id=dev, device_id_type=pl.DeviceIdType.MESH)


AHEAD, RAW, SUMMED = 0, 1, 2


class Ring:
    def __init__(self, me, chunk, neighbours, buf, acc, send_sem, recv_sem):
        self.me, self.chunk, self.buf, self.acc = me, chunk, buf, acc
        self.send = lambda d, kind, src: remote(
            src, buf.at[d, kind], send_sem.at[d, kind], recv_sem.at[d, kind], neighbours[d])
        self.sent = {}

    def at(self, step, half):
        return self.chunk((self.me + step) % 4, half)

    def go(self, d, kind, src):
        c = self.send(d, kind, src)
        c.start()
        self.sent[d, kind] = c

    def ahead(self):
        self.go(0, AHEAD, self.at(2, 0))
        self.go(1, AHEAD, self.at(2, 1))

    def raw(self):
        self.go(0, RAW, self.at(1, 1))
        self.go(1, RAW, self.at(3, 0))

    def forward(self):
        for d, step in ((0, 1), (1, 3)):
            self.sent[d, AHEAD].wait_recv()
            self.acc[d] = (self.at(step, d)[...].astype(F32) + self.buf[d, AHEAD].astype(F32)).astype(BF16)
            self.go(d, SUMMED, self.acc.at[d])

    def result(self, half):
        a, b = (SUMMED, RAW) if half == 0 else (RAW, SUMMED)
        self.sent[0, a].wait_recv()
        self.sent[1, b].wait_recv()
        return self.at(0, half)[...].astype(F32) + self.buf[0, a].astype(F32) + self.buf[1, b].astype(F32)

    def drain(self):
        for c in self.sent.values():
            c.wait_send()


class Exchange:
    def __init__(self, now, buf, send_sem, recv_sem, peers):
        self.now, self.buf, self.peers = now, buf, peers
        self.sems = send_sem, recv_sem
        self.sent = {}

    def start(self, stage):
        for d in range(3):
            c = remote(self.now.at[stage], self.buf.at[stage, d], self.sems[0].at[stage, d], self.sems[1].at[stage, d],
                       self.peers[stage][d])
            c.start()
            self.sent[stage, d] = c

    def parts(self, stage):
        for d in range(3):
            self.sent[stage, d].wait_recv()
        return [self.now[stage]] + [self.buf[stage, d] for d in range(3)]

    def drain(self):
        for c in self.sent.values():
            c.wait_send()


def whole_kernel(tiles_ref, pos_hbm, ct_hbm, q_hbm, p_hbm, losses_hbm, qg_hbm, got,
                 pos_ref, ct_ref, losses_ref, qg_ref, q_v, sel_a, sel_b, dq_v, pq_v, e_v, part_v, dp_v, slot_s, pos_v, ct_v, local, now, now_buf, pick, pick_buf,
                 a1_buf, a1_acc, a1_sum, b1_buf, b1_acc, b1_sum, a2_buf, a2_acc, b2_buf, b2_acc,
                 x_buf, x_acc, core_buf, back,
                 q_sem, own_sem, d_ssem, d_rsem, hand_ssem, hand_rsem, ex_ssem, ex_rsem, tell_ssem, tell_rsem,
                 r_ssem, r_rsem, core_ssem, core_rsem, back_ssem, back_rsem, keep_sem):
    group, owner = lax.axis_index("pb"), lax.axis_index("pa")
    x, core, z, y = around()
    me = z * 4 + y
    sel_v = sel_a, sel_b
    peers = [((z + dz) % 4, (y + dy) % 4) for dz in (2, 1, 3, 0) for dy in (2, 1, 3, 0) if dz or dy]
    z_peers = [device(x, core, (z + d) % 4, y) for d in (1, 2, 3)]
    y_peers = [device(x, core, z, (y + d) % 4) for d in (1, 2, 3)]
    x_next = [device((x + 1) % 4, core, z, y), device((x + 3) % 4, core, z, y)]
    mate = device(x, 1 - core, z, y)
    for b in range(NB):
        pltpu.make_async_copy(q_hbm.at[b], q_v.at[b], q_sem.at[b]).start()
    small = [pltpu.make_async_copy(pos_hbm, pos_ref, own_sem.at[3]), pltpu.make_async_copy(ct_hbm, ct_ref, own_sem.at[4])]
    for c in small:
        c.start()
    greet([device(x, core, tz, ty) for tz, ty in peers] + x_next + [mate])

    to = (x + 1 + 2 * core) % 4
    source = (x + 3 + 2 * core) % 4
    x_to, x_from = device(to, core, z, y), device(source, core, z, y)
    mine = (x + core) % 4
    theirs = (source + core) % 4

    def given(b, s, n):
        return p_hbm.at[b, s, pl.ds(HALF * PHASES[n][0], HALF), pl.ds(PHASES[n][1], 256)]

    def kept(b, n):
        return sel_v[PHASES[n][0]].at[b, :, :, pl.ds(PHASES[n][1], 256)]

    def kept_of(b, o, n):
        return sel_v[PHASES[n][0]].at[b, o, :, pl.ds(PHASES[n][1], 256)]

    def which(n):
        return theirs if PHASES[n][2] else mine

    owns = [pltpu.make_async_copy(p_hbm.at[mine, me, pl.ds(HALF * k, HALF)], sel_v[k].at[mine, me], own_sem.at[k])
            for k in range(2)]
    owns.append(pltpu.make_async_copy(given(theirs, me, -1), kept_of(theirs, me, -1), own_sem.at[2]))
    for c in owns:
        c.start()
    sends = []

    def fetch(n):
        for tz, ty in peers:
            c = remote(given(which(n), tz * 4 + ty, n), kept_of(which(n), me, n),
                       d_ssem.at[n, tz * 4 + ty], d_rsem.at[n, me], device(x, core, tz, ty))
            c.start()
            sends.append(c)

    def hand(n, kind, b, dev):
        return remote(kept(b, n), kept(b, n), hand_ssem.at[kind, n], hand_rsem.at[kind, n], dev)

    def hand_on(n):
        hand(n, 0, theirs, x_from).wait_recv()
        c = hand(n, 2, theirs, mate)
        c.start()
        sends.append(c)

    for n in range(AT_ONCE):
        fetch(n)
    for c in small:
        c.wait()
    for b in range(NB):
        def find(p, carry, b=b):
            at = jnp.int32(LISTED)
            for t in range(LISTED):
                at = jnp.where(tiles_ref[t, group * NB + b] == p, t, at)
            slot_s[b, p] = at
            return carry

        lax.fori_loop(0, 64, find, 0)
        part_v[b, :, LISTED] = jnp.zeros((2, HALF, D), BF16)
        for n in range(8):
            pos_v[b : b + 1, n * 128 : n * 128 + 128] = pos_ref[8 * b + n : 8 * b + n + 1, :]
            ct_v[b : b + 1, n * 128 : n * 128 + 128] = ct_ref[8 * b + n : 8 * b + n + 1, :]
    for c in owns:
        c.wait()
    def forward(half, b):
        first = half * LISTED * HALF
        for t in range(LISTED):
            block = tiles_ref[t, group * NB + b]
            pq_v[b, pl.ds(first + t * HALF, HALF), :] = sel_v[half][block & 3, block >> 2]
        base = (group * NB + b) * 2 * BLK + owner * SL + half * HALF
        for c in range(BLK // CH):
            r = pl.ds(c * CH, CH)
            s = lax.dot_general(pq_v[b, pl.ds(first, LISTED * HALF), :], q_v[b, r, :], (((1,), (1,)), ((), ())),
                                preferred_element_type=F32)
            top = jnp.max(s, axis=0, keepdims=True)
            e = jnp.exp2(s * (SCALE * LOG2E) - top * (SCALE * LOG2E))
            e_v[b, pl.ds(first, LISTED * HALF), r] = e.astype(BF16)
            local[half, pl.ds(b, 1), r] = top * SCALE
            local[half, pl.ds(NB + b, 1), r] = jnp.sum(e, axis=0, keepdims=True)
            at = lax.broadcasted_iota(jnp.int32, (HALF, CH), 0) == pos_v[pl.ds(b, 1), r] - base
            got_here = jnp.sum(jnp.where(at, s[0:HALF], 0.0), axis=0, keepdims=True) * SCALE
            pick[0, pl.ds(b, 1), r] = got_here if half == 0 else pick[0, pl.ds(b, 1), r] + got_here

    def run(body, steps):
        def one(n, carry):
            body(n)
            return carry

        lax.fori_loop(0, steps, one, 0)

    def passed(n):
        hand(n, 1, (x + 2 + core) % 4 if PHASES[n][2] else (x + 1 - core) % 4, mate).wait_recv()
        if PHASES[n][3]:
            hand(n, 2, (x + 2 + core) % 4, mate).wait_recv()

    for n in range(len(PHASES)):
        for tz, ty in peers:
            o = tz * 4 + ty
            remote(given(which(n), o, n), kept_of(which(n), o, n), d_ssem.at[n, o], d_rsem.at[n, o],
                   device(x, core, tz, ty)).wait_recv()
        for kind, dev in ((0, x_to), (1, mate)) if PHASES[n][3] else ((1, mate),):
            c = hand(n, kind, which(n), dev)
            c.start()
            sends.append(c)
        if n + AT_ONCE < len(PHASES):
            fetch(n + AT_ONCE)
        if n == len(PHASES) - 2:
            for k in range(EARLY):
                passed(k)
            for b in range(NB):
                pltpu.make_async_copy(q_hbm.at[b], q_v.at[b], q_sem.at[b]).wait()
            run(lambda b: forward(0, b), NB)
        if n >= 1 and PHASES[n - 1][3]:
            hand_on(n - 1)
    for n in range(EARLY, len(PHASES)):
        passed(n)

    spread = []

    def tell(half):
        two = slice(2 * half, 2 * half + 2)
        tot = slice(NB + 2 * half, NB + 2 * half + 2)
        high = jnp.maximum(local[0, two], local[1, two])
        now[half, 0, 0:2] = high
        now[half, 0, 2:4] = sum(local[k, tot] * jnp.exp(local[k, two] - high) for k in range(2))
        for tz, ty in peers:
            c = remote(now.at[half, 0], now_buf.at[half, me], tell_ssem.at[half, tz * 4 + ty], tell_rsem.at[half, me],
                       device(x, core, tz, ty))
            c.start()
            spread.append(c)

    picks = Exchange(pick, pick_buf, ex_ssem, ex_rsem, [z_peers, y_peers])

    def combine(half):
        parts = [now[half, 0]]
        for tz, ty in peers:
            o = tz * 4 + ty
            remote(now.at[half, 0], now_buf.at[half, o], tell_ssem.at[half, o], tell_rsem.at[half, o],
                   device(x, core, tz, ty)).wait_recv()
            parts.append(now_buf[half, o])
        high = parts[0][0:2]
        for p in parts[1:]:
            high = jnp.maximum(high, p[0:2])
        now[half, 1, 0:2] = high
        now[half, 1, 2:4] = sum(p[2:4] * jnp.exp(p[0:2] - high) for p in parts)

    run(lambda k: forward(1, k), 2)
    tell(0)
    run(lambda k: forward(1, 2 + k), 2)
    tell(1)
    combine(0)

    def grads(half, k):
        b = 2 * half + k
        weight = ct_v[pl.ds(b, 1), :] * SCALE
        for k2 in range(2):
            factor = weight * jnp.exp(local[k2, pl.ds(b, 1), :] - now[half, 1, pl.ds(k, 1), :]) / now[half, 1, pl.ds(2 + k, 1), :]
            base = (group * NB + b) * 2 * BLK + owner * SL + k2 * HALF
            at = lax.broadcasted_iota(jnp.int32, (HALF, BLK), 0) == pos_v[pl.ds(b, 1), :] - base
            one = slice(k2 * LISTED * HALF, k2 * LISTED * HALF + HALF)
            rest = slice(k2 * LISTED * HALF + HALF, (k2 + 1) * LISTED * HALF)
            e_v[b, one, :] = (e_v[b, one, :].astype(F32) * factor - jnp.where(at, weight, 0.0)).astype(BF16)
            e_v[b, rest, :] = (e_v[b, rest, :].astype(F32) * factor).astype(BF16)

    def passage_product(b):
        out = jnp.dot(e_v[b], q_v[b], preferred_element_type=F32)
        part_v[b, :, 0:LISTED] = out.astype(BF16).reshape(2, LISTED, HALF, D)

    def query_product(b, quarter):
        r = pl.ds(pl.multiple_of(quarter * 256, 256), 256)
        out = lax.dot_general(e_v[b, :, r], pq_v[b], (((0,), (0,)), ((), ())), preferred_element_type=F32)
        dq_v[b, pl.ds(quarter * 4, 4)] = out.astype(BF16).reshape(4, SL, D)

    def dense(piece, n):
        blocks = []
        for o in range(2):
            for k in range(2):
                p = (2 * n + o) * NB + 2 * piece + k
                at = [slot_s[b, p] for b in range(NB)]
                for half in range(2):
                    blocks.append((part_v[0, half, at[0]] + part_v[1, half, at[1]])
                                  + (part_v[2, half, at[2]] + part_v[3, half, at[3]]))
        flat = jnp.concatenate(blocks, axis=0).T
        dp_v[piece, :, :, :, :, pl.ds(pl.multiple_of(n * 256, 256), 256)] = flat.reshape(4, 2, 2, 48, 256)

    cores = {}

    def to_core(piece):
        for k, step in enumerate((2, 1, 3, 0)):
            c = remote(dp_v.at[piece, (x + step) % 4, 1 - core], core_buf.at[piece, k],
                       core_ssem.at[piece, k], core_rsem.at[piece, k], mate)
            c.start()
            cores[piece, k] = c

    def add_core(piece, k):
        place = (x + (2, 1, 3, 0)[k]) % 4
        cores[piece, k].wait_recv()
        for h in range(2):
            dp_v[piece, place, core, h] = (
                dp_v[piece, place, core, h].astype(F32) + core_buf[piece, k, h].astype(F32)).astype(BF16)

    z_next = [z_peers[0], z_peers[2]]
    y_next = [y_peers[0], y_peers[2]]
    left, right = pl.ds(0, 384), pl.ds(384, 384)
    a1 = Ring(z, lambda j, h: dq_v.at[j, pl.ds(8 * h, 8), :, left], z_next, a1_buf, a1_acc, r_ssem.at[0], r_rsem.at[0])
    b1 = Ring(y, lambda j, h: dq_v.at[pl.ds(2 * h, 2), pl.ds(4 * j, 4), :, right], y_next, b1_buf, b1_acc,
              r_ssem.at[1], r_rsem.at[1])
    a2 = Ring(y, lambda j, h: a1_sum.at[j, pl.ds(2 * h, 2)], y_next, a2_buf, a2_acc, r_ssem.at[2], r_rsem.at[2])
    b2 = Ring(z, lambda j, h: b1_sum.at[j, pl.ds(2 * h, 2)], z_next, b2_buf, b2_acc, r_ssem.at[3], r_rsem.at[3])
    xr = [Ring(x, lambda j, h, n=n: dp_v.at[n, j, core, h], x_next, x_buf.at[n], x_acc.at[n],
               r_ssem.at[4 + n], r_rsem.at[4 + n]) for n in range(PIECES)]
    returns, keeps = [], []

    def go_back(piece):
        for h in range(2):
            res = xr[piece].result(h).astype(BF16)
            for n in range(16):
                back[piece, n, pl.ds(48 * h, 48), :] = res[:, n * 128 : n * 128 + 128]
        for tz, ty in peers:
            o = tz * 4 + ty
            c = remote(back.at[piece, o], got.at[piece, me], back_ssem.at[piece, o], back_rsem.at[piece, me],
                       device(x, core, tz, ty))
            c.start()
            returns.append(c)
        c = pltpu.make_async_copy(back.at[piece, me], got.at[piece, me], keep_sem.at[piece])
        c.start()
        keeps.append(c)

    def both(k):
        grads(0, k)
        passage_product(k)

    run(both, 2)
    combine(1)
    run(lambda k: grads(1, k), 2)
    opposite = (z + 2) % 4
    for c in range(3):
        r = pl.ds(c * 256, 256)
        out = lax.dot_general(e_v[opposite], pq_v[opposite, :, r], (((0,), (0,)), ((), ())), preferred_element_type=F32)
        dq_v[opposite, :, :, r] = out.astype(BF16).reshape(16, SL, 256)
    a1.ahead()
    run(lambda n: query_product((z + 3 + n) % 4, (y + 2) % 4), 3)
    b1.ahead()
    run(lambda k: passage_product(2 + k), 2)
    run(lambda n: dense(0, n), 8)
    to_core(0)
    run(lambda n: query_product((z + 1) % 4, (y + 3 + n) % 4), 3)
    add_core(0, 0)
    xr[0].ahead()
    add_core(0, 1)
    add_core(0, 2)
    xr[0].raw()
    run(lambda n: query_product((z + 3) % 4, (y + 3 + n) % 4), 3)
    a1.raw()
    run(lambda n: query_product(z, (y + 3 + n) % 4), 3)
    b1.raw()
    run(lambda n: dense(1, n), 8)
    to_core(1)
    add_core(0, 3)
    a1.forward()
    b1.forward()
    xr[0].forward()
    add_core(1, 0)
    xr[1].ahead()
    add_core(1, 1)
    add_core(1, 2)
    xr[1].raw()
    add_core(1, 3)
    picks.start(0)
    go_back(0)
    pick[1] = sum(picks.parts(0))
    picks.start(1)
    xr[1].forward()
    for h in range(2):
        a1_sum[pl.ds(2 * h, 2)] = a1.result(h).astype(BF16).reshape(2, 4, SL, 384)
    a2.ahead()
    a2.raw()
    for h in range(2):
        b1_sum[pl.ds(2 * h, 2)] = b1.result(h).astype(BF16)
    b2.ahead()
    b2.raw()
    a2.forward()
    b2.forward()
    go_back(1)
    span = pl.ds(pl.multiple_of(y * 256, 256), 256)
    pick[2] = sum(picks.parts(1))

    def final(row):
        return now[z // 2, 1, pl.ds(2 * row + z % 2, 1), span]

    losses_ref[...] = final(0) + jnp.log(final(1)) - pick[2, pl.ds(z, 1), span]
    for h in range(2):
        qg_ref[pl.ds(128 * h, 128), left] = a2.result(h).astype(BF16).reshape(128, 384)
        qg_ref[pl.ds(128 * h, 128), right] = b2.result(h).astype(BF16).reshape(128, 384)
    keeps.append(pltpu.make_async_copy(losses_ref, losses_hbm, keep_sem.at[2]))
    keeps.append(pltpu.make_async_copy(qg_ref, qg_hbm, keep_sem.at[3]))
    for c in keeps[-2:]:
        c.start()
    for piece in range(PIECES):
        for tz, ty in peers:
            n = tz * 4 + ty
            remote(back.at[piece, n], got.at[piece, n], back_ssem.at[piece, n], back_rsem.at[piece, n],
                   device(x, core, tz, ty)).wait_recv()
    for moved in [picks, a1, b1, a2, b2] + xr:
        moved.drain()
    for c in sends + list(cores.values()) + returns + spread:
        c.wait_send()
    for c in keeps:
        c.wait()


def lay_kernel(losses_in, qg_in, got, losses_ref, qg_ref, pg_ref):
    losses_ref[...] = losses_in[...]
    qg_ref[...] = qg_in[...]
    for piece in range(PIECES):
        for n in range(8):
            one, two = got[piece, 2 * n], got[piece, 2 * n + 1]
            for k in range(2):
                h = slice(k * SL, k * SL + SL)
                first = (2 * piece + k) * BLK + n * 128
                pg_ref[:, first : first + 128] = jnp.concatenate([one[:, h], two[:, h]], axis=1)


SMEM = pl.BlockSpec(memory_space=pltpu.SMEM)
VMEM = pl.BlockSpec(memory_space=pltpu.VMEM)
ANY = pl.BlockSpec(memory_space=pl.ANY)


def whole(tiles, positives, cotangent, queries, passages):
    dma = pltpu.SemaphoreType.DMA
    return pl.pallas_call(
        whole_kernel,
        out_shape=[
            jax.ShapeDtypeStruct((1, 256), F32),
            jax.ShapeDtypeStruct((256, D), BF16),
            jax.ShapeDtypeStruct((PIECES, 16, 96, 128), BF16),
        ],
        in_specs=[SMEM, ANY, ANY, ANY, ANY],
        out_specs=[ANY, ANY, ANY],
        scratch_shapes=[
            pltpu.VMEM((32, 128), jnp.int32), pltpu.VMEM((32, 128), F32),
            pltpu.VMEM((1, 256), F32), pltpu.VMEM((256, D), BF16),
            pltpu.VMEM((NB, BLK, D), BF16),
            pltpu.VMEM((NB, 16, HALF, D), BF16), pltpu.VMEM((NB, 16, HALF, D), BF16),
            pltpu.VMEM((NB, 16, SL, D), BF16),
            pltpu.VMEM((NB, LISTED * SL, D), BF16),
            pltpu.VMEM((NB, LISTED * SL, BLK), BF16),
            pltpu.VMEM((NB, 2, LISTED + 1, HALF, D), BF16),
            pltpu.VMEM((PIECES, 4, 2, 2, 48, 2048), BF16),
            pltpu.SMEM((NB, 64), jnp.int32),
            pltpu.VMEM((8, BLK), jnp.int32), pltpu.VMEM((8, BLK), F32), pltpu.VMEM((2, 8, BLK), F32),
            pltpu.VMEM((2, 2, 4, BLK), F32), pltpu.VMEM((2, 16, 4, BLK), F32),
            pltpu.VMEM((3, 4, BLK), F32), pltpu.VMEM((2, 3, 4, BLK), F32),
            pltpu.VMEM((2, 3, 8, SL, 384), BF16), pltpu.VMEM((2, 8, SL, 384), BF16),
            pltpu.VMEM((4, 4, SL, 384), BF16),
            pltpu.VMEM((2, 3, 2, 4, SL, 384), BF16), pltpu.VMEM((2, 2, 4, SL, 384), BF16),
            pltpu.VMEM((4, 4, SL, 384), BF16),
            pltpu.VMEM((2, 3, 2, SL, 384), BF16), pltpu.VMEM((2, 2, SL, 384), BF16),
            pltpu.VMEM((2, 3, 2, SL, 384), BF16), pltpu.VMEM((2, 2, SL, 384), BF16),
            pltpu.VMEM((PIECES, 2, 3, 48, 2048), BF16), pltpu.VMEM((PIECES, 2, 48, 2048), BF16),
            pltpu.VMEM((PIECES, 4, 2, 48, 2048), BF16),
            pltpu.VMEM((PIECES, 16, 96, 128), BF16),
            dma((NB,)), dma((5,)),
            dma((len(PHASES), 16)), dma((len(PHASES), 16)),
            dma((3, len(PHASES))), dma((3, len(PHASES))),
            dma((2, 3)), dma((2, 3)), dma((2, 16)), dma((2, 16)),
            dma((6, 2, 3)), dma((6, 2, 3)),
            dma((PIECES, 4)), dma((PIECES, 4)),
            dma((PIECES, 16)), dma((PIECES, 16)), dma((4,)),
        ],
        compiler_params=pltpu.CompilerParams(
            collective_id=1, has_side_effects=True, vmem_limit_bytes=62 * 2**20),
        name="whole",
    )(tiles, positives, cotangent, queries, passages)


def lay(losses, query_grads, got):
    return pl.pallas_call(
        lay_kernel,
        out_shape=[
            jax.ShapeDtypeStruct((1, 256), F32),
            jax.ShapeDtypeStruct((256, D), BF16),
            jax.ShapeDtypeStruct((96, NB * BLK), BF16),
        ],
        in_specs=[VMEM, VMEM, VMEM],
        out_specs=[VMEM, VMEM, VMEM],
        name="lay",
    )(losses, query_grads, got)


def per_device(queries, passages, tiles, positives, cotangent):
    losses, query_grads, passage_grads = lay(*whole(
        tiles.T, positives.reshape(32, 128), cotangent.reshape(32, 128),
        queries.reshape(NB, BLK, D), passages.reshape(NB, 16, SL, D)))
    return losses.reshape(256), query_grads, passage_grads.T


def solution(mesh):
    in_specs = (P("pb", None), P("pa", None), P(), P("pb"), P("pb"))
    out_specs = (P(("pb", "pa")), P(("pb", "pa"), None), P("pa", "pb"))
    return jax.shard_map(
        per_device, mesh=mesh, in_specs=in_specs, out_specs=out_specs, check_vma=False
    )
```

```python
import jax
import jax.numpy as jnp
from jax import lax
from jax.experimental import pallas as pl
from jax.experimental.pallas import tpu as pltpu
from jax.sharding import PartitionSpec as P

D = 768
BLK = 1024
NB = 4
LISTED = 8
SL = 64
HALF = SL // 2
PHASES = ((0, 0, False, True), (0, 256, False, True), (0, 512, False, True),
          (1, 0, False, True), (1, 256, False, True), (1, 512, False, False), (1, 512, True, False))
EARLY = 3
AT_ONCE = 3
PIECES = 2
SCALE = D ** (-0.5)
LOG2E = 1.4426950408889634
CH = 256
F32 = jnp.float32
BF16 = jnp.bfloat16


def around():
    group, owner = lax.axis_index("pb"), lax.axis_index("pa")
    return group // 2, group % 2, owner // 4, owner % 4


def device(x, core, z, y):
    return (x * 2 + core, z * 4 + y)


def greet(devices):
    barrier = pltpu.get_barrier_semaphore()
    for dev in devices:
        pl.semaphore_signal(barrier, inc=1, device_id=dev, device_id_type=pl.DeviceIdType.MESH)
    pl.semaphore_wait(barrier, len(devices))


def remote(src, dst, send_sem, recv_sem, dev):
    return pltpu.make_async_remote_copy(
        src_ref=src, dst_ref=dst, send_sem=send_sem, recv_sem=recv_sem,
        device_id=dev, device_id_type=pl.DeviceIdType.MESH)


AHEAD, RAW, SUMMED = 0, 1, 2


class Ring:
    def __init__(self, me, chunk, neighbours, buf, acc, send_sem, recv_sem):
        self.me, self.chunk, self.buf, self.acc = me, chunk, buf, acc
        self.send = lambda d, kind, src: remote(
            src, buf.at[d, kind], send_sem.at[d, kind], recv_sem.at[d, kind], neighbours[d])
        self.sent = {}

    def at(self, step, half):
        return self.chunk((self.me + step) % 4, half)

    def go(self, d, kind, src):
        c = self.send(d, kind, src)
        c.start()
        self.sent[d, kind] = c

    def ahead(self):
        self.go(0, AHEAD, self.at(2, 0))
        self.go(1, AHEAD, self.at(2, 1))

    def raw(self):
        self.go(0, RAW, self.at(1, 1))
        self.go(1, RAW, self.at(3, 0))

    def forward(self):
        for d, step in ((0, 1), (1, 3)):
            self.sent[d, AHEAD].wait_recv()
            self.acc[d] = (self.at(step, d)[...].astype(F32) + self.buf[d, AHEAD].astype(F32)).astype(BF16)
            self.go(d, SUMMED, self.acc.at[d])

    def result(self, half):
        a, b = (SUMMED, RAW) if half == 0 else (RAW, SUMMED)
        self.sent[0, a].wait_recv()
        self.sent[1, b].wait_recv()
        return self.at(0, half)[...].astype(F32) + self.buf[0, a].astype(F32) + self.buf[1, b].astype(F32)

    def drain(self):
        for c in self.sent.values():
            c.wait_send()


class Exchange:
    def __init__(self, now, buf, send_sem, recv_sem, peers):
        self.now, self.buf, self.peers = now, buf, peers
        self.sems = send_sem, recv_sem
        self.sent = {}

    def start(self, stage):
        for d in range(3):
            c = remote(self.now.at[stage], self.buf.at[stage, d], self.sems[0].at[stage, d], self.sems[1].at[stage, d],
                       self.peers[stage][d])
            c.start()
            self.sent[stage, d] = c

    def parts(self, stage):
        for d in range(3):
            self.sent[stage, d].wait_recv()
        return [self.now[stage]] + [self.buf[stage, d] for d in range(3)]

    def drain(self):
        for c in self.sent.values():
            c.wait_send()


def whole_kernel(tiles_ref, pos_hbm, ct_hbm, q_hbm, p_hbm, losses_hbm, qg_hbm, got,
                 pos_ref, ct_ref, losses_ref, qg_ref, q_v, sel_a, sel_b, dq_v, pq_v, e_v, part_v, dp_v, slot_s, pos_v, ct_v, local, now, now_buf, pick, pick_buf,
                 a1_buf, a1_acc, a1_sum, b1_buf, b1_acc, b1_sum, a2_buf, a2_acc, b2_buf, b2_acc,
                 x_buf, x_acc, core_buf, back,
                 q_sem, own_sem, d_ssem, d_rsem, hand_ssem, hand_rsem, ex_ssem, ex_rsem, tell_ssem, tell_rsem,
                 r_ssem, r_rsem, core_ssem, core_rsem, back_ssem, back_rsem, keep_sem):
    group, owner = lax.axis_index("pb"), lax.axis_index("pa")
    x, core, z, y = around()
    me = z * 4 + y
    sel_v = sel_a, sel_b
    peers = [((z + dz) % 4, (y + dy) % 4) for dz in (2, 1, 3, 0) for dy in (2, 1, 3, 0) if dz or dy]
    z_peers = [device(x, core, (z + d) % 4, y) for d in (1, 2, 3)]
    y_peers = [device(x, core, z, (y + d) % 4) for d in (1, 2, 3)]
    x_next = [device((x + 1) % 4, core, z, y), device((x + 3) % 4, core, z, y)]
    mate = device(x, 1 - core, z, y)
    for b in range(NB):
        pltpu.make_async_copy(q_hbm.at[b], q_v.at[b], q_sem.at[b]).start()
    small = [pltpu.make_async_copy(pos_hbm, pos_ref, own_sem.at[3]), pltpu.make_async_copy(ct_hbm, ct_ref, own_sem.at[4])]
    for c in small:
        c.start()
    greet([device(x, core, tz, ty) for tz, ty in peers] + x_next + [mate])

    to = (x + 1 + 2 * core) % 4
    source = (x + 3 + 2 * core) % 4
    x_to, x_from = device(to, core, z, y), device(source, core, z, y)
    mine = (x + core) % 4
    theirs = (source + core) % 4

    def given(b, s, n):
        return p_hbm.at[b, s, pl.ds(HALF * PHASES[n][0], HALF), pl.ds(PHASES[n][1], 256)]

    def kept(b, n):
        return sel_v[PHASES[n][0]].at[b, :, :, pl.ds(PHASES[n][1], 256)]

    def kept_of(b, o, n):
        return sel_v[PHASES[n][0]].at[b, o, :, pl.ds(PHASES[n][1], 256)]

    def which(n):
        return theirs if PHASES[n][2] else mine

    owns = [pltpu.make_async_copy(p_hbm.at[mine, me, pl.ds(HALF * k, HALF)], sel_v[k].at[mine, me], own_sem.at[k])
            for k in range(2)]
    owns.append(pltpu.make_async_copy(given(theirs, me, -1), kept_of(theirs, me, -1), own_sem.at[2]))
    for c in owns:
        c.start()
    sends = []

    def fetch(n):
        for tz, ty in peers:
            c = remote(given(which(n), tz * 4 + ty, n), kept_of(which(n), me, n),
                       d_ssem.at[n, tz * 4 + ty], d_rsem.at[n, me], device(x, core, tz, ty))
            c.start()
            sends.append(c)

    def hand(n, kind, b, dev):
        return remote(kept(b, n), kept(b, n), hand_ssem.at[kind, n], hand_rsem.at[kind, n], dev)

    def hand_on(n):
        hand(n, 0, theirs, x_from).wait_recv()
        c = hand(n, 2, theirs, mate)
        c.start()
        sends.append(c)

    for n in range(AT_ONCE):
        fetch(n)
    for c in small:
        c.wait()
    for b in range(NB):
        def find(p, carry, b=b):
            at = jnp.int32(LISTED)
            for t in range(LISTED):
                at = jnp.where(tiles_ref[t, group * NB + b] == p, t, at)
            slot_s[b, p] = at
            return carry

        lax.fori_loop(0, 64, find, 0)
        part_v[b, :, LISTED] = jnp.zeros((2, HALF, D), BF16)
        for n in range(8):
            pos_v[b : b + 1, n * 128 : n * 128 + 128] = pos_ref[8 * b + n : 8 * b + n + 1, :]
            ct_v[b : b + 1, n * 128 : n * 128 + 128] = ct_ref[8 * b + n : 8 * b + n + 1, :]
    for c in owns:
        c.wait()
    def forward(half, b):
        first = half * LISTED * HALF
        for t in range(LISTED):
            block = tiles_ref[t, group * NB + b]
            pq_v[b, pl.ds(first + t * HALF, HALF), :] = sel_v[half][block & 3, block >> 2]
        base = (group * NB + b) * 2 * BLK + owner * SL + half * HALF
        for c in range(BLK // CH):
            r = pl.ds(c * CH, CH)
            s = lax.dot_general(pq_v[b, pl.ds(first, LISTED * HALF), :], q_v[b, r, :], (((1,), (1,)), ((), ())),
                                preferred_element_type=F32)
            top = jnp.max(s, axis=0, keepdims=True)
            e = jnp.exp2(s * (SCALE * LOG2E) - top * (SCALE * LOG2E))
            e_v[b, pl.ds(first, LISTED * HALF), r] = e.astype(BF16)
            local[half, pl.ds(b, 1), r] = top * SCALE
            local[half, pl.ds(NB + b, 1), r] = jnp.sum(e, axis=0, keepdims=True)
            at = lax.broadcasted_iota(jnp.int32, (HALF, CH), 0) == pos_v[pl.ds(b, 1), r] - base
            got_here = jnp.sum(jnp.where(at, s[0:HALF], 0.0), axis=0, keepdims=True) * SCALE
            pick[0, pl.ds(b, 1), r] = got_here if half == 0 else pick[0, pl.ds(b, 1), r] + got_here

    def run(body, steps):
        def one(n, carry):
            body(n)
            return carry

        lax.fori_loop(0, steps, one, 0)

    def passed(n):
        hand(n, 1, (x + 2 + core) % 4 if PHASES[n][2] else (x + 1 - core) % 4, mate).wait_recv()
        if PHASES[n][3]:
            hand(n, 2, (x + 2 + core) % 4, mate).wait_recv()

    for n in range(len(PHASES)):
        for tz, ty in peers:
            o = tz * 4 + ty
            remote(given(which(n), o, n), kept_of(which(n), o, n), d_ssem.at[n, o], d_rsem.at[n, o],
                   device(x, core, tz, ty)).wait_recv()
        for kind, dev in ((0, x_to), (1, mate)) if PHASES[n][3] else ((1, mate),):
            c = hand(n, kind, which(n), dev)
            c.start()
            sends.append(c)
        if n + AT_ONCE < len(PHASES):
            fetch(n + AT_ONCE)
        if n == len(PHASES) - 2:
            for k in range(EARLY):
                passed(k)
            for b in range(NB):
                pltpu.make_async_copy(q_hbm.at[b], q_v.at[b], q_sem.at[b]).wait()
            run(lambda b: forward(0, b), NB)
        if n >= 1 and PHASES[n - 1][3]:
            hand_on(n - 1)
    for n in range(EARLY, len(PHASES)):
        passed(n)

    spread = []

    def tell(half):
        two = slice(2 * half, 2 * half + 2)
        tot = slice(NB + 2 * half, NB + 2 * half + 2)
        high = jnp.maximum(local[0, two], local[1, two])
        now[half, 0, 0:2] = high
        now[half, 0, 2:4] = sum(local[k, tot] * jnp.exp(local[k, two] - high) for k in range(2))
        for tz, ty in peers:
            c = remote(now.at[half, 0], now_buf.at[half, me], tell_ssem.at[half, tz * 4 + ty], tell_rsem.at[half, me],
                       device(x, core, tz, ty))
            c.start()
            spread.append(c)

    picks = Exchange(pick, pick_buf, ex_ssem, ex_rsem, [z_peers, y_peers])

    def combine(half):
        parts = [now[half, 0]]
        for tz, ty in peers:
            o = tz * 4 + ty
            remote(now.at[half, 0], now_buf.at[half, o], tell_ssem.at[half, o], tell_rsem.at[half, o],
                   device(x, core, tz, ty)).wait_recv()
            parts.append(now_buf[half, o])
        high = parts[0][0:2]
        for p in parts[1:]:
            high = jnp.maximum(high, p[0:2])
        now[half, 1, 0:2] = high
        now[half, 1, 2:4] = sum(p[2:4] * jnp.exp(p[0:2] - high) for p in parts)

    run(lambda k: forward(1, k), 2)
    tell(0)
    run(lambda k: forward(1, 2 + k), 2)
    tell(1)
    combine(0)

    def grads(half, k):
        b = 2 * half + k
        weight = ct_v[pl.ds(b, 1), :] * SCALE
        for k2 in range(2):
            factor = weight * jnp.exp(local[k2, pl.ds(b, 1), :] - now[half, 1, pl.ds(k, 1), :]) / now[half, 1, pl.ds(2 + k, 1), :]
            base = (group * NB + b) * 2 * BLK + owner * SL + k2 * HALF
            at = lax.broadcasted_iota(jnp.int32, (HALF, BLK), 0) == pos_v[pl.ds(b, 1), :] - base
            one = slice(k2 * LISTED * HALF, k2 * LISTED * HALF + HALF)
            rest = slice(k2 * LISTED * HALF + HALF, (k2 + 1) * LISTED * HALF)
            e_v[b, one, :] = (e_v[b, one, :].astype(F32) * factor - jnp.where(at, weight, 0.0)).astype(BF16)
            e_v[b, rest, :] = (e_v[b, rest, :].astype(F32) * factor).astype(BF16)

    def passage_product(b):
        out = jnp.dot(e_v[b], q_v[b], preferred_element_type=F32)
        part_v[b, :, 0:LISTED] = out.astype(BF16).reshape(2, LISTED, HALF, D)

    def query_product(b, quarter):
        r = pl.ds(pl.multiple_of(quarter * 256, 256), 256)
        out = lax.dot_general(e_v[b, :, r], pq_v[b], (((0,), (0,)), ((), ())), preferred_element_type=F32)
        dq_v[b, pl.ds(quarter * 4, 4)] = out.astype(BF16).reshape(4, SL, D)

    def dense(piece, n):
        blocks = []
        for o in range(2):
            for k in range(2):
                p = (2 * n + o) * NB + 2 * piece + k
                at = [slot_s[b, p] for b in range(NB)]
                for half in range(2):
                    blocks.append((part_v[0, half, at[0]] + part_v[1, half, at[1]])
                                  + (part_v[2, half, at[2]] + part_v[3, half, at[3]]))
        flat = jnp.concatenate(blocks, axis=0).T
        dp_v[piece, :, :, :, :, pl.ds(pl.multiple_of(n * 256, 256), 256)] = flat.reshape(4, 2, 2, 48, 256)

    cores = {}

    def to_core(piece):
        for k, step in enumerate((2, 1, 3, 0)):
            c = remote(dp_v.at[piece, (x + step) % 4, 1 - core], core_buf.at[piece, k],
                       core_ssem.at[piece, k], core_rsem.at[piece, k], mate)
            c.start()
            cores[piece, k] = c

    def add_core(piece, k):
        place = (x + (2, 1, 3, 0)[k]) % 4
        cores[piece, k].wait_recv()
        for h in range(2):
            dp_v[piece, place, core, h] = (
                dp_v[piece, place, core, h].astype(F32) + core_buf[piece, k, h].astype(F32)).astype(BF16)

    z_next = [z_peers[0], z_peers[2]]
    y_next = [y_peers[0], y_peers[2]]
    left, right = pl.ds(0, 384), pl.ds(384, 384)
    a1 = Ring(z, lambda j, h: dq_v.at[j, pl.ds(8 * h, 8), :, left], z_next, a1_buf, a1_acc, r_ssem.at[0], r_rsem.at[0])
    b1 = Ring(y, lambda j, h: dq_v.at[pl.ds(2 * h, 2), pl.ds(4 * j, 4), :, right], y_next, b1_buf, b1_acc,
              r_ssem.at[1], r_rsem.at[1])
    a2 = Ring(y, lambda j, h: a1_sum.at[j, pl.ds(2 * h, 2)], y_next, a2_buf, a2_acc, r_ssem.at[2], r_rsem.at[2])
    b2 = Ring(z, lambda j, h: b1_sum.at[j, pl.ds(2 * h, 2)], z_next, b2_buf, b2_acc, r_ssem.at[3], r_rsem.at[3])
    xr = [Ring(x, lambda j, h, n=n: dp_v.at[n, j, core, h], x_next, x_buf.at[n], x_acc.at[n],
               r_ssem.at[4 + n], r_rsem.at[4 + n]) for n in range(PIECES)]
    returns, keeps = [], []

    def go_back(piece):
        for h in range(2):
            res = xr[piece].result(h).astype(BF16)
            for n in range(16):
                back[piece, n, pl.ds(48 * h, 48), :] = res[:, n * 128 : n * 128 + 128]
        for tz, ty in peers:
            o = tz * 4 + ty
            c = remote(back.at[piece, o], got.at[piece, me], back_ssem.at[piece, o], back_rsem.at[piece, me],
                       device(x, core, tz, ty))
            c.start()
            returns.append(c)
        c = pltpu.make_async_copy(back.at[piece, me], got.at[piece, me], keep_sem.at[piece])
        c.start()
        keeps.append(c)

    def both(k):
        grads(0, k)
        passage_product(k)

    run(both, 2)
    run(lambda b: query_product(b, (y + 2) % 4), 2)
    combine(1)
    run(lambda k: grads(1, k), 2)
    opposite = (z + 2) % 4
    for c in range(3):
        r = pl.ds(c * 256, 256)
        out = lax.dot_general(e_v[opposite], pq_v[opposite, :, r], (((0,), (0,)), ((), ())), preferred_element_type=F32)
        dq_v[opposite, :, :, r] = out.astype(BF16).reshape(16, SL, 256)
    a1.ahead()

    def late(k):
        @pl.when(2 + k != opposite)
        def _():
            query_product(2 + k, (y + 2) % 4)

    run(late, 2)
    b1.ahead()
    run(lambda k: passage_product(2 + k), 2)
    run(lambda n: dense(0, n), 8)
    to_core(0)
    run(lambda n: query_product((z + 1) % 4, (y + 3 + n) % 4), 3)
    add_core(0, 0)
    xr[0].ahead()
    add_core(0, 1)
    add_core(0, 2)
    xr[0].raw()
    run(lambda n: query_product((z + 3) % 4, (y + 3 + n) % 4), 3)
    a1.raw()
    run(lambda n: query_product(z, (y + 3 + n) % 4), 3)
    b1.raw()
    run(lambda n: dense(1, n), 8)
    to_core(1)
    add_core(0, 3)
    a1.forward()
    b1.forward()
    xr[0].forward()
    add_core(1, 0)
    xr[1].ahead()
    add_core(1, 1)
    add_core(1, 2)
    xr[1].raw()
    add_core(1, 3)
    picks.start(0)
    go_back(0)
    pick[1] = sum(picks.parts(0))
    picks.start(1)
    xr[1].forward()
    for h in range(2):
        a1_sum[pl.ds(2 * h, 2)] = a1.result(h).astype(BF16).reshape(2, 4, SL, 384)
    a2.ahead()
    a2.raw()
    for h in range(2):
        b1_sum[pl.ds(2 * h, 2)] = b1.result(h).astype(BF16)
    b2.ahead()
    b2.raw()
    a2.forward()
    b2.forward()
    go_back(1)
    span = pl.ds(pl.multiple_of(y * 256, 256), 256)
    pick[2] = sum(picks.parts(1))

    def final(row):
        return now[z // 2, 1, pl.ds(2 * row + z % 2, 1), span]

    losses_ref[...] = final(0) + jnp.log(final(1)) - pick[2, pl.ds(z, 1), span]
    for h in range(2):
        qg_ref[pl.ds(128 * h, 128), left] = a2.result(h).astype(BF16).reshape(128, 384)
        qg_ref[pl.ds(128 * h, 128), right] = b2.result(h).astype(BF16).reshape(128, 384)
    keeps.append(pltpu.make_async_copy(losses_ref, losses_hbm, keep_sem.at[2]))
    keeps.append(pltpu.make_async_copy(qg_ref, qg_hbm, keep_sem.at[3]))
    for c in keeps[-2:]:
        c.start()
    for piece in range(PIECES):
        for tz, ty in peers:
            n = tz * 4 + ty
            remote(back.at[piece, n], got.at[piece, n], back_ssem.at[piece, n], back_rsem.at[piece, n],
                   device(x, core, tz, ty)).wait_recv()
    for moved in [picks, a1, b1, a2, b2] + xr:
        moved.drain()
    for c in sends + list(cores.values()) + returns + spread:
        c.wait_send()
    for c in keeps:
        c.wait()


def lay_kernel(losses_in, qg_in, got, losses_ref, qg_ref, pg_ref):
    losses_ref[...] = losses_in[...]
    qg_ref[...] = qg_in[...]
    for piece in range(PIECES):
        for n in range(8):
            one, two = got[piece, 2 * n], got[piece, 2 * n + 1]
            for k in range(2):
                h = slice(k * SL, k * SL + SL)
                first = (2 * piece + k) * BLK + n * 128
                pg_ref[:, first : first + 128] = jnp.concatenate([one[:, h], two[:, h]], axis=1)


SMEM = pl.BlockSpec(memory_space=pltpu.SMEM)
VMEM = pl.BlockSpec(memory_space=pltpu.VMEM)
ANY = pl.BlockSpec(memory_space=pl.ANY)


def whole(tiles, positives, cotangent, queries, passages):
    dma = pltpu.SemaphoreType.DMA
    return pl.pallas_call(
        whole_kernel,
        out_shape=[
            jax.ShapeDtypeStruct((1, 256), F32),
            jax.ShapeDtypeStruct((256, D), BF16),
            jax.ShapeDtypeStruct((PIECES, 16, 96, 128), BF16),
        ],
        in_specs=[SMEM, ANY, ANY, ANY, ANY],
        out_specs=[ANY, ANY, ANY],
        scratch_shapes=[
            pltpu.VMEM((32, 128), jnp.int32), pltpu.VMEM((32, 128), F32),
            pltpu.VMEM((1, 256), F32), pltpu.VMEM((256, D), BF16),
            pltpu.VMEM((NB, BLK, D), BF16),
            pltpu.VMEM((NB, 16, HALF, D), BF16), pltpu.VMEM((NB, 16, HALF, D), BF16),
            pltpu.VMEM((NB, 16, SL, D), BF16),
            pltpu.VMEM((NB, LISTED * SL, D), BF16),
            pltpu.VMEM((NB, LISTED * SL, BLK), BF16),
            pltpu.VMEM((NB, 2, LISTED + 1, HALF, D), BF16),
            pltpu.VMEM((PIECES, 4, 2, 2, 48, 2048), BF16),
            pltpu.SMEM((NB, 64), jnp.int32),
            pltpu.VMEM((8, BLK), jnp.int32), pltpu.VMEM((8, BLK), F32), pltpu.VMEM((2, 8, BLK), F32),
            pltpu.VMEM((2, 2, 4, BLK), F32), pltpu.VMEM((2, 16, 4, BLK), F32),
            pltpu.VMEM((3, 4, BLK), F32), pltpu.VMEM((2, 3, 4, BLK), F32),
            pltpu.VMEM((2, 3, 8, SL, 384), BF16), pltpu.VMEM((2, 8, SL, 384), BF16),
            pltpu.VMEM((4, 4, SL, 384), BF16),
            pltpu.VMEM((2, 3, 2, 4, SL, 384), BF16), pltpu.VMEM((2, 2, 4, SL, 384), BF16),
            pltpu.VMEM((4, 4, SL, 384), BF16),
            pltpu.VMEM((2, 3, 2, SL, 384), BF16), pltpu.VMEM((2, 2, SL, 384), BF16),
            pltpu.VMEM((2, 3, 2, SL, 384), BF16), pltpu.VMEM((2, 2, SL, 384), BF16),
            pltpu.VMEM((PIECES, 2, 3, 48, 2048), BF16), pltpu.VMEM((PIECES, 2, 48, 2048), BF16),
            pltpu.VMEM((PIECES, 4, 2, 48, 2048), BF16),
            pltpu.VMEM((PIECES, 16, 96, 128), BF16),
            dma((NB,)), dma((5,)),
            dma((len(PHASES), 16)), dma((len(PHASES), 16)),
            dma((3, len(PHASES))), dma((3, len(PHASES))),
            dma((2, 3)), dma((2, 3)), dma((2, 16)), dma((2, 16)),
            dma((6, 2, 3)), dma((6, 2, 3)),
            dma((PIECES, 4)), dma((PIECES, 4)),
            dma((PIECES, 16)), dma((PIECES, 16)), dma((4,)),
        ],
        compiler_params=pltpu.CompilerParams(
            collective_id=1, has_side_effects=True, vmem_limit_bytes=62 * 2**20),
        name="whole",
    )(tiles, positives, cotangent, queries, passages)


def lay(losses, query_grads, got):
    return pl.pallas_call(
        lay_kernel,
        out_shape=[
            jax.ShapeDtypeStruct((1, 256), F32),
            jax.ShapeDtypeStruct((256, D), BF16),
            jax.ShapeDtypeStruct((96, NB * BLK), BF16),
        ],
        in_specs=[VMEM, VMEM, VMEM],
        out_specs=[VMEM, VMEM, VMEM],
        name="lay",
    )(losses, query_grads, got)


def per_device(queries, passages, tiles, positives, cotangent):
    losses, query_grads, passage_grads = lay(*whole(
        tiles.T, positives.reshape(32, 128), cotangent.reshape(32, 128),
        queries.reshape(NB, BLK, D), passages.reshape(NB, 16, SL, D)))
    return losses.reshape(256), query_grads, passage_grads.T


def solution(mesh):
    in_specs = (P("pb", None), P("pa", None), P(), P("pb"), P("pb"))
    out_specs = (P(("pb", "pa")), P(("pb", "pa"), None), P("pa", "pb"))
    return jax.shard_map(
        per_device, mesh=mesh, in_specs=in_specs, out_specs=out_specs, check_vma=False
    )
```
